32 devices in a mesh: fsdp: 8 (over z, y), dp: 4 (over x, core).
Axes of the slice: x: 2, y: 2, z: 4, core: 2. Of those that a mesh axis runs over, the one named last changes fastest.
Arguments:
- tokens: bfloat16 [32768, 1024], P(('fsdp', 'dp')), may hold values from -6 to 6
- time_index: int32 [256], P(('fsdp', 'dp')), may hold values from 0 to 127
- time_table: bfloat16 [128, 1024], P(None, 'fsdp'), may hold values from -2.5 to 2.5
- ln1_gain: bfloat16 [1024], P('fsdp'), may hold values from 0.5 to 1.5
- ln1_bias: bfloat16 [1024], P('fsdp'), may hold values from -1.75 to 1.75
- w_qkv: bfloat16 [1024, 3072], P('fsdp'), may hold values from -0.1875 to 0.1875
- w_out: bfloat16 [1024, 1024], P('fsdp'), may hold values from -0.75 to 0.75
- b_out: bfloat16 [1024], P('fsdp'), may hold values from -1.75 to 1.75
- ln2_gain: bfloat16 [1024], P('fsdp'), may hold values from 0.5 to 1.5
- ln2_bias: bfloat16 [1024], P('fsdp'), may hold values from -1.75 to 1.75
- w_up: bfloat16 [1024, 4096], P('fsdp'), may hold values from -0.1875 to 0.1875
- b_up: bfloat16 [4096], P('fsdp'), may hold values from -3 to 3
- w_down: bfloat16 [4096, 1024], P('fsdp'), may hold values from -0.09375 to 0.09375
- b_down: bfloat16 [1024], P('fsdp'), may hold values from -1.75 to 1.75
- cotangent: bfloat16 [32768, 1024], P(('fsdp', 'dp')), may hold values from -6 to 6
Outputs:
- block_out: bfloat16 [32768, 1024], P(('fsdp', 'dp'))
- grad_tokens: bfloat16 [32768, 1024], P(('fsdp', 'dp'))
- grad_table: float32 [128, 1024], P(None, 'fsdp')
- grad_ln1_gain: float32 [1024], P('fsdp')
- grad_ln1_bias: float32 [1024], P('fsdp')
- grad_qkv: float32 [1024, 3072], P('fsdp')
- grad_out_w: float32 [1024, 1024], P('fsdp')
- grad_out_b: float32 [1024], P('fsdp')
- grad_ln2_gain: float32 [1024], P('fsdp')
- grad_ln2_bias: float32 [1024], P('fsdp')
- grad_up: float32 [1024, 4096], P('fsdp')
- grad_up_b: float32 [4096], P('fsdp')
- grad_down: float32 [4096, 1024], P('fsdp')
- grad_down_b: float32 [1024], P('fsdp')
The draws below stay inside these ranges and needn't reach their ends.
All inputs are finite; a program needn't handle non-finite values.
Results may differ from the reference program's by a relative error of at most 0.012.
Values may be sent and summed in bfloat16 or wider, within the bound.
No kernel may reach another device: no remote copies, remote signals or barrier semaphores. Data moves between devices by JAX's collectives and lax.ppermute only.
A program may use at most 256 MiB of HBM per device.

```python
import jax
import jax.numpy as jnp
from jax import lax

D = 1024
HEADS = 16
FF = 4096
SEQ = 128
TIMES = 128
SEQ_DEV = 8
SEQS = 256
TOKENS = 32768
N_FSDP = 8
N_DP = 4


def with_ends(values, key, low, high):
    dims = values.shape
    place = [jax.random.randint(jax.random.fold_in(key, axis), (), 0, dims[axis]) for axis in range(len(dims))]
    values = values.at[tuple(place)].set(low)
    longest = dims.index(max(dims))
    place[longest] = (place[longest] + 1) % dims[longest]
    return values.at[tuple(place)].set(high)


def shard_levels(rng, extent, cuts, least, high):
    factor_of = 1.0
    for dim, blocks in cuts:
        steps = jax.random.uniform(jax.random.fold_in(jax.random.fold_in(rng, 6), dim), (blocks,), jnp.float32, least / len(cuts), high / len(cuts))
        factor_of = factor_of * jnp.repeat(jnp.exp(steps), extent[dim] // blocks).reshape((-1,) + (1,) * (len(extent) - 1 - dim))
    return factor_of


def gaussian(key, dims, scale, limit, shards=(), kind=jnp.bfloat16):
    values = jax.random.normal(key, dims, jnp.float32) * scale
    if len(shards) > 0:
        values = shard_levels(key, dims, shards, -0.22, 0.18) * values
    return jnp.clip(values, min=-limit, max=limit).astype(kind)


def setup_inputs(seed: int = 0) -> dict:
    seeds = jax.random.split(jax.random.key(seed), 16)
    return {
        "tokens": gaussian(seeds[0], (TOKENS, D), 1.0, 6.0, ((0, 32),)),
        "time_index": with_ends(jax.random.randint(seeds[1], (SEQS,), 0, TIMES), jax.random.fold_in(seeds[1], 1), 0, TIMES - 1).astype(jnp.int32),
        "time_table": gaussian(seeds[2], (TIMES, D), 0.3, 2.5, ((1, 8),)),
        "ln1_gain": jnp.clip(1.0 + 0.1 * jax.random.normal(seeds[3], (D,), jnp.float32), 0.5, 1.5).astype(jnp.bfloat16),
        "ln1_bias": gaussian(seeds[4], (D,), 0.3, 1.75, ((0, 8),)),
        "w_qkv": gaussian(seeds[5], (D, 3 * D), D ** -0.5, 0.1875, ((0, 8),)),
        "w_out": gaussian(seeds[6], (D, D), (D // 16) ** -0.5, 0.75, ((0, 8),)),
        "b_out": gaussian(seeds[7], (D,), 0.3, 1.75, ((0, 8),)),
        "ln2_gain": jnp.clip(1.0 + 0.1 * jax.random.normal(seeds[8], (D,), jnp.float32), 0.5, 1.5).astype(jnp.bfloat16),
        "ln2_bias": gaussian(seeds[9], (D,), 0.3, 1.75, ((0, 8),)),
        "w_up": gaussian(seeds[10], (D, FF), D ** -0.5, 0.1875, ((0, 8),)),
        "b_up": gaussian(seeds[11], (FF,), 0.5, 3.0, ((0, 8),)),
        "w_down": gaussian(seeds[12], (FF, D), FF ** -0.5, 0.09375, ((0, 8),)),
        "b_down": gaussian(seeds[13], (D,), 0.3, 1.75, ((0, 8),)),
        "cotangent": gaussian(seeds[14], (TOKENS, D), 1.0, 6.0, ((0, 32),)),
    }


@jax.custom_vjp
def low(v):
    return lax.optimization_barrier(v.astype(jnp.bfloat16)).astype(jnp.float32)

@jax.custom_vjp
def low_back(v):
    return v

def low_keep(v):
    return (low(v), None)

def low_pass(kept, grad):
    return (grad,)

def back_keep(v):
    return (v, None)

def back_low(kept, grad):
    return (low(grad),)
low.defvjp(low_keep, low_pass)
low_back.defvjp(back_keep, back_low)

def normalize(values):
    centred = values - lax.optimization_barrier(jnp.mean(values, axis=-1, keepdims=True))
    spread = lax.optimization_barrier(jnp.mean(centred * centred, axis=-1, keepdims=True))
    return centred * lax.rsqrt(spread + 1e-05)

def matmul(left, right):
    return jnp.einsum('sti,ij->stj', left, right, precision=lax.Precision.HIGHEST)

def softmax_rows(scores):
    shifted = scores - lax.optimization_barrier(jnp.max(scores, axis=-1, keepdims=True))
    expont = jnp.exp(shifted)
    return expont / lax.optimization_barrier(jnp.sum(expont, axis=-1, keepdims=True))

def forward(params, inputs, block_times):
    table_all, gain_one, bias_one, qkv_w, out_w, out_b, gain_two, bias_two, up_w, up_b, down_w, down_b = params
    group_count, length, model_width = inputs.shape
    head_dim = model_width // HEADS
    factor = head_dim ** (-0.5)
    embedding = table_all[block_times][:, None, :]
    normed = normalize(inputs) * gain_one + bias_one
    scaled = low(normed * (1.0 + embedding))
    packed = low_back(low(matmul(scaled, qkv_w)))
    queries = packed[..., :model_width].reshape(group_count, length, HEADS, head_dim)
    key_heads = packed[..., model_width:2 * model_width].reshape(group_count, length, HEADS, head_dim)
    value_heads = packed[..., 2 * model_width:].reshape(group_count, length, HEADS, head_dim)
    scores = low_back(jnp.einsum('sqhd,skhd->shqk', queries, key_heads, precision=lax.Precision.HIGHEST) * factor)
    attn_probs = softmax_rows(scores)
    attn_mix = jnp.einsum('shqk,skhd->sqhd', low(attn_probs), value_heads, precision=lax.Precision.HIGHEST)
    attn_mix = low_back(low(attn_mix.reshape(group_count, length, model_width)))
    branch = low_back(matmul(attn_mix, out_w) + out_b)
    middle = inputs + branch
    hidden_in = low(normalize(middle) * gain_two + bias_two)
    pre_act = low_back(matmul(hidden_in, up_w) + up_b)
    activated = low(jax.nn.gelu(pre_act, approximate=False))
    return middle + matmul(activated, down_w) + down_b

def reference(tokens, time_index, time_table, ln1_gain, ln1_bias, w_qkv, w_out, b_out, ln2_gain, ln2_bias, w_up, b_up, w_down, b_down, cotangent):
    params = tuple((item.astype(jnp.float32) for item in (time_table, ln1_gain, ln1_bias, w_qkv, w_out, b_out, ln2_gain, ln2_bias, w_up, b_up, w_down, b_down)))
    group_seqs = SEQ_DEV * N_DP
    inputs = tokens.astype(jnp.float32).reshape(N_FSDP, group_seqs, SEQ, D)
    upstream = cotangent.astype(jnp.float32).reshape(N_FSDP, group_seqs, SEQ, D)
    picked = time_index.reshape(N_FSDP, group_seqs).astype(jnp.int32)

    def step(totals, item):
        block_in, block_times, block_up = item

        def apply(weights, values):
            return forward(weights, values, block_times)
        result, pull = jax.vjp(apply, params, block_in)
        grads, grad_in = pull(block_up)
        totals = jax.tree.map(jnp.add, totals, grads)
        return (totals, (result.astype(jnp.bfloat16), grad_in.astype(jnp.bfloat16)))
    start = jax.tree.map(jnp.zeros_like, params)
    totals, outputs = lax.scan(step, start, (inputs, picked, upstream))
    results, grad_ins = outputs
    return (results.reshape(TOKENS, D), grad_ins.reshape(TOKENS, D), totals[0], totals[1], totals[2], totals[3], totals[4], totals[5], totals[6], totals[7], totals[8], totals[9], totals[10], totals[11])
```

```python
import functools

import jax
import jax.numpy as jnp
from jax import lax
from jax.experimental import pallas as pl
from jax.experimental.pallas import tpu as pltpu
from jax.sharding import PartitionSpec as P

HEADS = 16
BOTH = ("fsdp", "dp")


def flips(which):
    pairs = []
    for f in range(8):
        for d in range(4):
            z, y, x, c = f // 2, f % 2, d // 2, d % 2
            if which == "x":
                x = 1 - x
            elif which == "y":
                y = 1 - y
            elif which == "c":
                c = 1 - c
            elif which == "z1":
                z = z ^ 1
            elif which == "z2":
                z = z ^ 2
            pairs.append((f * 4 + d, (z * 2 + y) * 4 + x * 2 + c))
    return pairs


def swap(values, which):
    return lax.ppermute(values, BOTH, flips(which))


def coords():
    f, d = lax.axis_index("fsdp"), lax.axis_index("dp")
    return f // 2, f % 2, d // 2, d % 2


def part(values, start, size, axis):
    return lax.dynamic_slice_in_dim(values, start, size, axis)


class Split:
    def __init__(self, n):
        self.n = n
        self.e = n * 3 // 8
        self.m = n - 2 * self.e
        self.eh = self.e // 2
        self.mh = self.m // 2

    def e_start(self, x, c):
        return x * (self.n - self.e) + c * self.eh

    def m_start(self, c):
        return self.e + c * self.mh


def spread(own, split, axis):
    z, y, x, c = coords()
    piece = jnp.concatenate(
        [
            part(own, split.e_start(x, c), split.eh, axis),
            part(own, split.m_start(c), split.mh, axis),
        ],
        axis=axis,
    )
    near = swap(piece, "z1")
    two = jnp.stack([piece, near])
    far = swap(two, "z2")
    four = jnp.concatenate([two, far])
    beside = swap(four, "y")
    seven = jnp.concatenate([near[None], far, beside])
    across = swap(lax.slice_in_dim(seven, 0, split.eh, axis=axis + 1), "x")
    return seven, across, swap(seven, "c"), swap(across, "c")


def assemble_kernel(split, axis, where_ref, own, seven, across, seven_c, across_c, out, sems, out_sems, hold):
    z, y, x, c = where_ref[0], where_ref[1], where_ref[2], where_ref[3]
    rows = own.shape[0]
    unit = 128 if axis == 1 else 16

    def at(ref, base, start, size):
        start = pl.multiple_of(start, unit)
        if axis == 1:
            return ref.at[pl.ds(base, rows), pl.ds(start, size)]
        return ref.at[pl.ds(pl.multiple_of(base + start, unit), size), :]

    def cut(ref, j, start, size):
        if axis == 1:
            return ref.at[j, :, pl.ds(start, size)]
        return ref.at[j, pl.ds(start, size), :]

    shards = []
    for j in range(8):
        zz = (z, z ^ 1, z ^ 2, z ^ 3)[j % 4]
        yy = y if j < 4 else 1 - y
        shards.append(zz * 2 + yy)
    groups = []
    for j in range(8):
        base = pl.multiple_of(shards[j] * rows, rows)
        if j == 0:
            copies = [(own, hold.at[pl.ds(base, rows), :])]
        else:
            k = j - 1
            oc = 1 - c
            copies = [
                (cut(seven, k, 0, split.eh), at(hold, base, split.e_start(x, c), split.eh)),
                (cut(seven, k, split.eh, split.mh), at(hold, base, split.m_start(c), split.mh)),
                (across.at[k], at(hold, base, split.e_start(1 - x, c), split.eh)),
                (cut(seven_c, k, 0, split.eh), at(hold, base, split.e_start(x, oc), split.eh)),
                (cut(seven_c, k, split.eh, split.mh), at(hold, base, split.m_start(oc), split.mh)),
                (across_c.at[k], at(hold, base, split.e_start(1 - x, oc), split.eh)),
            ]
        group = [pltpu.make_async_copy(s, d, sems.at[j]) for s, d in copies]
        for copy in group:
            copy.start()
        groups.append(group)
    outs = []
    for j in range(8):
        base = pl.multiple_of(shards[j] * rows, rows)
        for copy in groups[j]:
            copy.wait()
        copy = pltpu.make_async_copy(hold.at[pl.ds(base, rows), :], out.at[pl.ds(base, rows), :], out_sems.at[j])
        copy.start()
        outs.append(copy)
    for copy in outs:
        copy.wait()


def assemble(where, own, parts, split, axis):
    rows, cols = own.shape
    anywhere = pl.BlockSpec(memory_space=pl.ANY)
    return pl.pallas_call(
        functools.partial(assemble_kernel, split, axis),
        out_shape=jax.ShapeDtypeStruct((8 * rows, cols), own.dtype),
        grid_spec=pltpu.PrefetchScalarGridSpec(
            num_scalar_prefetch=1,
            grid=(),
            in_specs=[anywhere] * 5,
            out_specs=anywhere,
            scratch_shapes=[
                pltpu.SemaphoreType.DMA((8,)),
                pltpu.SemaphoreType.DMA((8,)),
                pltpu.VMEM((8 * rows, cols), own.dtype),
            ],
        ),
        compiler_params=pltpu.CompilerParams(vmem_limit_bytes=32 * 2**20),
        cost_estimate=pl.CostEstimate(flops=0, bytes_accessed=32 * rows * cols, transcendentals=0),
    )(where, own, *parts)


def small_kernel(where_ref, parts, out, sems):
    z, y = where_ref[0], where_ref[1]
    copies = []
    for j in range(8):
        zz = (z, z ^ 1, z ^ 2, z ^ 3)[j % 4]
        yy = y if j < 4 else 1 - y
        start = pl.multiple_of((zz * 2 + yy) * 128, 128)
        copies.append(pltpu.make_async_copy(parts.at[j], out.at[:, pl.ds(start, 128)], sems.at[j]))
    for copy in copies:
        copy.start()
    for copy in copies:
        copy.wait()


def gather_small(where, own):
    near = jnp.stack([own, swap(own, "z1")])
    four = jnp.concatenate([near, swap(near, "z2")])
    eight = jnp.concatenate([four, swap(four, "y")])
    return pl.pallas_call(
        small_kernel,
        out_shape=jax.ShapeDtypeStruct((own.shape[0], 1024), own.dtype),
        grid_spec=pltpu.PrefetchScalarGridSpec(
            num_scalar_prefetch=1,
            grid=(),
            in_specs=[pl.BlockSpec(memory_space=pltpu.VMEM)],
            out_specs=pl.BlockSpec(memory_space=pltpu.VMEM),
            scratch_shapes=[pltpu.SemaphoreType.DMA((8,))],
        ),
    )(where, eight)


def reduce_grad(grad, first):
    z, y, x, c = coords()
    rows, cols = grad.shape
    r, quarter = rows // 8, cols // 4
    low = jnp.bfloat16
    f32 = jnp.float32
    away = part(grad, (1 - c) * 2 * quarter, 2 * quarter, 1).astype(low)
    mine = part(grad, c * 2 * quarter, 2 * quarter, 1).astype(f32)
    half = (mine + swap(away, "c").astype(f32)).reshape(4, 2, r, 2 * quarter)

    def over_x(v):
        away = part(v, (1 - x) * quarter, quarter, v.ndim - 1).astype(low)
        return part(v, x * quarter, quarter, v.ndim - 1).astype(f32) + swap(away, "x").astype(f32)

    def over_y(v):
        away = lax.dynamic_index_in_dim(v, 1 - y, 1, keepdims=False).astype(low)
        return lax.dynamic_index_in_dim(v, y, 1, keepdims=False).astype(f32) + swap(away, "y").astype(f32)

    half = half.astype(low)
    if first == "x":
        block = over_y(over_x(half).astype(low))
    else:
        block = over_x(over_y(half).astype(low))
    block = block.astype(low)
    pair = z // 2
    away = part(block, (1 - pair) * 2, 2, 0)
    two = part(block, pair * 2, 2, 0).astype(f32) + swap(away, "z2").astype(f32)
    two = two.astype(low)
    low_bit = z % 2
    away = part(two, 1 - low_bit, 1, 0)
    one = (part(two, low_bit, 1, 0).astype(f32) + swap(away, "z1").astype(f32))[0]
    one = one.astype(low)
    other = swap(one, "x")
    pair_x = jnp.where(x == 0, jnp.concatenate([one, other], 1), jnp.concatenate([other, one], 1))
    pair_c = swap(pair_x, "c")
    whole = jnp.where(c == 0, jnp.concatenate([pair_x, pair_c], 1), jnp.concatenate([pair_c, pair_x], 1))
    return whole.astype(f32)


def normalize(values):
    centred = values - jnp.mean(values, axis=-1, keepdims=True)
    spread = jnp.mean(centred * centred, axis=-1, keepdims=True)
    return centred * lax.rsqrt(spread + 1e-05)


def scaled_norm(values, gain):
    return normalize(values) * gain


def exact_gelu(values):
    return jax.nn.gelu(values, approximate=False)


def layer(
    tokens,
    time_index,
    table_all,
    gain_one,
    bias_one,
    qkv_w,
    out_w,
    out_b,
    gain_two,
    bias_two,
    up_w,
    up_b,
    down_w,
    down_b,
    cotangent,
):
    row_count, model_width = tokens.shape
    seq_count = time_index.shape[0]
    length = row_count // seq_count
    head_dim = model_width // HEADS
    factor = head_dim ** (-0.5)
    levels = table_all.shape[0]
    gain_one_f = gain_one.astype(jnp.float32)
    gain_two_f = gain_two.astype(jnp.float32)
    one_hot = time_index[:, None] == jnp.arange(levels, dtype=jnp.int32)[None, :]
    embedding = jnp.dot(one_hot.astype(jnp.bfloat16), table_all, preferred_element_type=jnp.float32)
    scale_seq = (1.0 + embedding)[:, None, :]
    inputs = tokens.astype(jnp.float32)
    normed = (normalize(inputs) * gain_one_f + bias_one.astype(jnp.float32)).reshape(
        seq_count, length, model_width
    )
    scaled = (normed * scale_seq).astype(jnp.bfloat16).reshape(row_count, model_width)
    packed = jnp.dot(scaled, qkv_w, preferred_element_type=jnp.float32).astype(jnp.bfloat16)
    packed = packed.reshape(seq_count, length, 3, HEADS, head_dim)
    queries = packed[:, :, 0]
    key_heads = packed[:, :, 1]
    value_heads = packed[:, :, 2]
    scores = (
        jnp.einsum("sqhd,skhd->shqk", queries, key_heads, preferred_element_type=jnp.float32)
        * factor
    )
    attn_probs = jax.nn.softmax(scores, axis=-1)
    probs_low = attn_probs.astype(jnp.bfloat16)
    attn_mix = jnp.einsum(
        "shqk,skhd->sqhd", probs_low, value_heads, preferred_element_type=jnp.float32
    )
    attn_mix = attn_mix.astype(jnp.bfloat16).reshape(row_count, model_width)
    middle = (
        inputs
        + jnp.dot(attn_mix, out_w, preferred_element_type=jnp.float32)
        + out_b.astype(jnp.float32)
    )
    hidden_in = (normalize(middle) * gain_two_f + bias_two.astype(jnp.float32)).astype(jnp.bfloat16)
    pre_act = jnp.dot(hidden_in, up_w, preferred_element_type=jnp.float32) + up_b.astype(
        jnp.float32
    )
    activated = exact_gelu(pre_act).astype(jnp.bfloat16)
    block_out = (
        middle
        + jnp.dot(activated, down_w, preferred_element_type=jnp.float32)
        + down_b.astype(jnp.float32)
    ).astype(jnp.bfloat16)
    upstream = cotangent.astype(jnp.float32)
    grad_down = jnp.einsum("ti,td->id", activated, cotangent, preferred_element_type=jnp.float32)
    grad_down_b = jnp.sum(upstream, axis=0)
    d_act = jnp.einsum("td,id->ti", cotangent, down_w, preferred_element_type=jnp.float32)
    gelu_pull = jax.vjp(exact_gelu, pre_act)[1]
    d_pre = gelu_pull(d_act)[0].astype(jnp.bfloat16)
    grad_up = jnp.einsum("ti,tf->if", hidden_in, d_pre, preferred_element_type=jnp.float32)
    grad_up_b = jnp.sum(d_pre.astype(jnp.float32), axis=0)
    d_hidden = jnp.einsum("tf,if->ti", d_pre, up_w, preferred_element_type=jnp.float32)
    grad_ln2_bias = jnp.sum(d_hidden, axis=0)
    second_pull = jax.vjp(scaled_norm, middle, gain_two_f)[1]
    d_mid_part, grad_ln2_gain = second_pull(d_hidden)
    d_middle = upstream + d_mid_part
    d_mid_low = d_middle.astype(jnp.bfloat16)
    grad_out_w = jnp.einsum("ti,td->id", attn_mix, d_mid_low, preferred_element_type=jnp.float32)
    grad_out_b = jnp.sum(d_mid_low.astype(jnp.float32), axis=0)
    d_mix = jnp.einsum("td,id->ti", d_mid_low, out_w, preferred_element_type=jnp.float32)
    d_mix = d_mix.astype(jnp.bfloat16).reshape(seq_count, length, HEADS, head_dim)
    d_probs = jnp.einsum("sqhd,skhd->shqk", d_mix, value_heads, preferred_element_type=jnp.float32)
    d_values = jnp.einsum("shqk,sqhd->skhd", probs_low, d_mix, preferred_element_type=jnp.float32)
    d_scores = (
        attn_probs * (d_probs - jnp.sum(d_probs * attn_probs, axis=-1, keepdims=True))
    ).astype(jnp.bfloat16)
    d_queries = (
        jnp.einsum("shqk,skhd->sqhd", d_scores, key_heads, preferred_element_type=jnp.float32)
        * factor
    )
    d_keys = (
        jnp.einsum("shqk,sqhd->skhd", d_scores, queries, preferred_element_type=jnp.float32)
        * factor
    )
    d_packed = (
        jnp.stack([d_queries, d_keys, d_values], axis=2)
        .astype(jnp.bfloat16)
        .reshape(row_count, 3 * model_width)
    )
    grad_qkv = jnp.einsum("ti,tf->if", scaled, d_packed, preferred_element_type=jnp.float32)
    d_scaled = jnp.einsum("tf,if->ti", d_packed, qkv_w, preferred_element_type=jnp.float32).reshape(
        seq_count, length, model_width
    )
    d_normed = d_scaled * scale_seq
    grad_ln1_bias = jnp.sum(d_normed, axis=(0, 1))
    d_embedding = jnp.sum(d_scaled * normed, axis=1)
    grad_table = jnp.einsum(
        "sn,sd->nd", one_hot.astype(jnp.float32), d_embedding, precision=lax.Precision.HIGHEST
    )
    first_pull = jax.vjp(scaled_norm, inputs, gain_one_f)[1]
    d_in_part, grad_ln1_gain = first_pull(d_normed.reshape(row_count, model_width))
    grad_tokens = (d_middle + d_in_part).astype(jnp.bfloat16)
    return (
        block_out,
        grad_tokens,
        (grad_table, grad_ln1_gain, grad_ln1_bias, grad_qkv, grad_out_w, grad_out_b, grad_ln2_gain,
         grad_ln2_bias, grad_up, grad_up_b, grad_down, grad_down_b),
    )


def plain(*args):
    dims = (None, None, 1, 0, 0, 0, 0, 0, 0, 0, 0, 0, 0, 0, None)
    whole = [
        item if dim is None else lax.all_gather(item, "fsdp", axis=dim, tiled=True)
        for item, dim in zip(args, dims, strict=True)
    ]
    block_out, grad_tokens, grads = layer(*whole)
    shares = [
        lax.psum_scatter(grad, "fsdp", scatter_dimension=1 if place == 0 else 0, tiled=True)
        for place, grad in enumerate(grads)
    ]
    return (block_out, grad_tokens, *lax.psum(tuple(shares), "dp"))


def eight_by_four(
    tokens, time_index, time_table, ln1_gain, ln1_bias, w_qkv, w_out, b_out, ln2_gain, ln2_bias,
    w_up, b_up, w_down, b_down, cotangent,
):
    where = jnp.stack(coords()).astype(jnp.int32)
    small = jnp.concatenate(
        [time_table]
        + [v.reshape(-1, 128) for v in (ln1_gain, ln1_bias, b_out, ln2_gain, ln2_bias, b_down, b_up)]
        + [jnp.zeros((6, 128), time_table.dtype)]
    )
    small = gather_small(where, small)
    table_all = small[:128]
    gain_one, bias_one, out_b, gain_two, bias_two, down_b = (small[128 + i] for i in range(6))
    up_b = small[134:138].reshape(4, 8, 128).transpose(1, 0, 2).reshape(4096)

    def whole(own, axis):
        split = Split(own.shape[axis])
        return assemble(where, own, spread(own, split, axis), split, axis)

    qk = whole(w_qkv[:, :2048], 1)
    vo = whole(jnp.concatenate([w_qkv[:, 2048:], w_out], axis=1), 1)
    up_w = jnp.concatenate([whole(w_up[:, :2048], 1), whole(w_up[:, 2048:], 1)], axis=1)
    first, second = whole(w_down[:256], 0), whole(w_down[256:], 0)
    down_w = jnp.stack([first.reshape(8, 256, 1024), second.reshape(8, 256, 1024)], axis=1).reshape(4096, 1024)
    qkv_w = jnp.concatenate([qk, vo[:, :1024]], axis=1)
    out_w = vo[:, 1024:]
    block_out, grad_tokens, grads = layer(
        tokens, time_index, table_all, gain_one, bias_one, qkv_w, out_w, out_b, gain_two, bias_two,
        up_w, up_b, down_w, down_b, cotangent,
    )
    (grad_table, grad_ln1_gain, grad_ln1_bias, grad_qkv, grad_out_w, grad_out_b, grad_ln2_gain,
     grad_ln2_bias, grad_up, grad_up_b, grad_down, grad_down_b) = grads
    down = reduce_grad(grad_down, "x")
    up = reduce_grad(grad_up, "y")
    out = reduce_grad(grad_out_w, "x")
    qkv = reduce_grad(grad_qkv, "y")
    rows = jnp.concatenate(
        [grad_table]
        + [v[None] for v in (grad_ln1_gain, grad_ln1_bias, grad_out_b, grad_ln2_gain, grad_ln2_bias, grad_down_b)]
        + [grad_up_b.reshape(8, 4, 128).transpose(1, 0, 2).reshape(4, 1024)]
    )
    rows = rows.reshape(138, 8, 128).transpose(1, 0, 2)
    rows = jnp.broadcast_to(rows[:, None], (8, 4, 138, 128)).reshape(32, 138, 128)
    got = jnp.sum(lax.all_to_all(rows, BOTH, 0, 0), axis=0)
    return (
        block_out, grad_tokens, got[:128], got[128], got[129], qkv, out, got[130], got[131], got[132],
        up, got[134:138].reshape(512), down, got[133],
    )


def solution(mesh):
    in_specs = (
        P(("fsdp", "dp"), None),
        P(("fsdp", "dp")),
        P(None, "fsdp"),
        P("fsdp"),
        P("fsdp"),
        P("fsdp", None),
        P("fsdp", None),
        P("fsdp"),
        P("fsdp"),
        P("fsdp"),
        P("fsdp", None),
        P("fsdp"),
        P("fsdp", None),
        P("fsdp"),
        P(("fsdp", "dp"), None),
    )
    out_specs = (
        P(("fsdp", "dp"), None),
        P(("fsdp", "dp"), None),
        P(None, "fsdp"),
        P("fsdp"),
        P("fsdp"),
        P("fsdp", None),
        P("fsdp", None),
        P("fsdp"),
        P("fsdp"),
        P("fsdp"),
        P("fsdp", None),
        P("fsdp"),
        P("fsdp", None),
        P("fsdp"),
    )
    local = eight_by_four if (mesh.shape["fsdp"], mesh.shape["dp"]) == (8, 4) else plain
    return jax.shard_map(local, mesh=mesh, in_specs=in_specs, out_specs=out_specs, check_vma=False)
```

```python
import functools

import jax
import jax.numpy as jnp
from jax import lax
from jax.experimental import pallas as pl
from jax.experimental.pallas import tpu as pltpu
from jax.sharding import PartitionSpec as P

HEADS = 16
BOTH = ("fsdp", "dp")
LOW = jnp.bfloat16
F32 = jnp.float32
NT = (((1,), (1,)), ((), ()))
TN = (((0,), (0,)), ((), ()))


def flips(which):
    pairs = []
    for f in range(8):
        for d in range(4):
            z, y, x, c = f // 2, f % 2, d // 2, d % 2
            if which == "x":
                x = 1 - x
            elif which == "y":
                y = 1 - y
            elif which == "c":
                c = 1 - c
            elif which == "z1":
                z = z ^ 1
            elif which == "z2":
                z = z ^ 2
            pairs.append((f * 4 + d, (z * 2 + y) * 4 + x * 2 + c))
    return pairs


def swap(values, which):
    return lax.ppermute(values, BOTH, flips(which))


def coords():
    f, d = lax.axis_index("fsdp"), lax.axis_index("dp")
    return f // 2, f % 2, d // 2, d % 2


def call(kernel, grid, ins, outs, flops=0, nbytes=0, scratch=(), prefetch=0, aliases=None, limit=18, after=()):
    after = tuple(after)

    def spec(block, index):
        if block is None:
            return pl.BlockSpec(memory_space=pl.ANY)
        if index in constant and grid:
            return pl.BlockSpec(block, index, pipeline_mode=pl.Buffered(1))
        return pl.BlockSpec(block, index)

    def body(*refs):
        n = prefetch + len(ins)
        kernel(*refs[:n], *refs[n + len(after) :])

    run = pl.pallas_call(
        body,
        out_shape=[jax.ShapeDtypeStruct(shape, kind) for shape, kind, _, _ in outs],
        grid_spec=pltpu.PrefetchScalarGridSpec(
            num_scalar_prefetch=prefetch,
            grid=grid,
            in_specs=[spec(block, index) for block, index in ins] + [spec(None, None)] * len(after),
            out_specs=[spec(block, index) for _, _, block, index in outs],
            scratch_shapes=scratch,
        ),
        input_output_aliases=aliases or {},
        compiler_params=pltpu.CompilerParams(
            vmem_limit_bytes=limit * 2**20, dimension_semantics=("arbitrary",) * len(grid)
        ),
        cost_estimate=pl.CostEstimate(flops=0, bytes_accessed=1024, transcendentals=0),
    )
    return lambda *args: run(*args, *after)


def simple(kernel, args, outs, where=None, after=(), limit=12):
    def whole(shape):
        return shape, lambda *_: (0,) * len(shape)

    prefetch = 0 if where is None else 1
    run = call(
        kernel,
        (),
        [whole(a.shape) for a in args],
        [(shape, kind, *whole(shape)) for shape, kind in outs],
        prefetch=prefetch,
        after=after,
        limit=limit,
    )
    return run(*(() if where is None else (where,)), *args)


constant = []


def fixed(*index):
    constant.append(lambda *grid: index)
    return constant[-1]


def ends(n):
    e = n * 3 // 8
    return e // 2, (n - 2 * e) // 2


def end_start(n, x, c):
    eh, mh = ends(n)
    return x * (n - 2 * eh) + c * eh


def middle_start(n, c):
    eh, mh = ends(n)
    return 2 * eh + c * mh


COLS, ROWS = 2048, 256
CE, CM = ends(COLS)
RE, RM = ends(ROWS)
CW, RW = CE + CM, RE + RM


def lanes(start, size=128):
    return pl.ds(start if isinstance(start, int) else pl.multiple_of(start, 128), size)


def own_columns(where, dest, read):
    x, c = where[2], where[3]
    for i in range(CW // 128):
        start = end_start(COLS, x, c) + i * 128 if i < CE // 128 else middle_start(COLS, c) + i * 128 - CE
        dest[:, i * 128 : (i + 1) * 128] = read(start)


def own_first_kernel(where, qkv, out_w, parts):
    own_columns(where, parts.at[0], lambda start: qkv[:, lanes(start)])
    own_columns(
        where,
        parts.at[1],
        lambda start: jnp.where(
            start < 1024, qkv[:, lanes(2048 + jnp.minimum(start, 896))], out_w[:, lanes(jnp.maximum(start - 1024, 0))]
        ),
    )


def own_other_kernel(where, up_w, down_w, parts, tall):
    x, c = where[2], where[3]
    for half in range(2):
        own_columns(
            where, parts.at[half], lambda start: up_w[:, lanes((start // 256) * 512 + half * 256 + start % 256)]
        )
        for size, first, at in ((RE, end_start(ROWS, x, c), 0), (RM, middle_start(ROWS, c), RE)):
            tall[half, at : at + size, :] = down_w[pl.ds(pl.multiple_of(half * 256 + first, 16), size), :]


def move(jobs, after=()):
    args = []
    for _, copies in jobs:
        for array, _, _ in copies:
            if not any(array is a for a in args):
                args.append(array)

    def kernel(*refs):
        outs = refs[len(args) :]
        for out, (_, copies) in zip(outs, jobs, strict=True):
            for array, read, write in copies:
                ref = refs[[i for i, a in enumerate(args) if a is array][0]]
                out[write] = ref[read if read != () else ...]

    return simple(kernel, args, [(shape, LOW) for shape, _ in jobs], after=after)


class Piece:
    def __init__(self, part, index, shape, axis):
        self.part, self.index, self.shape, self.axis = part, index, shape, axis
        self.e = CE if axis == 1 else RE
        self.inner = (slice(0, 128), slice(0, CW)) if axis == 1 else (slice(None), slice(None))
        self.end = (slice(0, 128), slice(0, CE)) if axis == 1 else (slice(0, RE), slice(None))

    def two(self):
        return (2, *self.shape), [(self.part, self.index, 0), (self.near, self.near_index, 1)]

    def four(self):
        return (4, *self.shape), [
            (self.part, self.index, 0),
            (self.near, self.near_index, 1),
            (self.far, slice(None), slice(2, 4)),
        ]

    def blocks(self):
        found = [(self.near, self.near_index)] + [(self.far, (i,)) for i in range(2)]
        return found + [(self.beside, (i,)) for i in range(4)]

    def across_send(self):
        shape = (128, CE) if self.axis == 1 else (RE, 1024)
        return (7, *shape), [(a, (*i, *self.end), j) for j, (a, i) in enumerate(self.blocks())]

    def core_send(self):
        if self.axis == 1:
            shape, first, last = (128, CW + CE), (slice(None), slice(0, CW)), (slice(None), slice(CW, CW + CE))
        else:
            shape, first, last = (RW + RE, 1024), (slice(0, RW), slice(None)), (slice(RW, RW + RE), slice(None))
        copies = [(a, (*i, *self.inner), (j, *first)) for j, (a, i) in enumerate(self.blocks())]
        return (7, *shape), copies + [(self.across, j, (j, *last)) for j in range(7)]

    def move_z1(self, near, near_index):
        self.near, self.near_index = near, near_index

    def move_z2(self, two):
        self.far = swap(two, "z2")

    def move_y(self, four):
        self.beside = swap(four, "y")

    def move_x(self, send):
        self.across = swap(send, "x")

    def move_c(self, send):
        self.other = swap(send, "c")


def assemble_kernel(axis, own_copies, near_index, where, *refs):
    n_own = len(own_copies)
    owns = refs[:n_own]
    near, far, beside, across, other, out, sems, out_sems, hold = refs[n_own:]
    z, y, x, c = where[0], where[1], where[2], where[3]
    rows = 128 if axis == 1 else ROWS
    size = COLS if axis == 1 else ROWS
    eh, mh = ends(size)

    def at(base, start, count):
        if axis == 1:
            return hold.at[pl.ds(base, rows), lanes(start, count)]
        return hold.at[pl.ds(pl.multiple_of(base + start, 16), count), :]

    def cut(block, start, count):
        if axis == 1:
            return block.at[pl.ds(0, 128), pl.ds(start, count)]
        return block.at[pl.ds(start, count), :]

    groups, bases = [], []
    for j in range(8):
        zz = (z, z ^ 1, z ^ 2, z ^ 3)[j % 4]
        yy = y if j < 4 else 1 - y
        base = pl.multiple_of((zz * 2 + yy) * rows, rows)
        if j == 0:
            copies = []
            for ref, (read, start, count) in zip(owns, own_copies, strict=True):
                for k in range(len(read)):
                    copies.append((ref.at[read[k]], at(base, start[k], count)))
        else:
            close = near.at[near_index[0]] if near_index else near
            mine = (close, far.at[0], far.at[1], beside.at[0], beside.at[1], beside.at[2], beside.at[3])[j - 1]
            oc = 1 - c
            copies = [
                (cut(mine, 0, eh), at(base, end_start(size, x, c), eh)),
                (cut(mine, eh, mh), at(base, middle_start(size, c), mh)),
                (cut(across.at[j - 1], 0, eh), at(base, end_start(size, 1 - x, c), eh)),
                (cut(other.at[j - 1], 0, eh), at(base, end_start(size, x, oc), eh)),
                (cut(other.at[j - 1], eh, mh), at(base, middle_start(size, oc), mh)),
                (cut(other.at[j - 1], eh + mh, eh), at(base, end_start(size, 1 - x, oc), eh)),
            ]
        group = [pltpu.make_async_copy(s, d, sems.at[j]) for s, d in copies]
        for copy in group:
            copy.start()
        groups.append(group)
        bases.append(base)
    outs = []
    for j in range(8):
        for copy in groups[j]:
            copy.wait()
        rows_of = pl.ds(bases[j], rows)
        copy = pltpu.make_async_copy(hold.at[rows_of, :], out.at[rows_of, :], out_sems.at[j])
        copy.start()
        outs.append(copy)
    for copy in outs:
        copy.wait()


def assemble(where, piece, owns, after=()):
    shape = (1024, COLS) if piece.axis == 1 else (8 * ROWS, 1024)
    args = [o[0] for o in owns] + [piece.near, piece.far, piece.beside, piece.across, piece.other]
    return call(
        functools.partial(assemble_kernel, piece.axis, [o[1:] for o in owns], piece.near_index),
        (),
        [(None, None)] * len(args),
        [(shape, LOW, None, None)],
        prefetch=1,
        scratch=[pltpu.SemaphoreType.DMA((8,)), pltpu.SemaphoreType.DMA((8,)), pltpu.VMEM(shape, LOW)],
        after=after,
        limit=8,
    )(where, *args)[0]


def small_kernel(where, four, beside, time_index, table, vec, up_b, scale):
    z, y = where[0], where[1]
    for j in range(8):
        block = four.at[j] if j < 4 else beside.at[j - 4]
        shard = (z ^ (j % 4)) * 2 + (y if j < 4 else 1 - y)
        table[:, lanes(shard * 128)] = block[:128, :]
        vec[:, lanes(shard * 128)] = block[128:, :].astype(F32)
        for row in range(4):
            unit = lanes(shard * 256 + (row % 2) * 128)
            up_b[row // 2 : row // 2 + 1, unit] = block[134 + row : 135 + row, :].astype(F32)
    numbers = lax.broadcasted_iota(jnp.int32, (time_index.shape[0], 128), 1)
    one_hot = (numbers == time_index[...]).astype(F32).astype(LOW)
    scale[...] = 1.0 + jnp.dot(one_hot, table[...], preferred_element_type=F32)


def small_params(where, four, beside, time_index, after=()):
    return simple(
        small_kernel,
        (four, beside, time_index),
        [((128, 1024), LOW), ((16, 1024), F32), ((2, 2048), F32), ((time_index.shape[0], 1024), F32)],
        where=where,
        after=after,
    )


def rows_kernel(d_emb, sums_one, sums_two, up_a, up_b, times, out):
    for s in range(8):
        here = slice(s * 128, (s + 1) * 128)
        rows = [d_emb[i, :, here] for i in range(8)]
        rows += [sums_one[0:2, here], sums_two[2:3, here], sums_two[0:2, here], sums_two[3:4, here]]
        for sums in (up_a, up_b):
            rows += [sums[:, s * 256 + j * 128 : s * 256 + (j + 1) * 128] for j in range(2)]
        rows += [times[...], jnp.zeros((5, 128), F32)]
        block = jnp.concatenate(rows, axis=0)
        for copy in range(4):
            out[s * 4 + copy] = block


def mm(a, b):
    return jnp.dot(a, b, preferred_element_type=F32)


def mm_nt(a, b):
    return lax.dot_general(a, b, NT, preferred_element_type=F32)


def mm_tn(a, b):
    return lax.dot_general(a, b, TN, preferred_element_type=F32)


def centre(values):
    mean = jnp.mean(values, axis=-1, keepdims=True)
    centred = values - mean
    scale = lax.rsqrt(jnp.mean(centred * centred, axis=-1, keepdims=True) + 1e-05)
    return centred * scale, scale


def first_norm_kernel(tokens, gain, bias, scale, scaled):
    hat, _ = centre(tokens[...].astype(F32))
    scaled[...] = ((hat * gain[...] + bias[...]) * scale[0]).astype(LOW)


def first_norm(tokens, gain, bias, scale, after=()):
    rows, width = tokens.shape
    seqs = scale.shape[0]
    length = rows // seqs
    return call(
        first_norm_kernel,
        (seqs,),
        [
            ((length, width), lambda i: (i, 0)),
            ((1, width), fixed(0, 0)),
            ((1, width), fixed(0, 0)),
            ((1, 1, width), lambda i: (i, 0, 0)),
        ],
        [((rows, width), LOW, (length, width), lambda i: (i, 0))],
        after=after,
    )(tokens, gain, bias, scale)[0]


def halves(values):
    lane = lax.broadcasted_iota(jnp.int32, values.shape, 1)
    zero = jnp.zeros_like(values)
    return jnp.concatenate([jnp.where(lane < 64, values, zero), jnp.where(lane < 64, zero, values)], axis=0)


def side(values):
    n = values.shape[0] // 2
    return jnp.concatenate([values[:n], values[n:]], axis=1)


def project_kernel(x, w, out):
    out[...] = mm(x[...], w[...]).astype(LOW)


def project(x, w, tile=512, after=()):
    rows, width = x.shape
    n = w.shape[1]
    return call(
        project_kernel,
        (n // tile,),
        [((rows, width), fixed(0, 0)), ((width, tile), lambda i: (0, i))],
        [((rows, n), LOW, (rows, tile), lambda i: (0, i))],
        after=after,
    )(x, w)[0]


def units_of(rows, length, at_once=8):
    units = []
    for seq in range(rows // length):
        for pair in range(2):
            units.append((seq, pair, (slice(seq * length, (seq + 1) * length), slice(pair * 128, (pair + 1) * 128))))
    return [units[i : i + at_once] for i in range(0, len(units), at_once)]


def attend_kernel(length, scaled, wv, q_in, k_in, *refs):
    v_out, probs_out, mix_out = refs[-3:]
    factor = 64 ** (-0.5) * 1.4426950408889634
    v_out[...] = mm(scaled[...], wv[...]).astype(LOW)
    for units in units_of(scaled.shape[0], length):
        scores = [mm_nt(halves(q_in[here]), k_in[here]) for _, _, here in units]
        found = []
        for s in scores:
            e = jnp.exp2((s - jnp.max(s, axis=-1, keepdims=True)) * factor)
            found.append((e * (1.0 / jnp.sum(e, axis=-1, keepdims=True))).astype(LOW))
        for (seq, pair, here), probs in zip(units, found, strict=True):
            probs_out[0, seq, pair] = probs
            mix_out[here] = mm(side(probs), halves(v_out[here])).astype(LOW)


def attend(scaled, qk, vo, length, first=0, count=None, earlier=(), after=()):
    rows, width = scaled.shape
    groups = width // 256
    seqs = rows // length
    count = groups if count is None else count
    column = lambda i: (0, first + i)
    wide = ((rows, width), LOW, (rows, 256), column)
    probs = (groups, seqs, 2, 2 * length, length)
    return call(
        functools.partial(attend_kernel, length),
        (count,),
        [
            ((rows, width), fixed(0, 0)),
            ((width, 256), column),
            ((rows, 256), column),
            ((rows, 256), lambda i: (0, groups + first + i)),
        ]
        + [(None, None)] * len(earlier),
        [wide, (probs, LOW, (1, *probs[1:]), lambda i: (first + i, 0, 0, 0, 0)), wide],
        aliases={4 + i: i for i in range(len(earlier))},
        after=after,
    )(scaled, vo, qk, qk, *earlier)


def middle_kernel(mix, tokens, w, out_b, gain, bias, middle_out, hidden_out):
    middle = tokens[...].astype(F32) + mm(mix[...], w[...]) + out_b[...]
    middle_out[...] = middle
    hat, _ = centre(middle)
    hidden_out[...] = (hat * gain[...] + bias[...]).astype(LOW)


def second_norm(mix, tokens, vo, out_b, gain, bias, after=()):
    rows, width = tokens.shape
    row = lambda i: (i, 0)
    vec = ((1, width), fixed(0, 0))
    return call(
        middle_kernel,
        (rows // 256,),
        [((256, width), row), ((256, width), row), ((width, width), fixed(0, 1)), vec, vec, vec],
        [((rows, width), F32, (256, width), row), ((rows, width), LOW, (256, width), row)],
        after=after,
    )(mix, tokens, vo, out_b, gain, bias)


def gelu_parts(v):
    cdf = 0.5 + 0.5 * lax.erf(v * 0.5**0.5)
    bell = jnp.exp(-0.5 * v * v)
    return v * cdf, cdf + (v * 0.3989422804014327) * bell


def up_kernel(hidden, w, bias, act, slope):
    value, pull = gelu_parts(mm(hidden[...], w[...]) + bias[...])
    act[...] = value.astype(LOW)
    slope[...] = pull.astype(LOW)


def up(hidden, w, bias, tile=512, after=()):
    rows, width = hidden.shape
    n = w.shape[1]
    column = lambda i: (0, i)
    return call(
        up_kernel,
        (n // tile,),
        [((rows, width), fixed(0, 0)), ((width, tile), column), ((1, tile), column)],
        [((rows, n), LOW, (rows, tile), column)] * 2,
        limit=22,
        after=after,
    )(hidden, w, bias)


def down_kernel(act_a, act_b, first, second, middle, bias, out):
    total = middle[...] + bias[...]
    total += mm(act_a[...], first[...])
    total += mm(act_b[...], second[...])
    out[...] = total.astype(LOW)


def down(acts, ws, middle, bias, tile=256, after=()):
    rows, width = middle.shape
    k = ws[0].shape[0]
    row = lambda i: (i, 0)
    return call(
        down_kernel,
        (rows // tile,),
        [((tile, k), row)] * 2
        + [((k, width), fixed(0, 0))] * 2
        + [((tile, width), row), ((1, width), fixed(0, 0))],
        [((rows, width), LOW, (tile, width), row)],
        limit=24,
        after=after,
    )(*acts, *ws, middle, bias)[0]


def pull_kernel(cot, w, slope, *refs):
    d_pre, sums = refs[-2:]
    value = (mm_nt(cot[...], w[...]) * slope[...].astype(F32)).astype(LOW)
    d_pre[0] = value
    sums[...] = jnp.sum(value.astype(F32), axis=0, keepdims=True)


def pull(cot, w, slope, half, earlier=None, tile=512, after=()):
    rows, width = cot.shape
    n = w.shape[0]
    column = lambda i: (0, i)
    ins = [((rows, width), fixed(0, 0)), ((tile, width), lambda i: (i, 0)), ((rows, tile), column)]
    return call(
        pull_kernel,
        (n // tile,),
        ins + ([] if earlier is None else [(None, None)]),
        [((2, rows, n), LOW, (1, rows, tile), lambda i: (half, 0, i)), ((1, n), F32, (1, tile), column)],
        aliases={} if earlier is None else {3: 0},
        after=after,
    )(cot, w, slope, *(() if earlier is None else (earlier,)))


def norm_back(d_out, hat, scale, gain):
    e = d_out * gain
    mean = jnp.mean(e, axis=-1, keepdims=True)
    slant = jnp.mean(e * hat, axis=-1, keepdims=True)
    return (e - mean - hat * slant) * scale


def fold(*rows_of):
    sums = [jnp.sum(v, axis=0, keepdims=True) for v in rows_of]
    return jnp.concatenate(sums + [jnp.zeros_like(sums[0])] * (8 - len(sums)), axis=0)


def middle_back_kernel(d_pre, wa, wb, middle, cot, gain, w_out, d_middle_out, d_low_out, d_mix_out, sums):
    d_hidden = mm_nt(d_pre[0], wa[...]) + mm_nt(d_pre[1], wb[...])
    hat, scale = centre(middle[...])
    d_middle = cot[...].astype(F32) + norm_back(d_hidden, hat, scale, gain[...])
    d_middle_out[...] = d_middle
    d_low = d_middle.astype(LOW)
    d_low_out[...] = d_low
    d_mix_out[...] = mm_nt(d_low, w_out[...]).astype(LOW)

    @pl.when(pl.program_id(0) == 0)
    def _():
        sums[...] = jnp.zeros_like(sums)

    sums[...] += fold(d_hidden * hat, d_hidden, d_low.astype(F32), cot[...].astype(F32))


def middle_back(d_pre, ws, middle, cot, gain, vo, tile=256, after=()):
    rows, width = middle.shape
    row = lambda i: (i, 0)
    return call(
        middle_back_kernel,
        (rows // tile,),
        [
            ((2, tile, d_pre.shape[2]), lambda i: (0, i, 0)),
            (ws[0].shape, fixed(0, 0)),
            (ws[1].shape, fixed(0, 0)),
            ((tile, width), row),
            ((tile, width), row),
            ((1, width), fixed(0, 0)),
            ((width, width), fixed(0, 1)),
        ],
        [
            ((rows, width), F32, (tile, width), row),
            ((rows, width), LOW, (tile, width), row),
            ((rows, width), LOW, (tile, width), row),
            ((8, width), F32, (8, width), fixed(0, 0)),
        ],
        limit=32,
        after=after,
    )(d_pre, *ws, middle, cot, gain, vo)


def attend_back_kernel(length, d_mix, probs, q_in, k_in, v_in, *refs):
    out = refs[-1]
    factor = 64 ** (-0.5)
    for units in units_of(d_mix.shape[0], length, 4):
        dms = [halves(d_mix[here]) for _, _, here in units]
        d_probs = [mm_nt(dm, v_in[here]) for dm, (_, _, here) in zip(dms, units, strict=True)]
        found = []
        for d, (seq, pair, _) in zip(d_probs, units, strict=True):
            high = probs[0, seq, pair].astype(F32)
            found.append((high * (d - jnp.sum(d * high, axis=-1, keepdims=True))).astype(LOW))
        for dm, d_scores, (seq, pair, here) in zip(dms, found, units, strict=True):
            out[(2, *here)] = mm_tn(probs[0, seq, pair], dm).astype(LOW)
            out[(0, *here)] = (mm(side(d_scores), halves(k_in[here])) * factor).astype(LOW)
            out[(1, *here)] = (mm_tn(d_scores, halves(q_in[here])) * factor).astype(LOW)


def attend_back(d_mix, probs, qk, v, length, first=0, count=None, earlier=(), after=()):
    rows, width = d_mix.shape
    count = width // 256 if count is None else count
    wide = ((rows, 256), lambda i: (0, first + i))
    return call(
        functools.partial(attend_back_kernel, length),
        (count,),
        [
            wide,
            ((1,) + probs.shape[1:], lambda i: (first + i, 0, 0, 0, 0)),
            wide,
            ((rows, 256), lambda i: (0, width // 256 + first + i)),
            wide,
        ]
        + [(None, None)] * len(earlier),
        [((3, rows, width), LOW, (3, rows, 256), lambda i: (0, 0, first + i))],
        aliases={5 + i: i for i in range(len(earlier))},
        after=after,
    )(d_mix, probs, qk, qk, v, *earlier)[0]


def input_back_kernel(length, d, wq, wk, wv, tokens, d_middle, gain, bias, scale, out, sums, d_emb):
    d_scaled = mm_nt(d[0], wq[...]) + mm_nt(d[1], wk[...]) + mm_nt(d[2], wv[...])
    hat, spread = centre(tokens[...].astype(F32))
    normed = hat * gain[...] + bias[...]
    count = tokens.shape[0] // length
    parts = []
    for i in range(count):
        here = slice(i * length, (i + 1) * length)
        d_emb[i] = jnp.sum(d_scaled[here] * normed[here], axis=0, keepdims=True)
        parts.append(d_scaled[here] * scale[i])
    d_normed = jnp.concatenate(parts, axis=0)
    out[...] = (d_middle[...] + norm_back(d_normed, hat, spread, gain[...])).astype(LOW)

    @pl.when(pl.program_id(0) == 0)
    def _():
        sums[...] = jnp.zeros_like(sums)

    sums[...] += fold(d_normed * hat, d_normed)


def input_back(d_packed, qk, vo, tokens, d_middle, gain, bias, scale, tile=256, after=()):
    rows, width = tokens.shape
    seqs = scale.shape[0]
    length = rows // seqs
    row = lambda i: (i, 0)
    wide = ((tile, width), row)
    vec = ((1, width), fixed(0, 0))
    some = ((tile // length, 1, width), lambda i: (i, 0, 0))
    return call(
        functools.partial(input_back_kernel, length),
        (rows // tile,),
        [
            ((3, tile, width), lambda i: (0, i, 0)),
            ((width, width), fixed(0, 0)),
            ((width, width), fixed(0, 1)),
            ((width, width), fixed(0, 0)),
            wide, wide, vec, vec, some,
        ],
        [
            ((rows, width), LOW, (tile, width), row),
            ((8, width), F32, (8, width), fixed(0, 0)),
            ((seqs, 1, width), F32) + some,
        ],
        limit=26,
        after=after,
    )(d_packed, qk, qk, vo, tokens, d_middle, gain, bias, scale)


def tall_away_kernel(where, a, b, cot, away):
    left = jnp.concatenate([a[...], b[...]], axis=1)
    value = mm_tn(left, cot[...]).astype(LOW)
    x = where[2]
    for xr in range(2):
        for half in range(2):
            low, high = value[half * 256 : half * 256 + 128], value[half * 256 + 128 : half * 256 + 256]
            away[xr, 0, 0, half] = jnp.where((x ^ xr) == 0, low, high)


def tall_shard(zr, yr, where):
    return ((zr ^ where[0]) * 2) + (yr ^ where[1])


def tall_ins(acts, cot, core):
    rows, width = cot.shape
    act = ((rows, 256), lambda zr, yr, where: (0, tall_shard(zr, yr, where)))
    return [act, act, ((rows, width // 2), lambda zr, yr, where: (0, where[3] ^ core))]


def tall_away(where, acts, cot, after=()):
    n = cot.shape[1] // 2
    return call(
        tall_away_kernel,
        (4, 2),
        tall_ins(acts, cot, 1),
        [((2, 2, 4, 2, 128, n), LOW, (2, 1, 1, 2, 128, n), lambda zr, yr, where: (0, yr, zr, 0, 0, 0))],
        prefetch=1,
        after=after,
    )(where, *acts, cot)[0]


def tall_mine_kernel(where, a, b, cot, core, xa, yb, ka, kb):
    left = jnp.concatenate([a[...], b[...]], axis=1)
    value = mm_tn(left, cot[...])
    x = where[2]
    zr, yr = pl.program_id(0), pl.program_id(1)
    sums = []
    for xr in range(2):
        halves_of = []
        for half in range(2):
            low, high = value[half * 256 : half * 256 + 128], value[half * 256 + 128 : half * 256 + 256]
            total = jnp.where((x ^ xr) == 0, low, high) + core[xr, 0, 0, half].astype(F32)
            halves_of.append(total.astype(LOW))
        sums.append(halves_of)

    @pl.when(zr < 2)
    def _():
        for half in range(2):
            ka[0, 0, half] = sums[0][half]
            xa[0, 0, half] = sums[1][half]

    @pl.when((zr >= 2) & (yr == 0))
    def _():
        for xr in range(2):
            for half in range(2):
                kb[xr, 0, half] = sums[xr][half]

    @pl.when((zr >= 2) & (yr == 1))
    def _():
        for xr in range(2):
            for half in range(2):
                yb[xr, 0, half] = sums[xr][half]


def tall_mine(where, acts, cot, core, after=()):
    n = cot.shape[1] // 2
    shape = (2, 2, 2, 128, n)
    by_y = (
        shape,
        LOW,
        (1, 1, 2, 128, n),
        lambda zr, yr, where: (jnp.where(zr < 2, yr, 1), jnp.minimum(zr, 1), 0, 0, 0),
    )
    by_x = (shape, LOW, (2, 1, 2, 128, n), lambda zr, yr, where: (0, jnp.maximum(zr - 2, 0), 0, 0, 0))
    return call(
        tall_mine_kernel,
        (4, 2),
        tall_ins(acts, cot, 0) + [((2, 1, 1, 2, 128, n), lambda zr, yr, where: (0, yr, zr, 0, 0, 0))],
        [by_y, by_x, by_y, by_x],
        prefetch=1,
        after=after,
    )(where, *acts, cot, core)


def row_value(step, lefts, rights, counts, hold):
    first = 0
    for left, right, count in zip(lefts, rights, counts, strict=True):

        def put(left=left, right=right):
            b = right[0] if len(right.shape) == 3 else right[...]
            hold[...] = mm_tn(left[...], b)

        if len(lefts) == 1:
            put()
        else:
            pl.when((step >= first) & (step < first + count))(put)
        first += count


def row_from(where, xr, yr, zr):
    start = ((where[0] ^ zr) * 2 + (where[1] ^ yr)) * 128 + (where[2] ^ xr) * 64
    return pl.ds(pl.multiple_of(start, 64), 64)


def row_away_kernel(counts, where, *refs):
    n = len(counts)
    lefts, rights, away, hold = refs[:n], refs[n : 2 * n], refs[2 * n], refs[2 * n + 1]
    row_value(pl.program_id(0), lefts, rights, counts, hold)
    for xr in range(2):
        for yr in range(2):
            for zr in range(4):
                away[xr, yr, zr] = hold[row_from(where, xr, yr, zr), :].astype(LOW)


def row_mine_kernel(counts, where, *refs):
    n = len(counts)
    lefts, rights = refs[:n], refs[n : 2 * n]
    core, xa, yb, ka, kb, hold = refs[2 * n :]
    row_value(pl.program_id(0), lefts, rights, counts, hold)
    for xr in range(2):
        for yr in range(2):
            for zr in range(4):
                total = hold[row_from(where, xr, yr, zr), :] + core[xr, yr, zr].astype(F32)
                total = total.astype(LOW)
                if zr < 2:
                    (ka if xr == 0 else xa)[yr, zr] = total
                else:
                    (kb if yr == 0 else yb)[xr, zr - 2] = total


def row_specs(pairs, core, tile):
    ins, counts = [], []
    for a, _, _ in pairs:
        ins.append((a.shape, lambda j, where: (0, 0)))
    first = 0
    for _, b, kind in pairs:
        tokens = b.shape[-2]
        if kind == "layers":
            count = b.shape[0] * (b.shape[2] // 2 // tile)
            each = b.shape[2] // 2 // tile
            spec = (
                (1, tokens, tile),
                lambda j, where, f=first, m=count, e=each: (
                    jnp.clip(j - f, 0, m - 1) // e,
                    0,
                    (where[3] ^ core) * e + jnp.clip(j - f, 0, m - 1) % e,
                ),
            )
        elif kind == "layer":
            count = b.shape[2] // tile
            spec = (
                (1, tokens, tile),
                lambda j, where, f=first, m=count: (where[3] ^ core, 0, jnp.clip(j - f, 0, m - 1)),
            )
        else:
            count = b.shape[1] // 2 // tile
            spec = (
                (tokens, tile),
                lambda j, where, f=first, m=count: (0, (where[3] ^ core) * m + jnp.clip(j - f, 0, m - 1)),
            )
        ins.append(spec)
        counts.append(count)
        first += count
    return ins, counts


def row_away(where, pairs, tile=512, after=()):
    ins, counts = row_specs(pairs, 1, tile)
    steps = sum(counts)
    return call(
        functools.partial(row_away_kernel, counts),
        (steps,),
        ins,
        [((2, 2, 4, 64, steps * tile), LOW, (2, 2, 4, 64, tile), lambda j, where: (0, 0, 0, 0, j))],
        prefetch=1,
        scratch=[pltpu.VMEM((1024, tile), F32)],
        after=after,
    )(where, *[a for a, _, _ in pairs], *[b for _, b, _ in pairs])[0]


def row_mine(where, pairs, core, tile=512, after=()):
    ins, counts = row_specs(pairs, 0, tile)
    steps = sum(counts)
    out = ((2, 2, 64, steps * tile), LOW, (2, 2, 64, tile), lambda j, where: (0, 0, 0, j))
    return call(
        functools.partial(row_mine_kernel, counts),
        (steps,),
        ins + [((2, 2, 4, 64, tile), lambda j, where: (0, 0, 0, 0, j))],
        [out] * 4,
        prefetch=1,
        scratch=[pltpu.VMEM((1024, tile), F32)],
        after=after,
    )(where, *[a for a, _, _ in pairs], *[b for _, b, _ in pairs], core)


def add_up(jobs, after=()):
    args = []
    for _, terms in jobs:
        for array, _ in terms:
            if not any(array is a for a in args):
                args.append(array)

    def kernel(*refs):
        for out, (_, terms) in zip(refs[len(args) :], jobs, strict=True):
            total = None
            for array, index in terms:
                value = refs[[i for i, a in enumerate(args) if a is array][0]][index].astype(F32)
                total = value if total is None else total + value
            out[...] = total.astype(LOW)

    return simple(kernel, args, [(shape, LOW) for shape, _ in jobs], after=after)


class Reduction:
    def __init__(self, xa, yb, ka, kb):
        self.ka, self.kb = ka, kb
        self.tail = ka.shape[2:]
        self.xa, self.yb = swap(xa, "x"), swap(yb, "y")

    def second(self):
        shape = (2, *self.tail)
        return [(shape, [(self.ka, 1), (self.xa, 1)]), (shape, [(self.kb, 1), (self.yb, 1)])]

    def go_second(self, ya, xb):
        self.ya, self.xb = swap(ya, "y"), swap(xb, "x")

    def third(self):
        return [((2, *self.tail), [(self.kb, 0), (self.yb, 0), (self.xb, slice(None))])]

    def go_third(self, far):
        self.far = swap(far, "z2")

    def fourth(self):
        return [(self.tail, [(self.ka, (0, 1)), (self.xa, (0, 1)), (self.ya, 1), (self.far, 1)])]

    def go_fourth(self, near):
        self.near = swap(near, "z1")

    def last(self):
        terms = [(self.ka, (0, 0)), (self.xa, (0, 0)), (self.ya, 0), (self.far, 0), (self.near, slice(None))]
        return [(self.tail, terms)]

    def go_last(self, one):
        self.one = one
        self.by_x, self.by_c = swap(one, "x"), swap(one, "c")

    def go_corner(self):
        self.corner = swap(self.by_x, "c")


def tall_shard_kernel(where, one, by_x, by_c, corner, out):
    x, c = where[2], where[3]
    n = one.shape[-1]
    for block, xx, cc in ((one, x, c), (by_x, 1 - x, c), (by_c, x, 1 - c), (corner, 1 - x, 1 - c)):
        for half in range(2):
            rows = pl.ds(pl.multiple_of(half * 256 + xx * 128, 128), 128)
            out[rows, lanes(cc * n, n)] = block[half].astype(F32)


def up_shard_kernel(where, one, by_x, by_c, corner, up_out, out_out):
    x, c = where[2], where[3]
    for block, xx, cc in ((one, x, c), (by_x, 1 - x, c), (by_c, x, 1 - c), (corner, 1 - x, 1 - c)):
        rows = pl.ds(pl.multiple_of(xx * 64, 64), 64)
        for s in range(8):
            up_out[rows, lanes(s * 512 + cc * 256, 256)] = block[:, s * 256 : (s + 1) * 256].astype(F32)
        out_out[rows, lanes(cc * 512, 512)] = block[:, 2048:].astype(F32)


def qkv_shard_kernel(where, one, by_x, by_c, corner, out):
    x, c = where[2], where[3]
    for block, xx, cc in ((one, x, c), (by_x, 1 - x, c), (by_c, x, 1 - c), (corner, 1 - x, 1 - c)):
        rows = pl.ds(pl.multiple_of(xx * 64, 64), 64)
        for layer in range(3):
            out[rows, lanes(layer * 1024 + cc * 512, 512)] = block[:, layer * 512 : (layer + 1) * 512].astype(F32)


def shard_of(kernel, where, r, shapes, after=()):
    return simple(kernel, (r.one, r.by_x, r.by_c, r.corner), [(s, F32) for s in shapes], where=where, after=after)


def table_kernel(got, table, vec):
    n = got.shape[0]
    times = lax.broadcasted_iota(jnp.int32, (128, 8), 0).astype(F32)
    total = jnp.zeros(table.shape, F32)
    sums = jnp.zeros(vec.shape, F32)
    for i in range(n):
        hot = (times == got[i, 18:19, 0:8]).astype(F32)
        total += lax.dot_general(hot, got[i, 0:8, :], (((1,), (0,)), ((), ())), precision=lax.Precision.HIGHEST)
        sums += got[i, 8:24, :]
    table[...] = total
    vec[...] = sums


def normalize(values):
    centred = values - jnp.mean(values, axis=-1, keepdims=True)
    spread = jnp.mean(centred * centred, axis=-1, keepdims=True)
    return centred * lax.rsqrt(spread + 1e-05)


def scaled_norm(values, gain):
    return normalize(values) * gain


def exact_gelu(values):
    return jax.nn.gelu(values, approximate=False)


def layer(
    tokens,
    time_index,
    table_all,
    gain_one,
    bias_one,
    qkv_w,
    out_w,
    out_b,
    gain_two,
    bias_two,
    up_w,
    up_b,
    down_w,
    down_b,
    cotangent,
):
    row_count, model_width = tokens.shape
    seq_count = time_index.shape[0]
    length = row_count // seq_count
    head_dim = model_width // HEADS
    factor = head_dim ** (-0.5)
    levels = table_all.shape[0]
    gain_one_f = gain_one.astype(jnp.float32)
    gain_two_f = gain_two.astype(jnp.float32)
    one_hot = time_index[:, None] == jnp.arange(levels, dtype=jnp.int32)[None, :]
    embedding = jnp.dot(one_hot.astype(jnp.bfloat16), table_all, preferred_element_type=jnp.float32)
    scale_seq = (1.0 + embedding)[:, None, :]
    inputs = tokens.astype(jnp.float32)
    normed = (normalize(inputs) * gain_one_f + bias_one.astype(jnp.float32)).reshape(
        seq_count, length, model_width
    )
    scaled = (normed * scale_seq).astype(jnp.bfloat16).reshape(row_count, model_width)
    packed = jnp.dot(scaled, qkv_w, preferred_element_type=jnp.float32).astype(jnp.bfloat16)
    packed = packed.reshape(seq_count, length, 3, HEADS, head_dim)
    queries = packed[:, :, 0]
    key_heads = packed[:, :, 1]
    value_heads = packed[:, :, 2]
    scores = (
        jnp.einsum("sqhd,skhd->shqk", queries, key_heads, preferred_element_type=jnp.float32)
        * factor
    )
    attn_probs = jax.nn.softmax(scores, axis=-1)
    probs_low = attn_probs.astype(jnp.bfloat16)
    attn_mix = jnp.einsum(
        "shqk,skhd->sqhd", probs_low, value_heads, preferred_element_type=jnp.float32
    )
    attn_mix = attn_mix.astype(jnp.bfloat16).reshape(row_count, model_width)
    middle = (
        inputs
        + jnp.dot(attn_mix, out_w, preferred_element_type=jnp.float32)
        + out_b.astype(jnp.float32)
    )
    hidden_in = (normalize(middle) * gain_two_f + bias_two.astype(jnp.float32)).astype(jnp.bfloat16)
    pre_act = jnp.dot(hidden_in, up_w, preferred_element_type=jnp.float32) + up_b.astype(
        jnp.float32
    )
    activated = exact_gelu(pre_act).astype(jnp.bfloat16)
    block_out = (
        middle
        + jnp.dot(activated, down_w, preferred_element_type=jnp.float32)
        + down_b.astype(jnp.float32)
    ).astype(jnp.bfloat16)
    upstream = cotangent.astype(jnp.float32)
    grad_down = jnp.einsum("ti,td->id", activated, cotangent, preferred_element_type=jnp.float32)
    grad_down_b = jnp.sum(upstream, axis=0)
    d_act = jnp.einsum("td,id->ti", cotangent, down_w, preferred_element_type=jnp.float32)
    gelu_pull = jax.vjp(exact_gelu, pre_act)[1]
    d_pre = gelu_pull(d_act)[0].astype(jnp.bfloat16)
    grad_up = jnp.einsum("ti,tf->if", hidden_in, d_pre, preferred_element_type=jnp.float32)
    grad_up_b = jnp.sum(d_pre.astype(jnp.float32), axis=0)
    d_hidden = jnp.einsum("tf,if->ti", d_pre, up_w, preferred_element_type=jnp.float32)
    grad_ln2_bias = jnp.sum(d_hidden, axis=0)
    second_pull = jax.vjp(scaled_norm, middle, gain_two_f)[1]
    d_mid_part, grad_ln2_gain = second_pull(d_hidden)
    d_middle = upstream + d_mid_part
    d_mid_low = d_middle.astype(jnp.bfloat16)
    grad_out_w = jnp.einsum("ti,td->id", attn_mix, d_mid_low, preferred_element_type=jnp.float32)
    grad_out_b = jnp.sum(d_mid_low.astype(jnp.float32), axis=0)
    d_mix = jnp.einsum("td,id->ti", d_mid_low, out_w, preferred_element_type=jnp.float32)
    d_mix = d_mix.astype(jnp.bfloat16).reshape(seq_count, length, HEADS, head_dim)
    d_probs = jnp.einsum("sqhd,skhd->shqk", d_mix, value_heads, preferred_element_type=jnp.float32)
    d_values = jnp.einsum("shqk,sqhd->skhd", probs_low, d_mix, preferred_element_type=jnp.float32)
    d_scores = (
        attn_probs * (d_probs - jnp.sum(d_probs * attn_probs, axis=-1, keepdims=True))
    ).astype(jnp.bfloat16)
    d_queries = (
        jnp.einsum("shqk,skhd->sqhd", d_scores, key_heads, preferred_element_type=jnp.float32)
        * factor
    )
    d_keys = (
        jnp.einsum("shqk,sqhd->skhd", d_scores, queries, preferred_element_type=jnp.float32)
        * factor
    )
    d_packed = (
        jnp.stack([d_queries, d_keys, d_values], axis=2)
        .astype(jnp.bfloat16)
        .reshape(row_count, 3 * model_width)
    )
    grad_qkv = jnp.einsum("ti,tf->if", scaled, d_packed, preferred_element_type=jnp.float32)
    d_scaled = jnp.einsum("tf,if->ti", d_packed, qkv_w, preferred_element_type=jnp.float32).reshape(
        seq_count, length, model_width
    )
    d_normed = d_scaled * scale_seq
    grad_ln1_bias = jnp.sum(d_normed, axis=(0, 1))
    d_embedding = jnp.sum(d_scaled * normed, axis=1)
    grad_table = jnp.einsum(
        "sn,sd->nd", one_hot.astype(jnp.float32), d_embedding, precision=lax.Precision.HIGHEST
    )
    first_pull = jax.vjp(scaled_norm, inputs, gain_one_f)[1]
    d_in_part, grad_ln1_gain = first_pull(d_normed.reshape(row_count, model_width))
    grad_tokens = (d_middle + d_in_part).astype(jnp.bfloat16)
    return (
        block_out,
        grad_tokens,
        (grad_table, grad_ln1_gain, grad_ln1_bias, grad_qkv, grad_out_w, grad_out_b, grad_ln2_gain,
         grad_ln2_bias, grad_up, grad_up_b, grad_down, grad_down_b),
    )


def plain(*args):
    dims = (None, None, 1, 0, 0, 0, 0, 0, 0, 0, 0, 0, 0, 0, None)
    whole = [
        item if dim is None else lax.all_gather(item, "fsdp", axis=dim, tiled=True)
        for item, dim in zip(args, dims, strict=True)
    ]
    block_out, grad_tokens, grads = layer(*whole)
    shares = [
        lax.psum_scatter(grad, "fsdp", scatter_dimension=1 if place == 0 else 0, tiled=True)
        for place, grad in enumerate(grads)
    ]
    return (block_out, grad_tokens, *lax.psum(tuple(shares), "dp"))


def eight_by_four(
    tokens, time_index, time_table, ln1_gain, ln1_bias, w_qkv, w_out, b_out, ln2_gain, ln2_bias,
    w_up, b_up, w_down, b_down, cotangent,
):
    where = jnp.stack(coords()).astype(jnp.int32)
    seqs = time_index.shape[0]
    length = tokens.shape[0] // seqs
    vec = jnp.concatenate(
        [v.reshape(-1, 128) for v in (ln1_gain, ln1_bias, b_out, ln2_gain, ln2_bias, b_down, b_up)]
        + [jnp.zeros((6, 128), LOW)]
    )
    times = time_index.reshape(seqs, 1)
    token = [where]

    def then(values):
        token[0] = values[0] if isinstance(values, (list, tuple)) else values
        return values

    def after(*more):
        return (token[0], *more)

    (parts_first,) = then(
        simple(own_first_kernel, (w_qkv, w_out), [((2, 128, CW), LOW)], where=where)
    )
    small = jnp.concatenate([time_table, vec])
    small_near = swap(small, "z1")
    pieces = [Piece(parts_first, (i,), (128, CW), 1) for i in range(2)]
    near = swap(parts_first, "z1")
    for piece in pieces:
        piece.move_z1(near, piece.index)

    def tick(*jobs, extra=()):
        stages = {
            "z": ("two", "move_z2"), "y": ("four", "move_y"), "x": ("across_send", "move_x"), "c": ("core_send", "move_c"),
        }
        jobs = [(pieces[n], *stages[stage]) for stage, n in jobs]
        made = then(move([getattr(p, make)() for p, make, _ in jobs] + list(extra), after=after()))
        for (p, _, go), value in zip(jobs, made):
            getattr(p, go)(value)
        return made[len(jobs) :]

    tick(("z", 0), ("z", 1))
    parts_up, parts_down = then(
        simple(
            own_other_kernel, (w_up, w_down), [((2, 128, CW), LOW), ((2, RW, 1024), LOW)], where=where, after=after()
        )
    )
    pieces += [Piece(parts_up, (i,), (128, CW), 1) for i in range(2)]
    pieces += [Piece(parts_down, (i,), (RW, 1024), 0) for i in range(2)]
    near_up, near_down = swap(parts_up, "z1"), swap(parts_down, "z1")
    for i in range(2):
        pieces[2 + i].move_z1(near_up, (i,))
        pieces[4 + i].move_z1(near_down, (i,))
    everything = slice(None)
    owns = [
        [(w_qkv, [(everything, pl.ds(0, 2048))], [0], 2048)],
        [(w_qkv, [(everything, pl.ds(2048, 1024))], [0], 1024), (w_out, [(everything, everything)], [1024], 1024)],
    ]
    for half in range(2):
        reads = [(everything, pl.ds(s * 512 + half * 256, 256)) for s in range(8)]
        owns.append([(w_up, reads, [s * 256 for s in range(8)], 256)])
    for half in range(2):
        owns.append([(w_down, [(pl.ds(half * 256, 256), everything)], [0], 256)])

    def whole(n):
        return then(assemble(where, pieces[n], owns[n], after=after()))

    extra = [((2, 144, 128), [(small, (), 0), (small_near, (), 1)])]
    (small_two,) = tick(("y", 0), extra=extra)
    small_far = swap(small_two, "z2")
    extra = [((4, 144, 128), [(small_two, (), slice(0, 2)), (small_far, (), slice(2, 4))])]
    (small_four,) = tick(("x", 0), ("y", 1), ("z", 2), extra=extra)
    small_beside = swap(small_four, "y")
    table, vec, up_b, scale = then(small_params(where, small_four, small_beside, times, after=after()))
    gain_one, bias_one, out_b, gain_two, bias_two, down_b = (vec[i : i + 1] for i in range(6))
    scale = scale.reshape(seqs, 1, -1)
    scaled = then(first_norm(tokens, gain_one, bias_one, scale, after=after()))
    tick(("c", 0), ("x", 1), ("y", 2), ("z", 3))
    w_qk = whole(0)
    tick(("c", 1), ("x", 2), ("y", 3), ("z", 4))
    qk = then(project(scaled, w_qk, after=after()))
    vo = whole(1)
    tick(("c", 2), ("x", 3), ("y", 4), ("z", 5))
    begun = then(attend(scaled, qk, vo, length, 0, 2, after=after()))
    up_a = whole(2)
    tick(("c", 3), ("x", 4), ("y", 5))
    v, probs, mix = then(attend(scaled, qk, vo, length, 2, 2, begun, after=after()))
    tick(("c", 4), ("x", 5))
    middle, hidden = then(second_norm(mix, tokens, vo, out_b, gain_two, bias_two, after=after()))
    act_a, slope_a = then(up(hidden, up_a, up_b[0:1], after=after()))
    up_b_w = whole(3)
    tick(("c", 5))
    act_b, slope_b = then(up(hidden, up_b_w, up_b[1:2], after=after()))
    acts = (act_a, act_b)
    core_one = swap(then(tall_away(where, acts, cotangent, after=after())), "c")
    downs = [whole(4)]
    d_pre, up_sum_a = then(pull(cotangent, downs[0], slope_a, 0, after=after()))
    one = Reduction(*then(tall_mine(where, acts, cotangent, core_one, after=after())))
    downs.append(whole(5))
    d_pre, up_sum_b = then(pull(cotangent, downs[1], slope_b, 1, d_pre, after=after()))
    d_middle, d_low, d_mix, sums_two = then(
        middle_back(d_pre, (up_a, up_b_w), middle, cotangent, gain_two, vo, after=after())
    )

    def step(*jobs):
        names = {
            "second": Reduction.go_second, "third": Reduction.go_third, "fourth": Reduction.go_fourth,
            "last": Reduction.go_last,
        }
        lists = [getattr(r, stage)() for r, stage in jobs]
        made = then(add_up([item for items in lists for item in items], after=after()))
        for (r, stage), items in zip(jobs, lists, strict=True):
            values, made = made[: len(items)], made[len(items) :]
            names[stage](r, *values)

    step((one, "second"))
    pairs = [(hidden, d_pre, "layer"), (mix, d_low, "columns")]
    core_two = swap(then(row_away(where, pairs, after=after())), "c")
    begun = then(attend_back(d_mix, probs, qk, v, length, 0, 2, after=after()))
    step((one, "third"))
    two = Reduction(*then(row_mine(where, pairs, core_two, after=after())))
    d_packed = then(attend_back(d_mix, probs, qk, v, length, 2, 2, (begun,), after=after()))
    pairs = [(scaled, d_packed, "layers")]
    core_three = swap(then(row_away(where, pairs, after=after())), "c")
    grad_tokens, sums_one, d_emb = then(
        input_back(d_packed, w_qk, vo, tokens, d_middle, gain_one, bias_one, scale, after=after())
    )
    step((one, "fourth"), (two, "second"))
    three = Reduction(*then(row_mine(where, pairs, core_three, after=after())))
    (rows,) = then(
        simple(
            rows_kernel,
            (d_emb, sums_one, sums_two, up_sum_a, up_sum_b, jnp.pad(time_index.astype(F32), (0, 120))[None]),
            [((32, 24, 128), F32)],
            after=after(),
        )
    )
    got = lax.all_to_all(rows, BOTH, 0, 0)
    block_out = then(down(acts, downs, middle, down_b, after=after()))
    step((one, "last"), (two, "third"), (three, "second"))
    one.go_corner()
    (down_shard,) = then(shard_of(tall_shard_kernel, where, one, [(512, 1024)], after=after()))
    step((three, "third"))
    step((two, "fourth"))
    grad_table, sums = then(
        simple(table_kernel, (got,), [((128, 128), F32), ((16, 128), F32)], after=after())
    )
    step((two, "last"), (three, "fourth"))
    two.go_corner()
    step((three, "last"))
    three.go_corner()
    up_shard, out_shard = then(shard_of(up_shard_kernel, where, two, [(128, 4096), (128, 1024)], after=after()))
    (qkv_shard,) = then(shard_of(qkv_shard_kernel, where, three, [(128, 3072)], after=after()))
    return (
        block_out, grad_tokens, grad_table, sums[0], sums[1], qkv_shard, out_shard, sums[2], sums[3], sums[4],
        up_shard, sums[6:10].reshape(512), down_shard, sums[5],
    )


def solution(mesh):
    in_specs = (
        P(("fsdp", "dp"), None),
        P(("fsdp", "dp")),
        P(None, "fsdp"),
        P("fsdp"),
        P("fsdp"),
        P("fsdp", None),
        P("fsdp", None),
        P("fsdp"),
        P("fsdp"),
        P("fsdp"),
        P("fsdp", None),
        P("fsdp"),
        P("fsdp", None),
        P("fsdp"),
        P(("fsdp", "dp"), None),
    )
    out_specs = (
        P(("fsdp", "dp"), None),
        P(("fsdp", "dp"), None),
        P(None, "fsdp"),
        P("fsdp"),
        P("fsdp"),
        P("fsdp", None),
        P("fsdp", None),
        P("fsdp"),
        P("fsdp"),
        P("fsdp"),
        P("fsdp", None),
        P("fsdp"),
        P("fsdp", None),
        P("fsdp"),
    )
    local = eight_by_four if (mesh.shape["fsdp"], mesh.shape["dp"]) == (8, 4) else plain
    return jax.shard_map(local, mesh=mesh, in_specs=in_specs, out_specs=out_specs, check_vma=False)
```

```python
import functools

import jax
import jax.numpy as jnp
from jax import lax
from jax.experimental import pallas as pl
from jax.experimental.pallas import tpu as pltpu
from jax.sharding import PartitionSpec as P

HEADS = 16
BOTH = ("fsdp", "dp")
LOW = jnp.bfloat16
F32 = jnp.float32
NT = (((1,), (1,)), ((), ()))
TN = (((0,), (0,)), ((), ()))


def flips(which):
    pairs = []
    for f in range(8):
        for d in range(4):
            z, y, x, c = f // 2, f % 2, d // 2, d % 2
            if which == "x":
                x = 1 - x
            elif which == "y":
                y = 1 - y
            elif which == "c":
                c = 1 - c
            elif which == "z1":
                z = z ^ 1
            elif which == "z2":
                z = z ^ 2
            elif which == "z3":
                z = z ^ 3
            pairs.append((f * 4 + d, (z * 2 + y) * 4 + x * 2 + c))
    return pairs


def swap(values, which):
    return lax.ppermute(values, BOTH, flips(which))


def coords():
    f, d = lax.axis_index("fsdp"), lax.axis_index("dp")
    return f // 2, f % 2, d // 2, d % 2


def call(kernel, grid, ins, outs, flops=0, nbytes=0, scratch=(), prefetch=0, aliases=None, limit=18, pin=(), pin_out=()
):
    after = tuple(chain)

    def spec(block, index):
        if block is None:
            return pl.BlockSpec(memory_space=pl.ANY)
        if block == "hbm":
            return pl.BlockSpec(memory_space=pltpu.MemorySpace.HBM)
        if index in constant and grid:
            return pl.BlockSpec(block, index, pipeline_mode=pl.Buffered(1))
        return pl.BlockSpec(block, index)

    def body(*refs):
        n = prefetch + len(ins)
        m = n + len(after) + len(outs)
        kernel(*refs[:n], *refs[n + len(after) : m], *refs[m + 1 :])

    run = pl.pallas_call(
        body,
        out_shape=[
            pltpu.MemorySpace.HBM(shape, kind) if k in pin_out else jax.ShapeDtypeStruct(shape, kind)
            for k, (shape, kind, _, _) in enumerate(outs)
        ]
        + [pltpu.MemorySpace.HBM((8, 128), F32)],
        grid_spec=pltpu.PrefetchScalarGridSpec(
            num_scalar_prefetch=prefetch,
            grid=grid,
            in_specs=[spec(block, index) for block, index in ins] + [spec(None, None)] * len(after),
            out_specs=[spec(block, index) for _, _, block, index in outs] + [spec(None, None)],
            scratch_shapes=scratch,
        ),
        input_output_aliases=aliases or {},
        compiler_params=pltpu.CompilerParams(
            vmem_limit_bytes=limit * 2**20, dimension_semantics=("arbitrary",) * len(grid)
        ),
        cost_estimate=pl.CostEstimate(flops=0, bytes_accessed=1024, transcendentals=0),
    )

    def pinned(*args):
        args = [
            pltpu.with_memory_space_constraint(a, pltpu.MemorySpace.HBM) if k - prefetch in pin else a
            for k, a in enumerate(args)
        ]
        *values, token = run(*args, *(pltpu.with_memory_space_constraint(t, pltpu.MemorySpace.HBM) for t in after))
        chain[:] = [token]
        return values

    return pinned


def simple(kernel, args, outs, where=None, passing=(), limit=12, pin_out=()):
    def whole(shape):
        return shape, lambda *_: (0,) * len(shape)

    prefetch = 0 if where is None else 1
    n_in, n_out, n_pass = len(args), len(outs), len(passing)

    def body(*refs):
        first = prefetch + n_in
        kernel(*refs[:first], *refs[first + n_pass : first + n_pass + n_out])

    run = call(
        body,
        (),
        [whole(a.shape) for a in args] + [(None, None)] * n_pass,
        [(shape, kind, *whole(shape)) for shape, kind in outs] + [(a.shape, a.dtype, None, None) for a in passing],
        prefetch=prefetch,
        aliases={prefetch + n_in + k: n_out + k for k in range(n_pass)},
        limit=limit,
        pin_out=pin_out,
    )
    return run(*(() if where is None else (where,)), *args, *passing)


constant = []
chain = []


def fixed(*index):
    constant.append(lambda *grid: index)
    return constant[-1]


def ends(n):
    e = n * 3 // 8
    return e // 2, (n - 2 * e) // 2


def end_start(n, x, c):
    eh, mh = ends(n)
    return x * (n - 2 * eh) + c * eh


def middle_start(n, c):
    eh, mh = ends(n)
    return 2 * eh + c * mh


COLS, ROWS = 2048, 256
CE, CM = ends(COLS)
RE, RM = ends(ROWS)
CW, RW = CE + CM, RE + RM


def lanes(start, size=128):
    return pl.ds(start if isinstance(start, int) else pl.multiple_of(start, 128), size)


def own_columns(where, dest, read):
    x, c = where[2], where[3]
    for i in range(CW // 128):
        start = end_start(COLS, x, c) + i * 128 if i < CE // 128 else middle_start(COLS, c) + i * 128 - CE
        dest[:, i * 128 : (i + 1) * 128] = read(start)


def own_first_kernel(where, qkv, out_w, parts):
    own_columns(where, parts.at[0], lambda start: qkv[:, lanes(start)])
    own_columns(
        where,
        parts.at[1],
        lambda start: jnp.where(
            start < 1024, qkv[:, lanes(2048 + jnp.minimum(start, 896))], out_w[:, lanes(jnp.maximum(start - 1024, 0))]
        ),
    )


def own_other_kernel(where, up_w, down_w, parts, tall):
    x, c = where[2], where[3]
    for half in range(2):
        own_columns(
            where, parts.at[half], lambda start: up_w[:, lanes((start // 256) * 512 + half * 256 + start % 256)]
        )
        for size, first, at in ((RE, end_start(ROWS, x, c), 0), (RM, middle_start(ROWS, c), RE)):
            tall[half, at : at + size, :] = down_w[pl.ds(pl.multiple_of(half * 256 + first, 16), size), :]


def move(jobs, passing=()):
    args = []
    for _, copies in jobs:
        for array, _, _ in copies:
            if not any(array is a for a in args):
                args.append(array)

    def kernel(*refs):
        outs = refs[len(args) :]
        for out, (_, copies) in zip(outs, jobs, strict=True):
            for array, read, write in copies:
                ref = refs[[i for i, a in enumerate(args) if a is array][0]]
                out[write] = ref[read if read != () else ...]

    return simple(kernel, args, [(shape, LOW) for shape, _ in jobs], passing=passing)


class Piece:
    def __init__(self, part, index, shape, axis):
        self.part, self.index, self.shape, self.axis = part, index, shape, axis
        self.e = CE if axis == 1 else RE
        self.inner = (slice(0, 128), slice(0, CW)) if axis == 1 else (slice(None), slice(None))
        self.end = (slice(0, 128), slice(0, CE)) if axis == 1 else (slice(0, RE), slice(None))

    def two(self):
        return (2, *self.shape), [(self.part, self.index, 0), (self.near, self.near_index, 1)]

    def four(self):
        return (4, *self.shape), [
            (self.part, self.index, 0),
            (self.near, self.near_index, 1),
            (self.far, slice(None), slice(2, 4)),
        ]

    def blocks(self):
        found = [(self.near, self.near_index)] + [(self.far, (i,)) for i in range(2)]
        return found + [(self.beside, (i,)) for i in range(4)]

    def across_send(self):
        shape = (128, CE) if self.axis == 1 else (RE, 1024)
        return (7, *shape), [(a, (*i, *self.end), j) for j, (a, i) in enumerate(self.blocks())]

    def core_send(self):
        if self.axis == 1:
            shape, first, last = (128, CW + CE), (slice(None), slice(0, CW)), (slice(None), slice(CW, CW + CE))
        else:
            shape, first, last = (RW + RE, 1024), (slice(0, RW), slice(None)), (slice(RW, RW + RE), slice(None))
        copies = [(a, (*i, *self.inner), (j, *first)) for j, (a, i) in enumerate(self.blocks())]
        return (7, *shape), copies + [(self.across, j, (j, *last)) for j in range(7)]

    def move_z1(self, near, near_index):
        self.near, self.near_index = near, near_index

    def move_z2(self, two):
        self.far = swap(two, "z2")

    def move_y(self, four):
        self.beside = swap(four, "y")

    def move_x(self, send):
        self.across = swap(send, "x")

    def move_c(self, send):
        self.other = swap(send, "c")


def assemble_kernel(axis, own_copies, near_index, where, *refs):
    n_own = len(own_copies)
    owns = refs[:n_own]
    near, far, beside, across, other, out, sems, out_sems, hold = refs[n_own:]
    z, y, x, c = where[0], where[1], where[2], where[3]
    rows = 128 if axis == 1 else ROWS
    size = COLS if axis == 1 else ROWS
    eh, mh = ends(size)

    def at(base, start, count):
        if axis == 1:
            return hold.at[pl.ds(base, rows), lanes(start, count)]
        return hold.at[pl.ds(pl.multiple_of(base + start, 16), count), :]

    def cut(block, start, count):
        if axis == 1:
            return block.at[pl.ds(0, 128), pl.ds(start, count)]
        return block.at[pl.ds(start, count), :]

    groups, bases = [], []
    for j in range(8):
        zz = (z, z ^ 1, z ^ 2, z ^ 3)[j % 4]
        yy = y if j < 4 else 1 - y
        base = pl.multiple_of((zz * 2 + yy) * rows, rows)
        if j == 0:
            copies = []
            for ref, (read, start, count) in zip(owns, own_copies, strict=True):
                for k in range(len(read)):
                    copies.append((ref.at[read[k]], at(base, start[k], count)))
        else:
            close = near.at[near_index[0]] if near_index else near
            mine = (close, far.at[0], far.at[1], beside.at[0], beside.at[1], beside.at[2], beside.at[3])[j - 1]
            oc = 1 - c
            copies = [
                (cut(mine, 0, eh), at(base, end_start(size, x, c), eh)),
                (cut(mine, eh, mh), at(base, middle_start(size, c), mh)),
                (cut(across.at[j - 1], 0, eh), at(base, end_start(size, 1 - x, c), eh)),
                (cut(other.at[j - 1], 0, eh), at(base, end_start(size, x, oc), eh)),
                (cut(other.at[j - 1], eh, mh), at(base, middle_start(size, oc), mh)),
                (cut(other.at[j - 1], eh + mh, eh), at(base, end_start(size, 1 - x, oc), eh)),
            ]
        group = [pltpu.make_async_copy(s, d, sems.at[j]) for s, d in copies]
        for copy in group:
            copy.start()
        groups.append(group)
        bases.append(base)
    outs = []
    for j in range(8):
        for copy in groups[j]:
            copy.wait()
        rows_of = pl.ds(bases[j], rows)
        copy = pltpu.make_async_copy(hold.at[rows_of, :], out.at[rows_of, :], out_sems.at[j])
        copy.start()
        outs.append(copy)
    for copy in outs:
        copy.wait()


def assemble(where, piece, owns):
    shape = (1024, COLS) if piece.axis == 1 else (8 * ROWS, 1024)
    args = [o[0] for o in owns] + [piece.near, piece.far, piece.beside, piece.across, piece.other]
    return call(
        functools.partial(assemble_kernel, piece.axis, [o[1:] for o in owns], piece.near_index),
        (),
        [(None, None)] * len(args),
        [(shape, LOW, None, None)],
        prefetch=1,
        scratch=[pltpu.SemaphoreType.DMA((8,)), pltpu.SemaphoreType.DMA((8,)), pltpu.VMEM(shape, LOW)],
        limit=8,
    )(where, *args)[0]


def small_kernel(where, four, beside, time_index, table, vec, up_b, scale):
    z, y = where[0], where[1]
    for j in range(8):
        block = four.at[j] if j < 4 else beside.at[j - 4]
        shard = (z ^ (j // 2)) * 2 + (y ^ (j % 2))
        table[:, lanes(shard * 128)] = block[:128, :]
        vec[:, lanes(shard * 128)] = block[128:, :].astype(F32)
        for row in range(4):
            unit = lanes(shard * 256 + (row % 2) * 128)
            up_b[row // 2 : row // 2 + 1, unit] = block[134 + row : 135 + row, :].astype(F32)
    numbers = lax.broadcasted_iota(jnp.int32, (time_index.shape[0], 128), 1)
    one_hot = (numbers == time_index[...]).astype(F32).astype(LOW)
    scale[...] = 1.0 + jnp.dot(one_hot, table[...], preferred_element_type=F32)


def small_params(where, four, beside, time_index):
    return simple(
        small_kernel,
        (four, beside, time_index),
        [((128, 1024), LOW), ((16, 1024), F32), ((2, 2048), F32), ((time_index.shape[0], 1024), F32)],
        where=where,
    )


def rows_kernel(d_emb, sums_one, sums_two, up_a, up_b, times, out):
    for s in range(8):
        here = slice(s * 128, (s + 1) * 128)
        rows = [d_emb[i, :, here] for i in range(8)]
        rows += [sums_one[0:2, here], sums_two[2:3, here], sums_two[0:2, here], sums_two[3:4, here]]
        for sums in (up_a, up_b):
            rows += [sums[:, s * 256 + j * 128 : s * 256 + (j + 1) * 128] for j in range(2)]
        rows += [times[...], jnp.zeros((5, 128), F32)]
        block = jnp.concatenate(rows, axis=0)
        for copy in range(4):
            out[s * 4 + copy] = block


def mm(a, b):
    return jnp.dot(a, b, preferred_element_type=F32)


def mm_nt(a, b):
    return lax.dot_general(a, b, NT, preferred_element_type=F32)


def mm_tn(a, b):
    return lax.dot_general(a, b, TN, preferred_element_type=F32)


def centre(values):
    mean = jnp.mean(values, axis=-1, keepdims=True)
    centred = values - mean
    scale = lax.rsqrt(jnp.mean(centred * centred, axis=-1, keepdims=True) + 1e-05)
    return centred * scale, scale


def first_norm_kernel(tokens, gain, bias, scale, scaled):
    hat, _ = centre(tokens[...].astype(F32))
    scaled[...] = ((hat * gain[...] + bias[...]) * scale[0]).astype(LOW)


def first_norm(tokens, gain, bias, scale):
    rows, width = tokens.shape
    seqs = scale.shape[0]
    length = rows // seqs
    return call(
        first_norm_kernel,
        (seqs,),
        [
            ((length, width), lambda i: (i, 0)),
            ((1, width), fixed(0, 0)),
            ((1, width), fixed(0, 0)),
            ((1, 1, width), lambda i: (i, 0, 0)),
        ],
        [((rows, width), LOW, (length, width), lambda i: (i, 0))],
    )(tokens, gain, bias, scale)[0]


def halves(values):
    lane = lax.broadcasted_iota(jnp.int32, values.shape, 1)
    zero = jnp.zeros_like(values)
    return jnp.concatenate([jnp.where(lane < 64, values, zero), jnp.where(lane < 64, zero, values)], axis=0)


def side(values):
    n = values.shape[0] // 2
    return jnp.concatenate([values[:n], values[n:]], axis=1)


def project_kernel(x, w, out):
    out[...] = mm(x[...], w[...]).astype(LOW)


def project(x, w, tile=512):
    rows, width = x.shape
    n = w.shape[1]
    return call(
        project_kernel,
        (n // tile,),
        [((rows, width), fixed(0, 0)), ((width, tile), lambda i: (0, i))],
        [((rows, n), LOW, (rows, tile), lambda i: (0, i))],
    )(x, w)[0]


def units_of(rows, length, at_once=8):
    units = []
    for seq in range(rows // length):
        for pair in range(2):
            units.append((seq, pair, (slice(seq * length, (seq + 1) * length), slice(pair * 128, (pair + 1) * 128))))
    return [units[i : i + at_once] for i in range(0, len(units), at_once)]


def attend_kernel(length, scaled, wv, q_in, k_in, *refs):
    v_out, probs_out, mix_out = refs[-3:]
    factor = 64 ** (-0.5) * 1.4426950408889634
    v_out[...] = mm(scaled[...], wv[...]).astype(LOW)
    for units in units_of(scaled.shape[0], length):
        scores = [mm_nt(halves(q_in[here]), k_in[here]) for _, _, here in units]
        found = []
        for s in scores:
            e = jnp.exp2((s - jnp.max(s, axis=-1, keepdims=True)) * factor)
            found.append((e * (1.0 / jnp.sum(e, axis=-1, keepdims=True))).astype(LOW))
        for (seq, pair, here), probs in zip(units, found, strict=True):
            probs_out[0, seq, pair] = probs
            mix_out[here] = mm(side(probs), halves(v_out[here])).astype(LOW)


def attend(scaled, qk, vo, length, first=0, count=None, earlier=()):
    rows, width = scaled.shape
    groups = width // 256
    seqs = rows // length
    count = groups if count is None else count
    column = lambda i: (0, first + i)
    wide = ((rows, width), LOW, (rows, 256), column)
    probs = (groups, seqs, 2, 2 * length, length)
    return call(
        functools.partial(attend_kernel, length),
        (count,),
        [
            ((rows, width), fixed(0, 0)),
            ((width, 256), column),
            ((rows, 256), column),
            ((rows, 256), lambda i: (0, groups + first + i)),
        ]
        + [(None, None)] * len(earlier),
        [wide, (probs, LOW, (1, *probs[1:]), lambda i: (first + i, 0, 0, 0, 0)), wide],
        aliases={4 + i: i for i in range(len(earlier))},
    )(scaled, vo, qk, qk, *earlier)


def middle_kernel(mix, tokens, w, out_b, gain, bias, middle_out, hidden_out):
    middle = tokens[...].astype(F32) + mm(mix[...], w[...]) + out_b[...]
    middle_out[...] = middle
    hat, _ = centre(middle)
    hidden_out[...] = (hat * gain[...] + bias[...]).astype(LOW)


def second_norm(mix, tokens, vo, out_b, gain, bias):
    rows, width = tokens.shape
    row = lambda i: (i, 0)
    vec = ((1, width), fixed(0, 0))
    return call(
        middle_kernel,
        (rows // 256,),
        [((256, width), row), ((256, width), row), ((width, width), fixed(0, 1)), vec, vec, vec],
        [((rows, width), F32, (256, width), row), ((rows, width), LOW, (256, width), row)],
    )(mix, tokens, vo, out_b, gain, bias)


def gelu_parts(v):
    cdf = 0.5 + 0.5 * lax.erf(v * 0.5**0.5)
    bell = jnp.exp(-0.5 * v * v)
    return v * cdf, cdf + (v * 0.3989422804014327) * bell


def up_kernel(hidden, w, bias, act, slope):
    value, pull = gelu_parts(mm(hidden[...], w[...]) + bias[...])
    act[...] = value.astype(LOW)
    slope[...] = pull.astype(LOW)


def up(hidden, w, bias, tile=512):
    rows, width = hidden.shape
    n = w.shape[1]
    column = lambda i: (0, i)
    return call(
        up_kernel,
        (n // tile,),
        [((rows, width), fixed(0, 0)), ((width, tile), column), ((1, tile), column)],
        [((rows, n), LOW, (rows, tile), column)] * 2,
        limit=22,
    )(hidden, w, bias)


def down_kernel(act_a, act_b, first, second, middle, bias, out):
    total = middle[...] + bias[...]
    total += mm(act_a[...], first[...])
    total += mm(act_b[...], second[...])
    out[...] = total.astype(LOW)


def down(acts, ws, middle, bias, tile=256):
    rows, width = middle.shape
    k = ws[0].shape[0]
    row = lambda i: (i, 0)
    return call(
        down_kernel,
        (rows // tile,),
        [((tile, k), row)] * 2
        + [((k, width), fixed(0, 0))] * 2
        + [((tile, width), row), ((1, width), fixed(0, 0))],
        [((rows, width), LOW, (tile, width), row)],
        limit=24,
    )(*acts, *ws, middle, bias)[0]


def pull_kernel(cot, w, slope, *refs):
    d_pre, sums = refs[-2:]
    value = (mm_nt(cot[...], w[...]) * slope[...].astype(F32)).astype(LOW)
    d_pre[0] = value
    sums[...] = jnp.sum(value.astype(F32), axis=0, keepdims=True)


def pull(cot, w, slope, half, earlier=None, tile=512):
    rows, width = cot.shape
    n = w.shape[0]
    column = lambda i: (0, i)
    ins = [((rows, width), fixed(0, 0)), ((tile, width), lambda i: (i, 0)), ((rows, tile), column)]
    return call(
        pull_kernel,
        (n // tile,),
        ins + ([] if earlier is None else [(None, None)]),
        [((2, rows, n), LOW, (1, rows, tile), lambda i: (half, 0, i)), ((1, n), F32, (1, tile), column)],
        aliases={} if earlier is None else {3: 0},
    )(cot, w, slope, *(() if earlier is None else (earlier,)))


def norm_back(d_out, hat, scale, gain):
    e = d_out * gain
    mean = jnp.mean(e, axis=-1, keepdims=True)
    slant = jnp.mean(e * hat, axis=-1, keepdims=True)
    return (e - mean - hat * slant) * scale


def fold(*rows_of):
    sums = [jnp.sum(v, axis=0, keepdims=True) for v in rows_of]
    return jnp.concatenate(sums + [jnp.zeros_like(sums[0])] * (8 - len(sums)), axis=0)


def middle_back_kernel(d_pre, wa, wb, middle, cot, gain, w_out, d_middle_out, d_low_out, d_mix_out, sums):
    d_hidden = mm_nt(d_pre[0], wa[...]) + mm_nt(d_pre[1], wb[...])
    hat, scale = centre(middle[...])
    d_middle = cot[...].astype(F32) + norm_back(d_hidden, hat, scale, gain[...])
    d_middle_out[...] = d_middle
    d_low = d_middle.astype(LOW)
    d_low_out[...] = d_low
    d_mix_out[...] = mm_nt(d_low, w_out[...]).astype(LOW)

    @pl.when(pl.program_id(0) == 0)
    def _():
        sums[...] = jnp.zeros_like(sums)

    sums[...] += fold(d_hidden * hat, d_hidden, d_low.astype(F32), cot[...].astype(F32))


def middle_back(d_pre, ws, middle, cot, gain, vo, tile=256):
    rows, width = middle.shape
    row = lambda i: (i, 0)
    return call(
        middle_back_kernel,
        (rows // tile,),
        [
            ((2, tile, d_pre.shape[2]), lambda i: (0, i, 0)),
            (ws[0].shape, fixed(0, 0)),
            (ws[1].shape, fixed(0, 0)),
            ((tile, width), row),
            ((tile, width), row),
            ((1, width), fixed(0, 0)),
            ((width, width), fixed(0, 1)),
        ],
        [
            ((rows, width), F32, (tile, width), row),
            ((rows, width), LOW, (tile, width), row),
            ((rows, width), LOW, (tile, width), row),
            ((8, width), F32, (8, width), fixed(0, 0)),
        ],
        limit=32,
    )(d_pre, *ws, middle, cot, gain, vo)


def attend_back_kernel(length, d_mix, probs, q_in, k_in, v_in, *refs):
    out = refs[-1]
    factor = 64 ** (-0.5)
    for units in units_of(d_mix.shape[0], length, 4):
        dms = [halves(d_mix[here]) for _, _, here in units]
        d_probs = [mm_nt(dm, v_in[here]) for dm, (_, _, here) in zip(dms, units, strict=True)]
        found = []
        for d, (seq, pair, _) in zip(d_probs, units, strict=True):
            high = probs[0, seq, pair].astype(F32)
            found.append((high * (d - jnp.sum(d * high, axis=-1, keepdims=True))).astype(LOW))
        for dm, d_scores, (seq, pair, here) in zip(dms, found, units, strict=True):
            out[(2, *here)] = mm_tn(probs[0, seq, pair], dm).astype(LOW)
            out[(0, *here)] = (mm(side(d_scores), halves(k_in[here])) * factor).astype(LOW)
            out[(1, *here)] = (mm_tn(d_scores, halves(q_in[here])) * factor).astype(LOW)


def attend_back(d_mix, probs, qk, v, length, first=0, count=None, earlier=()):
    rows, width = d_mix.shape
    count = width // 256 if count is None else count
    wide = ((rows, 256), lambda i: (0, first + i))
    return call(
        functools.partial(attend_back_kernel, length),
        (count,),
        [
            wide,
            ((1,) + probs.shape[1:], lambda i: (first + i, 0, 0, 0, 0)),
            wide,
            ((rows, 256), lambda i: (0, width // 256 + first + i)),
            wide,
        ]
        + [(None, None)] * len(earlier),
        [((3, rows, width), LOW, (3, rows, 256), lambda i: (0, 0, first + i))],
        aliases={5 + i: i for i in range(len(earlier))},
    )(d_mix, probs, qk, qk, v, *earlier)[0]


def input_back_kernel(length, d, wq, wk, wv, tokens, d_middle, gain, bias, scale, out, sums, d_emb):
    d_scaled = mm_nt(d[0], wq[...]) + mm_nt(d[1], wk[...]) + mm_nt(d[2], wv[...])
    hat, spread = centre(tokens[...].astype(F32))
    normed = hat * gain[...] + bias[...]
    count = tokens.shape[0] // length
    parts = []
    for i in range(count):
        here = slice(i * length, (i + 1) * length)
        d_emb[i] = jnp.sum(d_scaled[here] * normed[here], axis=0, keepdims=True)
        parts.append(d_scaled[here] * scale[i])
    d_normed = jnp.concatenate(parts, axis=0)
    out[...] = (d_middle[...] + norm_back(d_normed, hat, spread, gain[...])).astype(LOW)

    @pl.when(pl.program_id(0) == 0)
    def _():
        sums[...] = jnp.zeros_like(sums)

    sums[...] += fold(d_normed * hat, d_normed)


def input_back(d_packed, qk, vo, tokens, d_middle, gain, bias, scale, tile=256):
    rows, width = tokens.shape
    seqs = scale.shape[0]
    length = rows // seqs
    row = lambda i: (i, 0)
    wide = ((tile, width), row)
    vec = ((1, width), fixed(0, 0))
    some = ((tile // length, 1, width), lambda i: (i, 0, 0))
    return call(
        functools.partial(input_back_kernel, length),
        (rows // tile,),
        [
            ((3, tile, width), lambda i: (0, i, 0)),
            ((width, width), fixed(0, 0)),
            ((width, width), fixed(0, 1)),
            ((width, width), fixed(0, 0)),
            wide, wide, vec, vec, some,
        ],
        [
            ((rows, width), LOW, (tile, width), row),
            ((8, width), F32, (8, width), fixed(0, 0)),
            ((seqs, 1, width), F32) + some,
        ],
        limit=26,
    )(d_packed, qk, qk, vo, tokens, d_middle, gain, bias, scale)


def tall_away_kernel(where, a, b, cot, away):
    left = jnp.concatenate([a[...], b[...]], axis=1)
    value = mm_tn(left, cot[...]).astype(LOW)
    x = where[2]
    for xr in range(2):
        for half in range(2):
            low, high = value[half * 256 : half * 256 + 128], value[half * 256 + 128 : half * 256 + 256]
            away[xr, 0, 0, half] = jnp.where((x ^ xr) == 0, low, high)


def tall_shard(zr, yr, where):
    return ((zr ^ where[0]) * 2) + (yr ^ where[1])


def tall_ins(acts, cot, core):
    rows, width = cot.shape
    act = ((rows, 256), lambda zr, yr, where: (0, tall_shard(zr, yr, where)))
    return [act, act, ((rows, width // 2), lambda zr, yr, where: (0, where[3] ^ core))]


def tall_away(where, acts, cot):
    n = cot.shape[1] // 2
    return call(
        tall_away_kernel,
        (4, 2),
        tall_ins(acts, cot, 1),
        [((2, 2, 4, 2, 128, n), LOW, (2, 1, 1, 2, 128, n), lambda zr, yr, where: (0, yr, zr, 0, 0, 0))],
        prefetch=1,
    )(where, *acts, cot)[0]


def tall_mine_kernel(where, a, b, cot, core, xa, yb, ka, kb):
    left = jnp.concatenate([a[...], b[...]], axis=1)
    value = mm_tn(left, cot[...])
    x = where[2]
    zr, yr = pl.program_id(0), pl.program_id(1)
    sums = []
    for xr in range(2):
        halves_of = []
        for half in range(2):
            low, high = value[half * 256 : half * 256 + 128], value[half * 256 + 128 : half * 256 + 256]
            total = jnp.where((x ^ xr) == 0, low, high) + core[xr, 0, 0, half].astype(F32)
            halves_of.append(total.astype(LOW))
        sums.append(halves_of)

    @pl.when(zr < 2)
    def _():
        for half in range(2):
            ka[0, 0, half] = sums[0][half]
            xa[0, 0, half] = sums[1][half]

    @pl.when((zr >= 2) & (yr == 0))
    def _():
        for xr in range(2):
            for half in range(2):
                kb[xr, 0, half] = sums[xr][half]

    @pl.when((zr >= 2) & (yr == 1))
    def _():
        for xr in range(2):
            for half in range(2):
                yb[xr, 0, half] = sums[xr][half]


def tall_mine(where, acts, cot, core):
    n = cot.shape[1] // 2
    shape = (2, 2, 2, 128, n)
    by_y = (
        shape,
        LOW,
        (1, 1, 2, 128, n),
        lambda zr, yr, where: (jnp.where(zr < 2, yr, 1), jnp.minimum(zr, 1), 0, 0, 0),
    )
    by_x = (shape, LOW, (2, 1, 2, 128, n), lambda zr, yr, where: (0, jnp.maximum(zr - 2, 0), 0, 0, 0))
    return call(
        tall_mine_kernel,
        (4, 2),
        tall_ins(acts, cot, 0) + [((2, 1, 1, 2, 128, n), lambda zr, yr, where: (0, yr, zr, 0, 0, 0))],
        [by_y, by_x, by_y, by_x],
        prefetch=1,
        pin=(3,),
        pin_out=(2, 3),
    )(where, *acts, cot, core)


def row_value(step, lefts, rights, counts, hold):
    first = 0
    for left, right, count in zip(lefts, rights, counts, strict=True):

        def put(left=left, right=right):
            b = right[0] if len(right.shape) == 3 else right[...]
            hold[...] = mm_tn(left[...], b)

        if len(lefts) == 1:
            put()
        else:
            pl.when((step >= first) & (step < first + count))(put)
        first += count


def row_from(where, xr, yr, zr):
    start = ((where[0] ^ zr) * 2 + (where[1] ^ yr)) * 128 + (where[2] ^ xr) * 64
    return pl.ds(pl.multiple_of(start, 64), 64)


def row_away_kernel(counts, where, *refs):
    n = len(counts)
    lefts, rights, away, hold = refs[:n], refs[n : 2 * n], refs[2 * n], refs[2 * n + 1]
    row_value(pl.program_id(0), lefts, rights, counts, hold)
    for xr in range(2):
        for yr in range(2):
            for zr in range(4):
                away[xr, yr, zr] = hold[row_from(where, xr, yr, zr), :].astype(LOW)


def row_mine_kernel(counts, where, *refs):
    n = len(counts)
    lefts, rights = refs[:n], refs[n : 2 * n]
    core, xa, yb, ka, kb, hold = refs[2 * n :]
    row_value(pl.program_id(0), lefts, rights, counts, hold)
    for xr in range(2):
        for yr in range(2):
            for zr in range(4):
                total = hold[row_from(where, xr, yr, zr), :] + core[xr, yr, zr].astype(F32)
                total = total.astype(LOW)
                if zr < 2:
                    (ka if xr == 0 else xa)[yr, zr] = total
                else:
                    (kb if yr == 0 else yb)[xr, zr - 2] = total


def row_specs(pairs, core, tile):
    ins, counts = [], []
    for a, _, _ in pairs:
        ins.append((a.shape, lambda j, where: (0, 0)))
    first = 0
    for _, b, kind in pairs:
        tokens = b.shape[-2]
        if kind == "layers":
            count = b.shape[0] * (b.shape[2] // 2 // tile)
            each = b.shape[2] // 2 // tile
            spec = (
                (1, tokens, tile),
                lambda j, where, f=first, m=count, e=each: (
                    jnp.clip(j - f, 0, m - 1) // e,
                    0,
                    (where[3] ^ core) * e + jnp.clip(j - f, 0, m - 1) % e,
                ),
            )
        elif kind == "layer":
            count = b.shape[2] // tile
            spec = (
                (1, tokens, tile),
                lambda j, where, f=first, m=count: (where[3] ^ core, 0, jnp.clip(j - f, 0, m - 1)),
            )
        else:
            count = b.shape[1] // 2 // tile
            spec = (
                (tokens, tile),
                lambda j, where, f=first, m=count: (0, (where[3] ^ core) * m + jnp.clip(j - f, 0, m - 1)),
            )
        ins.append(spec)
        counts.append(count)
        first += count
    return ins, counts


def row_away(where, pairs, tile=512):
    ins, counts = row_specs(pairs, 1, tile)
    steps = sum(counts)
    return call(
        functools.partial(row_away_kernel, counts),
        (steps,),
        ins,
        [((2, 2, 4, 64, steps * tile), LOW, (2, 2, 4, 64, tile), lambda j, where: (0, 0, 0, 0, j))],
        prefetch=1,
        scratch=[pltpu.VMEM((1024, tile), F32)],
    )(where, *[a for a, _, _ in pairs], *[b for _, b, _ in pairs])[0]


def row_mine(where, pairs, core, tile=512):
    ins, counts = row_specs(pairs, 0, tile)
    steps = sum(counts)
    out = ((2, 2, 64, steps * tile), LOW, (2, 2, 64, tile), lambda j, where: (0, 0, 0, j))
    return call(
        functools.partial(row_mine_kernel, counts),
        (steps,),
        ins + [((2, 2, 4, 64, tile), lambda j, where: (0, 0, 0, 0, j))],
        [out] * 4,
        prefetch=1,
        scratch=[pltpu.VMEM((1024, tile), F32)],
        pin=(2 * len(pairs),),
        pin_out=(2, 3),
    )(where, *[a for a, _, _ in pairs], *[b for _, b, _ in pairs], core)


def add_up(jobs, passing=()):
    args, pieces = [], []
    parts = [job[1] if isinstance(job[1][0][0], list) else [(job[1], ...)] for job in jobs]

    def number(array, index):
        here = [k for k, a in enumerate(args) if a is array]
        if not here:
            args.append(array)
            here = [len(args) - 1]
        if (here[0], index) not in pieces:
            pieces.append((here[0], index))
        return pieces.index((here[0], index))

    parts = [[([number(*term) for term in terms], write) for terms, write in part] for part in parts]
    shapes = [jax.eval_shape(lambda a, index=index: a[index], args[k]).shape for k, index in pieces]
    n_in, n_out, n_pass = len(args), len(jobs), len(passing)

    def kernel(*refs):
        ins, outs = refs[:n_in], refs[n_in + n_pass : n_in + n_pass + n_out]
        *held, sems = refs[n_in + 2 * n_pass + n_out :]
        copies = []
        for k, (at, index) in enumerate(pieces):
            copies.append(pltpu.make_async_copy(ins[at].at[index], held[k], sems.at[k]))
            copies[-1].start()
        waited = set()
        for out, part in zip(outs, parts, strict=True):
            for terms, write in part:
                total = None
                for k in terms:
                    if k not in waited:
                        copies[k].wait()
                        waited.add(k)
                    value = held[k][...].astype(F32)
                    total = value if total is None else total + value
                out[write] = total.astype(LOW)

    def whole(shape):
        return shape, lambda *_: (0,) * len(shape)

    return call(
        kernel,
        (),
        [("hbm", None)] * n_in + [(None, None)] * n_pass,
        [(job[0], LOW, *whole(job[0])) for job in jobs] + [(a.shape, a.dtype, None, None) for a in passing],
        aliases={n_in + k: n_out + k for k in range(n_pass)},
        scratch=[pltpu.VMEM(shape, LOW) for shape in shapes] + [pltpu.SemaphoreType.DMA((len(pieces),))],
        limit=12,
        pin=tuple(k for k, a in enumerate(args) if a.size >= 2**19),
    )(*args, *passing)


class Reduction:
    def __init__(self, ka, kb):
        self.ka, self.kb = ka, kb
        self.tail = ka.shape[2:]

    def go_first(self, xa, yb):
        self.xa, self.yb = swap(xa, "x"), swap(yb, "y")

    def second(self):
        shape = (2, *self.tail)
        return [(shape, [(self.ka, 1), (self.xa, 1)]), (shape, [(self.kb, 1), (self.yb, 1)])]

    def go_second(self, ya, xb):
        self.ya, self.xb = swap(ya, "y"), swap(xb, "x")

    def kept(self, i):
        return self.tail, [(self.ka, (0, i)), (self.xa, (0, i)), (self.ya, i)]

    def sent(self, i):
        return self.tail, [(self.kb, (0, i)), (self.yb, (0, i)), (self.xb, i)]

    def third(self):
        two = [((2, *self.tail), [(self.kb, 0), (self.yb, 0), (self.xb, slice(None))])]
        return two + [self.kept(0), self.kept(1)]

    def go_third(self, far, mine, next_one):
        self.far, self.mine, self.next_one = swap(far, "z2"), mine, next_one

    def fourth(self):
        return [(self.tail, [(self.next_one, slice(None)), (self.far, 1)])]

    def go_fourth(self, near):
        self.near = swap(near, "z1")

    def last(self):
        return [(self.tail, [(self.mine, slice(None)), (self.far, 0), (self.near, slice(None))])]

    def third_direct(self):
        return [self.kept(1), self.sent(0), self.sent(1), self.kept(0)]

    def go_third_direct(self, *blocks):
        self.got = [swap(block, name) for block, name in zip(blocks, ("z1", "z2", "z3"))]
        self.mine = blocks[3]

    def last_direct(self):
        return [(self.tail, [(self.mine, slice(None))] + [(got, slice(None)) for got in self.got])]

    def go_last(self, one):
        self.one = one


def join(first, second):
    parts = [([(first.one, half)], slice(half * 128, half * 128 + 128)) for half in range(2)]
    (_, terms), = second.last()
    for k in range(4):
        here = (slice(None), slice(k * 512, k * 512 + 512))
        cut = [(array, (0, *here) if index == 0 else here) for array, index in terms]
        parts.append((cut, slice(256 + k * 64, 320 + k * 64)))
    return (512, 512), parts


class Last:
    def __init__(self, one):
        self.one = one
        self.by_x, self.by_c = swap(one, "x"), swap(one, "c")

    def go_corner(self):
        self.corner = swap(self.by_x, "c")


def tall_shard_kernel(where, one, by_x, by_c, corner, out):
    x, c = where[2], where[3]
    n = one.shape[-1]
    for block, xx, cc in ((one, x, c), (by_x, 1 - x, c), (by_c, x, 1 - c), (corner, 1 - x, 1 - c)):
        for half in range(2):
            rows = pl.ds(pl.multiple_of(half * 256 + xx * 128, 128), 128)
            out[rows, lanes(cc * n, n)] = block[half * 128 : half * 128 + 128, :].astype(F32)


def up_shard_kernel(where, one, by_x, by_c, corner, up_out):
    x, c = where[2], where[3]
    for block, xx, cc in ((one, x, c), (by_x, 1 - x, c), (by_c, x, 1 - c), (corner, 1 - x, 1 - c)):
        rows = pl.ds(pl.multiple_of(xx * 64, 64), 64)
        for s in range(8):
            k = s // 2
            value = block[256 + k * 64 : 320 + k * 64, (s % 2) * 256 : (s % 2) * 256 + 256]
            up_out[rows, lanes(s * 512 + cc * 256, 256)] = value.astype(F32)


def qkv_shard_kernel(where, one, by_x, by_c, corner, out, out_out):
    x, c = where[2], where[3]
    for block, xx, cc in ((one, x, c), (by_x, 1 - x, c), (by_c, x, 1 - c), (corner, 1 - x, 1 - c)):
        rows = pl.ds(pl.multiple_of(xx * 64, 64), 64)
        for layer in range(3):
            out[rows, lanes(layer * 1024 + cc * 512, 512)] = block[:, layer * 512 : (layer + 1) * 512].astype(F32)
        out_out[rows, lanes(cc * 512, 512)] = block[:, 1536:].astype(F32)


def shard_of(kernel, where, r, shapes):
    return simple(kernel, (r.one, r.by_x, r.by_c, r.corner), [(s, F32) for s in shapes], where=where, pin_out=range(len(shapes)))


def table_kernel(got, table, vec):
    n = got.shape[0]
    times = lax.broadcasted_iota(jnp.int32, (128, 8), 0).astype(F32)
    total = jnp.zeros(table.shape, F32)
    sums = jnp.zeros(vec.shape, F32)
    for i in range(n):
        hot = (times == got[i, 18:19, 0:8]).astype(F32)
        total += lax.dot_general(hot, got[i, 0:8, :], (((1,), (0,)), ((), ())), precision=lax.Precision.HIGHEST)
        sums += got[i, 8:24, :]
    table[...] = total
    vec[...] = sums


def normalize(values):
    centred = values - jnp.mean(values, axis=-1, keepdims=True)
    spread = jnp.mean(centred * centred, axis=-1, keepdims=True)
    return centred * lax.rsqrt(spread + 1e-05)


def scaled_norm(values, gain):
    return normalize(values) * gain


def exact_gelu(values):
    return jax.nn.gelu(values, approximate=False)


def layer(
    tokens,
    time_index,
    table_all,
    gain_one,
    bias_one,
    qkv_w,
    out_w,
    out_b,
    gain_two,
    bias_two,
    up_w,
    up_b,
    down_w,
    down_b,
    cotangent,
):
    row_count, model_width = tokens.shape
    seq_count = time_index.shape[0]
    length = row_count // seq_count
    head_dim = model_width // HEADS
    factor = head_dim ** (-0.5)
    levels = table_all.shape[0]
    gain_one_f = gain_one.astype(jnp.float32)
    gain_two_f = gain_two.astype(jnp.float32)
    one_hot = time_index[:, None] == jnp.arange(levels, dtype=jnp.int32)[None, :]
    embedding = jnp.dot(one_hot.astype(jnp.bfloat16), table_all, preferred_element_type=jnp.float32)
    scale_seq = (1.0 + embedding)[:, None, :]
    inputs = tokens.astype(jnp.float32)
    normed = (normalize(inputs) * gain_one_f + bias_one.astype(jnp.float32)).reshape(
        seq_count, length, model_width
    )
    scaled = (normed * scale_seq).astype(jnp.bfloat16).reshape(row_count, model_width)
    packed = jnp.dot(scaled, qkv_w, preferred_element_type=jnp.float32).astype(jnp.bfloat16)
    packed = packed.reshape(seq_count, length, 3, HEADS, head_dim)
    queries = packed[:, :, 0]
    key_heads = packed[:, :, 1]
    value_heads = packed[:, :, 2]
    scores = (
        jnp.einsum("sqhd,skhd->shqk", queries, key_heads, preferred_element_type=jnp.float32)
        * factor
    )
    attn_probs = jax.nn.softmax(scores, axis=-1)
    probs_low = attn_probs.astype(jnp.bfloat16)
    attn_mix = jnp.einsum(
        "shqk,skhd->sqhd", probs_low, value_heads, preferred_element_type=jnp.float32
    )
    attn_mix = attn_mix.astype(jnp.bfloat16).reshape(row_count, model_width)
    middle = (
        inputs
        + jnp.dot(attn_mix, out_w, preferred_element_type=jnp.float32)
        + out_b.astype(jnp.float32)
    )
    hidden_in = (normalize(middle) * gain_two_f + bias_two.astype(jnp.float32)).astype(jnp.bfloat16)
    pre_act = jnp.dot(hidden_in, up_w, preferred_element_type=jnp.float32) + up_b.astype(
        jnp.float32
    )
    activated = exact_gelu(pre_act).astype(jnp.bfloat16)
    block_out = (
        middle
        + jnp.dot(activated, down_w, preferred_element_type=jnp.float32)
        + down_b.astype(jnp.float32)
    ).astype(jnp.bfloat16)
    upstream = cotangent.astype(jnp.float32)
    grad_down = jnp.einsum("ti,td->id", activated, cotangent, preferred_element_type=jnp.float32)
    grad_down_b = jnp.sum(upstream, axis=0)
    d_act = jnp.einsum("td,id->ti", cotangent, down_w, preferred_element_type=jnp.float32)
    gelu_pull = jax.vjp(exact_gelu, pre_act)[1]
    d_pre = gelu_pull(d_act)[0].astype(jnp.bfloat16)
    grad_up = jnp.einsum("ti,tf->if", hidden_in, d_pre, preferred_element_type=jnp.float32)
    grad_up_b = jnp.sum(d_pre.astype(jnp.float32), axis=0)
    d_hidden = jnp.einsum("tf,if->ti", d_pre, up_w, preferred_element_type=jnp.float32)
    grad_ln2_bias = jnp.sum(d_hidden, axis=0)
    second_pull = jax.vjp(scaled_norm, middle, gain_two_f)[1]
    d_mid_part, grad_ln2_gain = second_pull(d_hidden)
    d_middle = upstream + d_mid_part
    d_mid_low = d_middle.astype(jnp.bfloat16)
    grad_out_w = jnp.einsum("ti,td->id", attn_mix, d_mid_low, preferred_element_type=jnp.float32)
    grad_out_b = jnp.sum(d_mid_low.astype(jnp.float32), axis=0)
    d_mix = jnp.einsum("td,id->ti", d_mid_low, out_w, preferred_element_type=jnp.float32)
    d_mix = d_mix.astype(jnp.bfloat16).reshape(seq_count, length, HEADS, head_dim)
    d_probs = jnp.einsum("sqhd,skhd->shqk", d_mix, value_heads, preferred_element_type=jnp.float32)
    d_values = jnp.einsum("shqk,sqhd->skhd", probs_low, d_mix, preferred_element_type=jnp.float32)
    d_scores = (
        attn_probs * (d_probs - jnp.sum(d_probs * attn_probs, axis=-1, keepdims=True))
    ).astype(jnp.bfloat16)
    d_queries = (
        jnp.einsum("shqk,skhd->sqhd", d_scores, key_heads, preferred_element_type=jnp.float32)
        * factor
    )
    d_keys = (
        jnp.einsum("shqk,sqhd->skhd", d_scores, queries, preferred_element_type=jnp.float32)
        * factor
    )
    d_packed = (
        jnp.stack([d_queries, d_keys, d_values], axis=2)
        .astype(jnp.bfloat16)
        .reshape(row_count, 3 * model_width)
    )
    grad_qkv = jnp.einsum("ti,tf->if", scaled, d_packed, preferred_element_type=jnp.float32)
    d_scaled = jnp.einsum("tf,if->ti", d_packed, qkv_w, preferred_element_type=jnp.float32).reshape(
        seq_count, length, model_width
    )
    d_normed = d_scaled * scale_seq
    grad_ln1_bias = jnp.sum(d_normed, axis=(0, 1))
    d_embedding = jnp.sum(d_scaled * normed, axis=1)
    grad_table = jnp.einsum(
        "sn,sd->nd", one_hot.astype(jnp.float32), d_embedding, precision=lax.Precision.HIGHEST
    )
    first_pull = jax.vjp(scaled_norm, inputs, gain_one_f)[1]
    d_in_part, grad_ln1_gain = first_pull(d_normed.reshape(row_count, model_width))
    grad_tokens = (d_middle + d_in_part).astype(jnp.bfloat16)
    return (
        block_out,
        grad_tokens,
        (grad_table, grad_ln1_gain, grad_ln1_bias, grad_qkv, grad_out_w, grad_out_b, grad_ln2_gain,
         grad_ln2_bias, grad_up, grad_up_b, grad_down, grad_down_b),
    )


def plain(*args):
    dims = (None, None, 1, 0, 0, 0, 0, 0, 0, 0, 0, 0, 0, 0, None)
    whole = [
        item if dim is None else lax.all_gather(item, "fsdp", axis=dim, tiled=True)
        for item, dim in zip(args, dims, strict=True)
    ]
    block_out, grad_tokens, grads = layer(*whole)
    shares = [
        lax.psum_scatter(grad, "fsdp", scatter_dimension=1 if place == 0 else 0, tiled=True)
        for place, grad in enumerate(grads)
    ]
    return (block_out, grad_tokens, *lax.psum(tuple(shares), "dp"))


def eight_by_four(
    tokens, time_index, time_table, ln1_gain, ln1_bias, w_qkv, w_out, b_out, ln2_gain, ln2_bias,
    w_up, b_up, w_down, b_down, cotangent,
):
    where = jnp.stack(coords()).astype(jnp.int32)
    seqs = time_index.shape[0]
    length = tokens.shape[0] // seqs
    vec = jnp.concatenate(
        [v.reshape(-1, 128) for v in (ln1_gain, ln1_bias, b_out, ln2_gain, ln2_bias, b_down, b_up)]
        + [jnp.zeros((6, 128), LOW)]
    )
    times = time_index.reshape(seqs, 1)
    chain.clear()

    (parts_first,) = (
        simple(own_first_kernel, (w_qkv, w_out), [((2, 128, CW), LOW)], where=where)
    )
    small = jnp.concatenate([time_table, vec])
    small_side = swap(small, "y")
    pieces = [Piece(parts_first, (i,), (128, CW), 1) for i in range(2)]
    near = swap(parts_first, "z1")
    for piece in pieces:
        piece.move_z1(near, piece.index)

    def tick(*jobs, extra=(), passing=()):
        stages = {
            "z": ("two", "move_z2"), "y": ("four", "move_y"), "x": ("across_send", "move_x"), "c": ("core_send", "move_c"),
        }
        jobs = [(pieces[n], *stages[stage]) for stage, n in jobs]
        made = (move([getattr(p, make)() for p, make, _ in jobs] + list(extra), passing=passing))
        for (p, _, go), value in zip(jobs, made):
            getattr(p, go)(value)
        return made[len(jobs) :]

    extra = [((2, 144, 128), [(small, (), 0), (small_side, (), 1)])]
    (small_two,) = tick(("z", 0), ("z", 1), extra=extra)
    small_near = swap(small_two, "z1")
    parts_up, parts_down = (
        simple(
            own_other_kernel, (w_up, w_down), [((2, 128, CW), LOW), ((2, RW, 1024), LOW)], where=where
        )
    )
    pieces += [Piece(parts_up, (i,), (128, CW), 1) for i in range(2)]
    pieces += [Piece(parts_down, (i,), (RW, 1024), 0) for i in range(2)]
    near_up, near_down = swap(parts_up, "z1"), swap(parts_down, "z1")
    for i in range(2):
        pieces[2 + i].move_z1(near_up, (i,))
        pieces[4 + i].move_z1(near_down, (i,))
    everything = slice(None)
    owns = [
        [(w_qkv, [(everything, pl.ds(0, 2048))], [0], 2048)],
        [(w_qkv, [(everything, pl.ds(2048, 1024))], [0], 1024), (w_out, [(everything, everything)], [1024], 1024)],
    ]
    for half in range(2):
        reads = [(everything, pl.ds(s * 512 + half * 256, 256)) for s in range(8)]
        owns.append([(w_up, reads, [s * 256 for s in range(8)], 256)])
    for half in range(2):
        owns.append([(w_down, [(pl.ds(half * 256, 256), everything)], [0], 256)])

    def whole(n):
        return (assemble(where, pieces[n], owns[n]))

    extra = [((4, 144, 128), [(small_two, (), slice(0, 2)), (small_near, (), slice(2, 4))])]
    (small_four,) = tick(("y", 0), extra=extra)
    small_far = swap(small_four, "z2")
    table, vec, up_b, scale = (small_params(where, small_four, small_far, times))
    tick(("x", 0), ("y", 1), ("z", 2))
    tick(("c", 0), ("x", 1), ("y", 2), ("z", 3))
    gain_one, bias_one, out_b, gain_two, bias_two, down_b = (vec[i : i + 1] for i in range(6))
    scale = scale.reshape(seqs, 1, -1)
    scaled = (first_norm(tokens, gain_one, bias_one, scale))
    w_qk = whole(0)
    tick(("c", 1), ("x", 2), ("y", 3), ("z", 4))
    qk = (project(scaled, w_qk))
    vo = whole(1)
    begun = (attend(scaled, qk, vo, length, 0, 2))
    tick(("c", 2), ("x", 3), ("y", 4), ("z", 5))
    v, probs, mix = (attend(scaled, qk, vo, length, 2, 2, begun))
    middle, hidden = (second_norm(mix, tokens, vo, out_b, gain_two, bias_two))
    up_a = whole(2)
    tick(("c", 3), ("x", 4), ("y", 5))
    act_a, slope_a = (up(hidden, up_a, up_b[0:1]))
    up_b_w = whole(3)
    tick(("c", 4), ("x", 5))
    act_b, slope_b = (up(hidden, up_b_w, up_b[1:2]))
    def step(*jobs, passing=()):
        lists = [getattr(r, stage)() for r, stage in jobs]
        made = (add_up([item for items in lists for item in items], passing=passing))
        for (r, stage), items in zip(jobs, lists, strict=True):
            values, made = made[: len(items)], made[len(items) :]
            go = "go_last" if stage == "last_direct" else "go_" + stage
            getattr(r, go)(*values)
        return made

    acts = (act_a, act_b)
    downs = [whole(4)]
    away = (tall_away(where, acts, cotangent))
    (away,) = tick(("c", 5), passing=(away,))
    core_one = swap(away, "c")
    d_pre, up_sum_a = (pull(cotangent, downs[0], slope_a, 0))
    downs.append(whole(5))
    d_pre, up_sum_b = (pull(cotangent, downs[1], slope_b, 1, d_pre))
    pairs_two = [(hidden, d_pre, "layer")]
    core_two = swap((row_away(where, pairs_two)), "c")
    xa, yb, *keep = (tall_mine(where, acts, cotangent, core_one))
    one = Reduction(*keep)
    one.go_first(xa, yb)
    xa, yb, *keep = (row_mine(where, pairs_two, core_two))
    two = Reduction(*keep)
    two.go_first(xa, yb)
    d_middle, d_low, d_mix, sums_two = (
        middle_back(d_pre, (up_a, up_b_w), middle, cotangent, gain_two, vo)
    )
    step((one, "second"))
    d_packed = (attend_back(d_mix, probs, qk, v, length))
    pairs_three = [(scaled, d_packed, "layers"), (mix, d_low, "columns")]
    away = (row_away(where, pairs_three))
    (away,) = step((two, "second"), passing=(away,))
    core_three = swap(away, "c")
    grad_tokens, sums_one, d_emb = (
        input_back(d_packed, w_qk, vo, tokens, d_middle, gain_one, bias_one, scale)
    )
    step((one, "third"))
    *sends, ka, kb = (row_mine(where, pairs_three, core_three))
    three = Reduction(ka, kb)
    three.go_first(*step((two, "third"), passing=sends))
    (rows,) = (
        simple(
            rows_kernel,
            (d_emb, sums_one, sums_two, up_sum_a, up_sum_b, jnp.pad(time_index.astype(F32), (0, 120))[None]),
            [((32, 24, 128), F32)],
        )
    )
    got = lax.all_to_all(rows, BOTH, 0, 0)
    block_out = (down(acts, downs, middle, down_b))
    step((one, "fourth"), (three, "second"))
    step((two, "fourth"), (three, "third_direct"))
    step((one, "last"))
    (joined,) = (add_up([join(one, two)]))
    early = Last(joined)
    grad_table, sums = (
        simple(table_kernel, (got,), [((128, 128), F32), ((16, 128), F32)])
    )
    early.go_corner()
    step((three, "last_direct"))
    late = Last(three.one)
    (down_shard,) = (shard_of(tall_shard_kernel, where, early, [(512, 1024)]))
    (up_shard,) = (shard_of(up_shard_kernel, where, early, [(128, 4096)]))
    late.go_corner()
    qkv_shard, out_shard = (shard_of(qkv_shard_kernel, where, late, [(128, 3072), (128, 1024)]))
    return (
        block_out, grad_tokens, grad_table, sums[0], sums[1], qkv_shard, out_shard, sums[2], sums[3], sums[4],
        up_shard, sums[6:10].reshape(512), down_shard, sums[5],
    )


def solution(mesh):
    in_specs = (
        P(("fsdp", "dp"), None),
        P(("fsdp", "dp")),
        P(None, "fsdp"),
        P("fsdp"),
        P("fsdp"),
        P("fsdp", None),
        P("fsdp", None),
        P("fsdp"),
        P("fsdp"),
        P("fsdp"),
        P("fsdp", None),
        P("fsdp"),
        P("fsdp", None),
        P("fsdp"),
        P(("fsdp", "dp"), None),
    )
    out_specs = (
        P(("fsdp", "dp"), None),
        P(("fsdp", "dp"), None),
        P(None, "fsdp"),
        P("fsdp"),
        P("fsdp"),
        P("fsdp", None),
        P("fsdp", None),
        P("fsdp"),
        P("fsdp"),
        P("fsdp"),
        P("fsdp", None),
        P("fsdp"),
        P("fsdp", None),
        P("fsdp"),
    )
    local = eight_by_four if (mesh.shape["fsdp"], mesh.shape["dp"]) == (8, 4) else plain
    return jax.shard_map(local, mesh=mesh, in_specs=in_specs, out_specs=out_specs, check_vma=False)
```

```python
import functools

import jax
import jax.numpy as jnp
from jax import lax
from jax.experimental import pallas as pl
from jax.experimental.pallas import tpu as pltpu
from jax.sharding import PartitionSpec as P

HEADS = 16
BOTH = ("fsdp", "dp")
LOW = jnp.bfloat16
F32 = jnp.float32
NT = (((1,), (1,)), ((), ()))
TN = (((0,), (0,)), ((), ()))


def flips(which):
    pairs = []
    for f in range(8):
        for d in range(4):
            z, y, x, c = f // 2, f % 2, d // 2, d % 2
            if which == "x":
                x = 1 - x
            elif which == "y":
                y = 1 - y
            elif which == "c":
                c = 1 - c
            elif which == "z1":
                z = z ^ 1
            elif which == "z2":
                z = z ^ 2
            elif which == "z3":
                z = z ^ 3
            pairs.append((f * 4 + d, (z * 2 + y) * 4 + x * 2 + c))
    return pairs


def swap(values, which):
    return lax.ppermute(values, BOTH, flips(which))


def coords():
    f, d = lax.axis_index("fsdp"), lax.axis_index("dp")
    return f // 2, f % 2, d // 2, d % 2


def call(kernel, grid, ins, outs, flops=0, nbytes=0, scratch=(), prefetch=0, aliases=None, limit=18, pin=(), pin_out=(), cost=0
):
    after = tuple(chain)

    def spec(block, index):
        if block is None:
            return pl.BlockSpec(memory_space=pl.ANY)
        if block == "hbm":
            return pl.BlockSpec(memory_space=pltpu.MemorySpace.HBM)
        if index in constant and grid:
            return pl.BlockSpec(block, index, pipeline_mode=pl.Buffered(1))
        return pl.BlockSpec(block, index)

    def body(*refs):
        n = prefetch + len(ins)
        m = n + len(after) + len(outs)
        kernel(*refs[:n], *refs[n + len(after) : m], *refs[m + 1 :])

    run = pl.pallas_call(
        body,
        out_shape=[
            pltpu.MemorySpace.HBM(shape, kind) if k in pin_out else jax.ShapeDtypeStruct(shape, kind)
            for k, (shape, kind, _, _) in enumerate(outs)
        ]
        + [pltpu.MemorySpace.HBM((8, 128), F32)],
        grid_spec=pltpu.PrefetchScalarGridSpec(
            num_scalar_prefetch=prefetch,
            grid=grid,
            in_specs=[spec(block, index) for block, index in ins] + [spec(None, None)] * len(after),
            out_specs=[spec(block, index) for _, _, block, index in outs] + [spec(None, None)],
            scratch_shapes=scratch,
        ),
        input_output_aliases=aliases or {},
        compiler_params=pltpu.CompilerParams(
            vmem_limit_bytes=limit * 2**20, dimension_semantics=("arbitrary",) * len(grid)
        ),
        cost_estimate=pl.CostEstimate(flops=cost, bytes_accessed=1024, transcendentals=0),
    )

    def pinned(*args):
        args = [
            pltpu.with_memory_space_constraint(a, pltpu.MemorySpace.HBM) if k - prefetch in pin else a
            for k, a in enumerate(args)
        ]
        *values, token = run(*args, *(pltpu.with_memory_space_constraint(t, pltpu.MemorySpace.HBM) for t in after))
        chain[:] = [token]
        return values

    return pinned


def simple(kernel, args, outs, where=None, passing=(), limit=12, pin_out=(), cost=0):
    def whole(shape):
        return shape, lambda *_: (0,) * len(shape)

    prefetch = 0 if where is None else 1
    n_in, n_out, n_pass = len(args), len(outs), len(passing)

    def body(*refs):
        first = prefetch + n_in
        kernel(*refs[:first], *refs[first + n_pass : first + n_pass + n_out])

    run = call(
        body,
        (),
        [whole(a.shape) for a in args] + [(None, None)] * n_pass,
        [(shape, kind, *whole(shape)) for shape, kind in outs] + [(a.shape, a.dtype, None, None) for a in passing],
        prefetch=prefetch,
        aliases={prefetch + n_in + k: n_out + k for k in range(n_pass)},
        limit=limit,
        pin_out=pin_out,
        cost=cost,
    )
    return run(*(() if where is None else (where,)), *args, *passing)


constant = []
chain = []


def fixed(*index):
    constant.append(lambda *grid: index)
    return constant[-1]


def ends(n):
    e = n * 3 // 8
    return e // 2, (n - 2 * e) // 2


def end_start(n, x, c):
    eh, mh = ends(n)
    return x * (n - 2 * eh) + c * eh


def middle_start(n, c):
    eh, mh = ends(n)
    return 2 * eh + c * mh


COLS = 2048
CE, CM = ends(COLS)
CW = CE + CM


def lanes(start, size=128):
    return pl.ds(start if isinstance(start, int) else pl.multiple_of(start, 128), size)


def own_columns(where, dest, read):
    x, c = where[2], where[3]
    for i in range(CW // 128):
        start = end_start(COLS, x, c) + i * 128 if i < CE // 128 else middle_start(COLS, c) + i * 128 - CE
        dest[:, i * 128 : (i + 1) * 128] = read(start)


def own_first_kernel(where, qkv, out_w, parts):
    own_columns(where, parts.at[0], lambda start: qkv[:, lanes(start)])
    own_columns(
        where,
        parts.at[1],
        lambda start: jnp.where(
            start < 1024, qkv[:, lanes(2048 + jnp.minimum(start, 896))], out_w[:, lanes(jnp.maximum(start - 1024, 0))]
        ),
    )


def own_other_kernel(where, up_w, down_w, parts):
    for half in range(2):
        own_columns(
            where, parts.at[half], lambda start: up_w[:, lanes((start // 256) * 512 + half * 256 + start % 256)]
        )
        own_columns(
            where,
            parts.at[2 + half],
            lambda start: down_w[
                pl.ds(pl.multiple_of(half * 256 + (start // 1024) * 128, 128), 128), lanes(start % 1024)
            ],
        )


def move(jobs, passing=()):
    args = []
    for _, copies in jobs:
        for array, _, _ in copies:
            if not any(array is a for a in args):
                args.append(array)

    def kernel(*refs):
        outs = refs[len(args) :]
        for out, (_, copies) in zip(outs, jobs, strict=True):
            for array, read, write in copies:
                ref = refs[[i for i, a in enumerate(args) if a is array][0]]
                out[write] = ref[read if read != () else ...]

    return simple(kernel, args, [(shape, LOW) for shape, _ in jobs], passing=passing)


class Piece:
    def __init__(self, part, index, tall=False):
        self.part, self.index, self.tall = part, index, tall
        self.shape = (128, CW)

    def two(self):
        return (2, *self.shape), [(self.part, self.index, 0), (self.near, self.near_index, 1)]

    def four(self):
        return (4, *self.shape), [
            (self.part, self.index, 0),
            (self.near, self.near_index, 1),
            (self.far, slice(None), slice(2, 4)),
        ]

    def blocks(self):
        found = [(self.near, self.near_index)] + [(self.far, (i,)) for i in range(2)]
        return found + [(self.beside, (i,)) for i in range(4)]

    def across_send(self):
        end = (slice(None), slice(0, CE))
        return (7, 128, CE), [(a, (*i, *end), j) for j, (a, i) in enumerate(self.blocks())]

    def core_send(self):
        first, last = (slice(None), slice(0, CW)), (slice(None), slice(CW, CW + CE))
        copies = [(a, i, (j, *first)) for j, (a, i) in enumerate(self.blocks())]
        return (7, 128, CW + CE), copies + [(self.across, j, (j, *last)) for j in range(7)]

    def move_z1(self, near, near_index):
        self.near, self.near_index = near, near_index

    def move_z2(self, two):
        self.far = swap(two, "z2")

    def move_y(self, four):
        self.beside = swap(four, "y")

    def move_x(self, send):
        self.across = swap(send, "x")

    def move_c(self, send):
        self.other = swap(send, "c")


def assemble_kernel(tall, own_copies, near_index, where, *refs):
    n_own = len(own_copies)
    owns = refs[:n_own]
    near, far, beside, across, other, out, sems = refs[n_own:]
    z, y, x, c = where[0], where[1], where[2], where[3]
    eh, mh = CE, CM

    def at(shard, start, count):
        if not tall:
            return out.at[pl.ds(pl.multiple_of(shard * 128, 128), 128), lanes(start, count)]
        row = shard * 256 + (start // 1024) * 128
        return out.at[pl.ds(pl.multiple_of(row, 128), 128), lanes(start % 1024, count)]

    def cut(block, start, count):
        return block.at[:, pl.ds(start, count)]

    copies = []
    for j in range(8):
        shard = (z ^ (j % 4)) * 2 + (y if j < 4 else 1 - y)
        if j == 0:
            for ref, (read, start, count) in zip(owns, own_copies, strict=True):
                for k in range(len(read)):
                    copies.append((ref.at[read[k]], at(shard, start[k], count)))
            continue
        close = near.at[near_index[0]] if near_index else near
        mine = (close, far.at[0], far.at[1], beside.at[0], beside.at[1], beside.at[2], beside.at[3])[j - 1]
        oc = 1 - c
        copies += [
            (cut(mine, 0, eh), at(shard, end_start(COLS, x, c), eh)),
            (cut(mine, eh, mh), at(shard, middle_start(COLS, c), mh)),
            (cut(across.at[j - 1], 0, eh), at(shard, end_start(COLS, 1 - x, c), eh)),
            (cut(other.at[j - 1], 0, eh), at(shard, end_start(COLS, x, oc), eh)),
            (cut(other.at[j - 1], eh, mh), at(shard, middle_start(COLS, oc), mh)),
            (cut(other.at[j - 1], eh + mh, eh), at(shard, end_start(COLS, 1 - x, oc), eh)),
        ]
    copies = [pltpu.make_async_copy(s, d, sems.at[k]) for k, (s, d) in enumerate(copies)]
    for copy in copies:
        copy.start()
    for copy in copies:
        copy.wait()


def assemble(where, piece, owns):
    shape = (2048, 1024) if piece.tall else (1024, COLS)
    args = [o[0] for o in owns] + [piece.near, piece.far, piece.beside, piece.across, piece.other]
    n_copies = 42 + sum(len(o[1]) for o in owns)
    return call(
        functools.partial(assemble_kernel, piece.tall, [o[1:] for o in owns], piece.near_index),
        (),
        [(None, None)] * len(args),
        [(shape, LOW, shape, lambda *_: (0, 0))],
        prefetch=1,
        scratch=[pltpu.SemaphoreType.DMA((n_copies,))],
        limit=8,
    )(where, *args)[0]


def small_kernel(where, four, beside, time_index, table, vec, up_b, scale):
    z, y = where[0], where[1]
    for j in range(8):
        block = four.at[j] if j < 4 else beside.at[j - 4]
        shard = (z ^ (j // 2)) * 2 + (y ^ (j % 2))
        table[:, lanes(shard * 128)] = block[:128, :]
        vec[:, lanes(shard * 128)] = block[128:, :].astype(F32)
        for row in range(4):
            unit = lanes(shard * 256 + (row % 2) * 128)
            up_b[row // 2 : row // 2 + 1, unit] = block[134 + row : 135 + row, :].astype(F32)
    numbers = lax.broadcasted_iota(jnp.int32, (time_index.shape[0], 128), 1)
    one_hot = (numbers == time_index[...]).astype(F32).astype(LOW)
    scale[...] = 1.0 + jnp.dot(one_hot, table[...], preferred_element_type=F32)


def small_params(where, four, beside, time_index):
    return simple(
        small_kernel,
        (four, beside, time_index),
        [((128, 1024), LOW), ((16, 1024), F32), ((2, 2048), F32), ((time_index.shape[0], 1024), F32)],
        where=where,
    )


def rows_kernel(d_emb, sums_one, sums_two, up_a, up_b, times, out):
    for s in range(8):
        here = slice(s * 128, (s + 1) * 128)
        rows = [d_emb[i, :, here] for i in range(8)]
        rows += [sums_one[0:2, here], sums_two[2:3, here], sums_two[0:2, here], sums_two[3:4, here]]
        for sums in (up_a, up_b):
            rows += [sums[:, s * 256 + j * 128 : s * 256 + (j + 1) * 128] for j in range(2)]
        rows += [times[...], jnp.zeros((5, 128), F32)]
        block = jnp.concatenate(rows, axis=0)
        for copy in range(4):
            out[s * 4 + copy] = block


def mm(a, b):
    return jnp.dot(a, b, preferred_element_type=F32)


def mm_nt(a, b):
    return lax.dot_general(a, b, NT, preferred_element_type=F32)


def mm_tn(a, b):
    return lax.dot_general(a, b, TN, preferred_element_type=F32)


def centre(values):
    mean = jnp.mean(values, axis=-1, keepdims=True)
    centred = values - mean
    scale = lax.rsqrt(jnp.mean(centred * centred, axis=-1, keepdims=True) + 1e-05)
    return centred * scale, scale


def first_norm_kernel(tokens, gain, bias, scale, scaled):
    hat, _ = centre(tokens[...].astype(F32))
    scaled[...] = ((hat * gain[...] + bias[...]) * scale[0]).astype(LOW)


def first_norm(tokens, gain, bias, scale):
    rows, width = tokens.shape
    seqs = scale.shape[0]
    length = rows // seqs
    return call(
        first_norm_kernel,
        (seqs,),
        [
            ((length, width), lambda i: (i, 0)),
            ((1, width), fixed(0, 0)),
            ((1, width), fixed(0, 0)),
            ((1, 1, width), lambda i: (i, 0, 0)),
        ],
        [((rows, width), LOW, (length, width), lambda i: (i, 0))],
    )(tokens, gain, bias, scale)[0]


def halves(values):
    lane = lax.broadcasted_iota(jnp.int32, values.shape, 1)
    zero = jnp.zeros_like(values)
    return jnp.concatenate([jnp.where(lane < 64, values, zero), jnp.where(lane < 64, zero, values)], axis=0)


def side(values):
    n = values.shape[0] // 2
    return jnp.concatenate([values[:n], values[n:]], axis=1)


def project_kernel(x, w, out):
    out[...] = mm(x[...], w[...]).astype(LOW)


def project(x, w, tile=512):
    rows, width = x.shape
    n = w.shape[1]
    return call(
        project_kernel,
        (n // tile,),
        [((rows, width), fixed(0, 0)), ((width, tile), lambda i: (0, i))],
        [((rows, n), LOW, (rows, tile), lambda i: (0, i))],
    )(x, w)[0]


def units_of(rows, length, at_once=8):
    units = []
    for seq in range(rows // length):
        for pair in range(2):
            units.append((seq, pair, (slice(seq * length, (seq + 1) * length), slice(pair * 128, (pair + 1) * 128))))
    return [units[i : i + at_once] for i in range(0, len(units), at_once)]


def attend_kernel(length, scaled, wv, q_in, k_in, *refs):
    v_out, probs_out, mix_out = refs[-3:]
    factor = 64 ** (-0.5) * 1.4426950408889634
    v_out[...] = mm(scaled[...], wv[...]).astype(LOW)
    for units in units_of(scaled.shape[0], length):
        scores = [mm_nt(halves(q_in[here]), k_in[here]) for _, _, here in units]
        found = []
        for s in scores:
            e = jnp.exp2((s - jnp.max(s, axis=-1, keepdims=True)) * factor)
            found.append((e * (1.0 / jnp.sum(e, axis=-1, keepdims=True))).astype(LOW))
        for (seq, pair, here), probs in zip(units, found, strict=True):
            probs_out[0, seq, pair] = probs
            mix_out[here] = mm(side(probs), halves(v_out[here])).astype(LOW)


def attend(scaled, qk, vo, length, first=0, count=None, earlier=()):
    rows, width = scaled.shape
    groups = width // 256
    seqs = rows // length
    count = groups if count is None else count
    column = lambda i: (0, first + i)
    wide = ((rows, width), LOW, (rows, 256), column)
    probs = (groups, seqs, 2, 2 * length, length)
    return call(
        functools.partial(attend_kernel, length),
        (count,),
        [
            ((rows, width), fixed(0, 0)),
            ((width, 256), column),
            ((rows, 256), column),
            ((rows, 256), lambda i: (0, groups + first + i)),
        ]
        + [(None, None)] * len(earlier),
        [wide, (probs, LOW, (1, *probs[1:]), lambda i: (first + i, 0, 0, 0, 0)), wide],
        aliases={4 + i: i for i in range(len(earlier))},
    )(scaled, vo, qk, qk, *earlier)


def middle_kernel(mix, tokens, w, out_b, gain, bias, middle_out, hidden_out):
    middle = tokens[...].astype(F32) + mm(mix[...], w[...]) + out_b[...]
    middle_out[...] = middle
    hat, _ = centre(middle)
    hidden_out[...] = (hat * gain[...] + bias[...]).astype(LOW)


def second_norm(mix, tokens, vo, out_b, gain, bias):
    rows, width = tokens.shape
    row = lambda i: (i, 0)
    vec = ((1, width), fixed(0, 0))
    return call(
        middle_kernel,
        (rows // 256,),
        [((256, width), row), ((256, width), row), ((width, width), fixed(0, 1)), vec, vec, vec],
        [((rows, width), F32, (256, width), row), ((rows, width), LOW, (256, width), row)],
    )(mix, tokens, vo, out_b, gain, bias)


def gelu_parts(v):
    cdf = 0.5 + 0.5 * lax.erf(v * 0.5**0.5)
    bell = jnp.exp(-0.5 * v * v)
    return v * cdf, cdf + (v * 0.3989422804014327) * bell


def up_kernel(hidden, w, bias, act, slope):
    value, pull = gelu_parts(mm(hidden[...], w[...]) + bias[...])
    act[...] = value.astype(LOW)
    slope[...] = pull.astype(LOW)


def up(hidden, w, bias, tile=512):
    rows, width = hidden.shape
    n = w.shape[1]
    column = lambda i: (0, i)
    return call(
        up_kernel,
        (n // tile,),
        [((rows, width), fixed(0, 0)), ((width, tile), column), ((1, tile), column)],
        [((rows, n), LOW, (rows, tile), column)] * 2,
        limit=22,
    )(hidden, w, bias)


def down_kernel(act_a, act_b, first, second, middle, bias, *refs):
    total = middle[...] + bias[...]
    total += mm(act_a[...], first[...])
    total += mm(act_b[...], second[...])
    refs[-1][...] = total.astype(LOW)


def down(acts, ws, middle, bias, start, count, earlier=(), tile=256):
    rows, width = middle.shape
    k = ws[0].shape[0]
    row = lambda i: (start + i, 0)
    return call(
        down_kernel,
        (count,),
        [((tile, k), row)] * 2
        + [((k, width), fixed(0, 0))] * 2
        + [((tile, width), row), ((1, width), fixed(0, 0))]
        + [(None, None)] * len(earlier),
        [((rows, width), LOW, (tile, width), row)],
        aliases={6 + i: i for i in range(len(earlier))},
        limit=56,
    )(*acts, *ws, middle, bias, *earlier)[0]


def pull_kernel(cot, w, slope, *refs):
    d_pre, sums = refs[-2:]
    value = (mm_nt(cot[...], w[...]) * slope[...].astype(F32)).astype(LOW)
    d_pre[0] = value
    sums[...] = jnp.sum(value.astype(F32), axis=0, keepdims=True)


def pull(cot, w, slope, half, earlier=None, tile=512):
    rows, width = cot.shape
    n = w.shape[0]
    column = lambda i: (0, i)
    ins = [((rows, width), fixed(0, 0)), ((tile, width), lambda i: (i, 0)), ((rows, tile), column)]
    return call(
        pull_kernel,
        (n // tile,),
        ins + ([] if earlier is None else [(None, None)]),
        [((2, rows, n), LOW, (1, rows, tile), lambda i: (half, 0, i)), ((1, n), F32, (1, tile), column)],
        aliases={} if earlier is None else {3: 0},
    )(cot, w, slope, *(() if earlier is None else (earlier,)))


def norm_back(d_out, hat, scale, gain):
    e = d_out * gain
    mean = jnp.mean(e, axis=-1, keepdims=True)
    slant = jnp.mean(e * hat, axis=-1, keepdims=True)
    return (e - mean - hat * slant) * scale


def fold(*rows_of):
    sums = [jnp.sum(v, axis=0, keepdims=True) for v in rows_of]
    return jnp.concatenate(sums + [jnp.zeros_like(sums[0])] * (8 - len(sums)), axis=0)


def middle_back_kernel(d_pre, wa, wb, middle, cot, gain, w_out, d_middle_out, d_low_out, d_mix_out, sums):
    d_hidden = mm_nt(d_pre[0], wa[...]) + mm_nt(d_pre[1], wb[...])
    hat, scale = centre(middle[...])
    d_middle = cot[...].astype(F32) + norm_back(d_hidden, hat, scale, gain[...])
    d_middle_out[...] = d_middle
    d_low = d_middle.astype(LOW)
    d_low_out[...] = d_low
    d_mix_out[...] = mm_nt(d_low, w_out[...]).astype(LOW)

    @pl.when(pl.program_id(0) == 0)
    def _():
        sums[...] = jnp.zeros_like(sums)

    sums[...] += fold(d_hidden * hat, d_hidden, d_low.astype(F32), cot[...].astype(F32))


def middle_back(d_pre, ws, middle, cot, gain, vo, tile=256):
    rows, width = middle.shape
    row = lambda i: (i, 0)
    return call(
        middle_back_kernel,
        (rows // tile,),
        [
            ((2, tile, d_pre.shape[2]), lambda i: (0, i, 0)),
            (ws[0].shape, fixed(0, 0)),
            (ws[1].shape, fixed(0, 0)),
            ((tile, width), row),
            ((tile, width), row),
            ((1, width), fixed(0, 0)),
            ((width, width), fixed(0, 1)),
        ],
        [
            ((rows, width), F32, (tile, width), row),
            ((rows, width), LOW, (tile, width), row),
            ((rows, width), LOW, (tile, width), row),
            ((8, width), F32, (8, width), fixed(0, 0)),
        ],
        limit=32,
    )(d_pre, *ws, middle, cot, gain, vo)


def attend_back_kernel(length, d_mix, probs, q_in, k_in, v_in, *refs):
    out = refs[-1]
    factor = 64 ** (-0.5)
    for units in units_of(d_mix.shape[0], length, 4):
        dms = [halves(d_mix[here]) for _, _, here in units]
        d_probs = [mm_nt(dm, v_in[here]) for dm, (_, _, here) in zip(dms, units, strict=True)]
        found = []
        for d, (seq, pair, _) in zip(d_probs, units, strict=True):
            high = probs[0, seq, pair].astype(F32)
            found.append((high * (d - jnp.sum(d * high, axis=-1, keepdims=True))).astype(LOW))
        for dm, d_scores, (seq, pair, here) in zip(dms, found, units, strict=True):
            out[(2, *here)] = mm_tn(probs[0, seq, pair], dm).astype(LOW)
            out[(0, *here)] = (mm(side(d_scores), halves(k_in[here])) * factor).astype(LOW)
            out[(1, *here)] = (mm_tn(d_scores, halves(q_in[here])) * factor).astype(LOW)


def attend_back(d_mix, probs, qk, v, length, first=0, count=None, earlier=()):
    rows, width = d_mix.shape
    count = width // 256 if count is None else count
    wide = ((rows, 256), lambda i: (0, first + i))
    return call(
        functools.partial(attend_back_kernel, length),
        (count,),
        [
            wide,
            ((1,) + probs.shape[1:], lambda i: (first + i, 0, 0, 0, 0)),
            wide,
            ((rows, 256), lambda i: (0, width // 256 + first + i)),
            wide,
        ]
        + [(None, None)] * len(earlier),
        [((3, rows, width), LOW, (3, rows, 256), lambda i: (0, 0, first + i))],
        aliases={5 + i: i for i in range(len(earlier))},
    )(d_mix, probs, qk, qk, v, *earlier)[0]


def input_back_kernel(length, d, wq, wk, wv, tokens, d_middle, gain, bias, scale, out, sums, d_emb):
    d_scaled = mm_nt(d[0], wq[...]) + mm_nt(d[1], wk[...]) + mm_nt(d[2], wv[...])
    hat, spread = centre(tokens[...].astype(F32))
    normed = hat * gain[...] + bias[...]
    count = tokens.shape[0] // length
    parts = []
    for i in range(count):
        here = slice(i * length, (i + 1) * length)
        d_emb[i] = jnp.sum(d_scaled[here] * normed[here], axis=0, keepdims=True)
        parts.append(d_scaled[here] * scale[i])
    d_normed = jnp.concatenate(parts, axis=0)
    out[...] = (d_middle[...] + norm_back(d_normed, hat, spread, gain[...])).astype(LOW)

    @pl.when(pl.program_id(0) == 0)
    def _():
        sums[...] = jnp.zeros_like(sums)

    sums[...] += fold(d_normed * hat, d_normed)


def input_back(d_packed, qk, vo, tokens, d_middle, gain, bias, scale, tile=256, cost=0):
    rows, width = tokens.shape
    seqs = scale.shape[0]
    length = rows // seqs
    row = lambda i: (i, 0)
    wide = ((tile, width), row)
    vec = ((1, width), fixed(0, 0))
    some = ((tile // length, 1, width), lambda i: (i, 0, 0))
    return call(
        functools.partial(input_back_kernel, length),
        (rows // tile,),
        [
            ((3, tile, width), lambda i: (0, i, 0)),
            ((width, width), fixed(0, 0)),
            ((width, width), fixed(0, 1)),
            ((width, width), fixed(0, 0)),
            wide, wide, vec, vec, some,
        ],
        [
            ((rows, width), LOW, (tile, width), row),
            ((8, width), F32, (8, width), fixed(0, 0)),
            ((seqs, 1, width), F32) + some,
        ],
        cost=cost,
        limit=26,
    )(d_packed, qk, qk, vo, tokens, d_middle, gain, bias, scale)


def tall_parts(where, a, b, cot, yy):
    here = slice(yy * 256, (yy + 1) * 256)
    value = mm_tn(jnp.concatenate([a[:, here], b[:, here]], axis=1), cot[...])
    x = where[2]
    found = []
    for xr in range(2):
        pair = []
        for half in range(2):
            low, high = value[half * 256 : half * 256 + 128], value[half * 256 + 128 : half * 256 + 256]
            pair.append(jnp.where((x ^ xr) == 0, low, high))
        found.append(pair)
    return found


def tall_away_kernel(where, a, b, cot, away):
    for yy in range(2):
        found = tall_parts(where, a, b, cot, yy)
        for xr in range(2):
            for half in range(2):
                away[xr, yy ^ where[1], 0, half] = found[xr][half].astype(LOW)


def tall_ins(acts, cot, core):
    rows, width = cot.shape
    act = ((rows, 512), lambda zr, where: (0, zr ^ where[0]))
    return [act, act, ((rows, width // 2), lambda zr, where: (0, where[3] ^ core))]


def tall_away(where, acts, cot):
    n = cot.shape[1] // 2
    return call(
        tall_away_kernel,
        (4,),
        tall_ins(acts, cot, 1),
        [((2, 2, 4, 2, 128, n), LOW, (2, 2, 1, 2, 128, n), lambda zr, where: (0, 0, zr, 0, 0, 0))],
        prefetch=1,
    )(where, *acts, cot)[0]


def tall_mine_kernel(where, a, b, cot, core, xa, yb, ka, kb):
    far = pl.program_id(0) >= 2
    for yy in range(2):
        found = tall_parts(where, a, b, cot, yy)
        yr = yy ^ where[1]
        sums = []
        for xr in range(2):
            sums.append([(found[xr][h] + core[xr, yr, 0, h].astype(F32)).astype(LOW) for h in range(2)])

        @pl.when(jnp.logical_not(far))
        def _(sums=sums, yr=yr):
            for half in range(2):
                ka[yr, 0, half] = sums[0][half]
                xa[yr, 0, half] = sums[1][half]

        @pl.when(far & (yr == 0))
        def _(sums=sums):
            for xr in range(2):
                for half in range(2):
                    kb[xr, 0, half] = sums[xr][half]

        @pl.when(far & (yr == 1))
        def _(sums=sums):
            for xr in range(2):
                for half in range(2):
                    yb[xr, 0, half] = sums[xr][half]


def tall_mine(where, acts, cot, core):
    n = cot.shape[1] // 2
    shape = (2, 2, 2, 128, n)
    block = (2, 1, 2, 128, n)
    close = (shape, LOW, block, lambda zr, where: (0, jnp.minimum(zr, 1), 0, 0, 0))
    far = (shape, LOW, block, lambda zr, where: (0, jnp.maximum(zr - 2, 0), 0, 0, 0))
    return call(
        tall_mine_kernel,
        (4,),
        tall_ins(acts, cot, 0) + [((2, 2, 1, 2, 128, n), lambda zr, where: (0, 0, zr, 0, 0, 0))],
        [close, far, close, far],
        prefetch=1,
        pin=(3,),
    )(where, *acts, cot, core)


def row_value(step, lefts, rights, counts, hold):
    first = 0
    for left, right, count in zip(lefts, rights, counts, strict=True):

        def put(left=left, right=right):
            b = right[0] if len(right.shape) == 3 else right[...]
            hold[...] = mm_tn(left[...], b)

        if len(lefts) == 1:
            put()
        else:
            pl.when((step >= first) & (step < first + count))(put)
        first += count


def row_from(where, xr, yr, zr):
    start = ((where[0] ^ zr) * 2 + (where[1] ^ yr)) * 128 + (where[2] ^ xr) * 64
    return pl.ds(pl.multiple_of(start, 64), 64)


def row_away_kernel(counts, where, *refs):
    n = len(counts)
    lefts, rights, away, hold = refs[:n], refs[n : 2 * n], refs[2 * n], refs[2 * n + 1]
    row_value(pl.program_id(0), lefts, rights, counts, hold)
    for xr in range(2):
        for yr in range(2):
            for zr in range(4):
                away[xr, yr, zr] = hold[row_from(where, xr, yr, zr), :].astype(LOW)


def row_mine_kernel(counts, where, *refs):
    n = len(counts)
    lefts, rights = refs[:n], refs[n : 2 * n]
    core, xa, yb, ka, kb, hold = refs[2 * n :]
    row_value(pl.program_id(0), lefts, rights, counts, hold)
    for xr in range(2):
        for yr in range(2):
            for zr in range(4):
                total = hold[row_from(where, xr, yr, zr), :] + core[xr, yr, zr].astype(F32)
                total = total.astype(LOW)
                if zr < 2:
                    (ka if xr == 0 else xa)[yr, zr] = total
                else:
                    (kb if yr == 0 else yb)[xr, zr - 2] = total


def row_specs(pairs, core, tile):
    ins, counts = [], []
    for a, _, _ in pairs:
        ins.append((a.shape, lambda j, where: (0, 0)))
    first = 0
    for _, b, kind in pairs:
        tokens = b.shape[-2]
        if kind == "layers":
            count = b.shape[0] * (b.shape[2] // 2 // tile)
            each = b.shape[2] // 2 // tile
            spec = (
                (1, tokens, tile),
                lambda j, where, f=first, m=count, e=each: (
                    jnp.clip(j - f, 0, m - 1) // e,
                    0,
                    (where[3] ^ core) * e + jnp.clip(j - f, 0, m - 1) % e,
                ),
            )
        elif kind == "layer":
            count = b.shape[2] // tile
            spec = (
                (1, tokens, tile),
                lambda j, where, f=first, m=count: (where[3] ^ core, 0, jnp.clip(j - f, 0, m - 1)),
            )
        else:
            count = b.shape[1] // 2 // tile
            spec = (
                (tokens, tile),
                lambda j, where, f=first, m=count: (0, (where[3] ^ core) * m + jnp.clip(j - f, 0, m - 1)),
            )
        ins.append(spec)
        counts.append(count)
        first += count
    return ins, counts


def row_away(where, pairs, tile=512):
    ins, counts = row_specs(pairs, 1, tile)
    steps = sum(counts)
    return call(
        functools.partial(row_away_kernel, counts),
        (steps,),
        ins,
        [((2, 2, 4, 64, steps * tile), LOW, (2, 2, 4, 64, tile), lambda j, where: (0, 0, 0, 0, j))],
        prefetch=1,
        scratch=[pltpu.VMEM((1024, tile), F32)],
    )(where, *[a for a, _, _ in pairs], *[b for _, b, _ in pairs])[0]


def row_mine(where, pairs, core, tile=512):
    ins, counts = row_specs(pairs, 0, tile)
    steps = sum(counts)
    out = ((2, 2, 64, steps * tile), LOW, (2, 2, 64, tile), lambda j, where: (0, 0, 0, j))
    return call(
        functools.partial(row_mine_kernel, counts),
        (steps,),
        ins + [((2, 2, 4, 64, tile), lambda j, where: (0, 0, 0, 0, j))],
        [out] * 4,
        prefetch=1,
        scratch=[pltpu.VMEM((1024, tile), F32)],
        pin=(2 * len(pairs),),
    )(where, *[a for a, _, _ in pairs], *[b for _, b, _ in pairs], core)


def add_up(jobs, passing=(), cost=0):
    args, pieces = [], []
    parts = [job[1] if isinstance(job[1][0][0], list) else [(job[1], ...)] for job in jobs]

    def number(array, index):
        here = [k for k, a in enumerate(args) if a is array]
        if not here:
            args.append(array)
            here = [len(args) - 1]
        if (here[0], index) not in pieces:
            pieces.append((here[0], index))
        return pieces.index((here[0], index))

    parts = [[([number(*term) for term in terms], write) for terms, write in part] for part in parts]
    shapes = [jax.eval_shape(lambda a, index=index: a[index], args[k]).shape for k, index in pieces]
    n_in, n_out, n_pass = len(args), len(jobs), len(passing)

    def kernel(*refs):
        ins, outs = refs[:n_in], refs[n_in + n_pass : n_in + n_pass + n_out]
        *held, sems = refs[n_in + 2 * n_pass + n_out :]
        copies = []
        for k, (at, index) in enumerate(pieces):
            copies.append(pltpu.make_async_copy(ins[at].at[index], held[k], sems.at[k]))
            copies[-1].start()
        waited = set()
        for out, part in zip(outs, parts, strict=True):
            for terms, write in part:
                total = None
                for k in terms:
                    if k not in waited:
                        copies[k].wait()
                        waited.add(k)
                    value = held[k][...].astype(F32)
                    total = value if total is None else total + value
                out[write] = total.astype(LOW)

    def whole(shape):
        return shape, lambda *_: (0,) * len(shape)

    return call(
        kernel,
        (),
        [("hbm", None)] * n_in + [(None, None)] * n_pass,
        [(job[0], LOW, *whole(job[0])) for job in jobs] + [(a.shape, a.dtype, None, None) for a in passing],
        aliases={n_in + k: n_out + k for k in range(n_pass)},
        scratch=[pltpu.VMEM(shape, LOW) for shape in shapes] + [pltpu.SemaphoreType.DMA((len(pieces),))],
        cost=cost,
        limit=12,
    )(*args, *passing)


class Reduction:
    def __init__(self, ka, kb):
        self.ka, self.kb = ka, kb
        self.tail = ka.shape[2:]

    def go_first(self, xa, yb):
        self.xa, self.yb = swap(xa, "x"), swap(yb, "y")

    def second(self):
        shape = (2, *self.tail)
        return [(shape, [(self.ka, 1), (self.xa, 1)]), (shape, [(self.kb, 1), (self.yb, 1)])]

    def go_second(self, ya, xb):
        self.ya, self.xb = swap(ya, "y"), swap(xb, "x")

    def kept(self, i):
        return self.tail, [(self.ka, (0, i)), (self.xa, (0, i)), (self.ya, i)]

    def sent(self, i):
        return self.tail, [(self.kb, (0, i)), (self.yb, (0, i)), (self.xb, i)]

    def third(self):
        two = [((2, *self.tail), [(self.kb, 0), (self.yb, 0), (self.xb, slice(None))])]
        return two + [self.kept(0), self.kept(1)]

    def go_third(self, far, mine, next_one):
        self.far, self.mine, self.next_one = swap(far, "z2"), mine, next_one

    def fourth(self):
        return [(self.tail, [(self.next_one, slice(None)), (self.far, 1)])]

    def go_fourth(self, near):
        self.near = swap(near, "z1")

    def last(self):
        return [(self.tail, [(self.mine, slice(None)), (self.far, 0), (self.near, slice(None))])]

    def third_direct(self):
        return [self.kept(1), self.sent(0), self.sent(1), self.kept(0)]

    def go_third_direct(self, *blocks):
        self.got = [swap(block, name) for block, name in zip(blocks, ("z1", "z2", "z3"))]
        self.mine = blocks[3]

    def last_direct(self):
        return [(self.tail, [(self.mine, slice(None))] + [(got, slice(None)) for got in self.got])]


def join(first, second):
    (_, terms), = first.last()
    parts = []
    for half in range(2):
        cut = [(array, (0, half) if index == 0 else half) for array, index in terms]
        parts.append((cut, slice(half * 128, half * 128 + 128)))
    (_, terms), = second.last()
    for k in range(4):
        here = (slice(None), slice(k * 512, k * 512 + 512))
        cut = [(array, (0, *here) if index == 0 else here) for array, index in terms]
        parts.append((cut, slice(256 + k * 64, 320 + k * 64)))
    return (512, 512), parts


def pack_last(early, early_x, late):
    whole = slice(None)
    parts = [([(early, whole)], slice(0, 512)), ([(early_x, whole)], slice(512, 1024))]
    for k in range(4):
        here = (slice(None), slice(k * 512, k * 512 + 512))
        parts.append(([(late, here)], slice(1024 + k * 64, 1088 + k * 64)))
    return (1280, 512), parts


def pause_kernel(*_):
    pass


def early_blocks(where, early, early_x, other):
    x, c = where[2], where[3]
    return (
        (early, 0, x, c), (early_x, 0, 1 - x, c), (other, 0, x, 1 - c), (other, 512, 1 - x, 1 - c),
    )


def tall_shard_kernel(where, early, early_x, other, out):
    for block, first, xx, cc in early_blocks(where, early, early_x, other):
        for half in range(2):
            rows = pl.ds(pl.multiple_of(half * 256 + xx * 128, 128), 128)
            out[rows, lanes(cc * 512, 512)] = block[first + half * 128 : first + half * 128 + 128, :].astype(F32)


def up_shard_kernel(where, early, early_x, other, up_out):
    for block, first, xx, cc in early_blocks(where, early, early_x, other):
        rows = pl.ds(pl.multiple_of(xx * 64, 64), 64)
        for s in range(8):
            start = first + 256 + (s // 2) * 64
            value = block[start : start + 64, (s % 2) * 256 : (s % 2) * 256 + 256]
            up_out[rows, lanes(s * 512 + cc * 256, 256)] = value.astype(F32)


def qkv_shard_kernel(where, late, late_x, other, corner, out, out_out):
    x, c = where[2], where[3]
    for block, packed, xx, cc in (
        (late, False, x, c), (late_x, False, 1 - x, c), (other, True, x, 1 - c), (corner, False, 1 - x, 1 - c),
    ):
        rows = pl.ds(pl.multiple_of(xx * 64, 64), 64)
        for k in range(4):
            if packed:
                value = block[1024 + k * 64 : 1088 + k * 64, :]
            else:
                value = block[:, k * 512 : (k + 1) * 512]
            if k < 3:
                out[rows, lanes(k * 1024 + cc * 512, 512)] = value.astype(F32)
            else:
                out_out[rows, lanes(cc * 512, 512)] = value.astype(F32)


def shard_of(kernel, where, blocks, shapes):
    return simple(kernel, blocks, [(s, F32) for s in shapes], where=where, pin_out=range(len(shapes)))


def table_kernel(got, table, vec):
    n = got.shape[0]
    times = lax.broadcasted_iota(jnp.int32, (128, 8), 0).astype(F32)
    total = jnp.zeros(table.shape, F32)
    sums = jnp.zeros(vec.shape, F32)
    for i in range(n):
        hot = (times == got[i, 18:19, 0:8]).astype(F32)
        total += lax.dot_general(hot, got[i, 0:8, :], (((1,), (0,)), ((), ())), precision=lax.Precision.HIGHEST)
        sums += got[i, 8:24, :]
    table[...] = total
    vec[...] = sums


def normalize(values):
    centred = values - jnp.mean(values, axis=-1, keepdims=True)
    spread = jnp.mean(centred * centred, axis=-1, keepdims=True)
    return centred * lax.rsqrt(spread + 1e-05)


def scaled_norm(values, gain):
    return normalize(values) * gain


def exact_gelu(values):
    return jax.nn.gelu(values, approximate=False)


def layer(
    tokens,
    time_index,
    table_all,
    gain_one,
    bias_one,
    qkv_w,
    out_w,
    out_b,
    gain_two,
    bias_two,
    up_w,
    up_b,
    down_w,
    down_b,
    cotangent,
):
    row_count, model_width = tokens.shape
    seq_count = time_index.shape[0]
    length = row_count // seq_count
    head_dim = model_width // HEADS
    factor = head_dim ** (-0.5)
    levels = table_all.shape[0]
    gain_one_f = gain_one.astype(jnp.float32)
    gain_two_f = gain_two.astype(jnp.float32)
    one_hot = time_index[:, None] == jnp.arange(levels, dtype=jnp.int32)[None, :]
    embedding = jnp.dot(one_hot.astype(jnp.bfloat16), table_all, preferred_element_type=jnp.float32)
    scale_seq = (1.0 + embedding)[:, None, :]
    inputs = tokens.astype(jnp.float32)
    normed = (normalize(inputs) * gain_one_f + bias_one.astype(jnp.float32)).reshape(
        seq_count, length, model_width
    )
    scaled = (normed * scale_seq).astype(jnp.bfloat16).reshape(row_count, model_width)
    packed = jnp.dot(scaled, qkv_w, preferred_element_type=jnp.float32).astype(jnp.bfloat16)
    packed = packed.reshape(seq_count, length, 3, HEADS, head_dim)
    queries = packed[:, :, 0]
    key_heads = packed[:, :, 1]
    value_heads = packed[:, :, 2]
    scores = (
        jnp.einsum("sqhd,skhd->shqk", queries, key_heads, preferred_element_type=jnp.float32)
        * factor
    )
    attn_probs = jax.nn.softmax(scores, axis=-1)
    probs_low = attn_probs.astype(jnp.bfloat16)
    attn_mix = jnp.einsum(
        "shqk,skhd->sqhd", probs_low, value_heads, preferred_element_type=jnp.float32
    )
    attn_mix = attn_mix.astype(jnp.bfloat16).reshape(row_count, model_width)
    middle = (
        inputs
        + jnp.dot(attn_mix, out_w, preferred_element_type=jnp.float32)
        + out_b.astype(jnp.float32)
    )
    hidden_in = (normalize(middle) * gain_two_f + bias_two.astype(jnp.float32)).astype(jnp.bfloat16)
    pre_act = jnp.dot(hidden_in, up_w, preferred_element_type=jnp.float32) + up_b.astype(
        jnp.float32
    )
    activated = exact_gelu(pre_act).astype(jnp.bfloat16)
    block_out = (
        middle
        + jnp.dot(activated, down_w, preferred_element_type=jnp.float32)
        + down_b.astype(jnp.float32)
    ).astype(jnp.bfloat16)
    upstream = cotangent.astype(jnp.float32)
    grad_down = jnp.einsum("ti,td->id", activated, cotangent, preferred_element_type=jnp.float32)
    grad_down_b = jnp.sum(upstream, axis=0)
    d_act = jnp.einsum("td,id->ti", cotangent, down_w, preferred_element_type=jnp.float32)
    gelu_pull = jax.vjp(exact_gelu, pre_act)[1]
    d_pre = gelu_pull(d_act)[0].astype(jnp.bfloat16)
    grad_up = jnp.einsum("ti,tf->if", hidden_in, d_pre, preferred_element_type=jnp.float32)
    grad_up_b = jnp.sum(d_pre.astype(jnp.float32), axis=0)
    d_hidden = jnp.einsum("tf,if->ti", d_pre, up_w, preferred_element_type=jnp.float32)
    grad_ln2_bias = jnp.sum(d_hidden, axis=0)
    second_pull = jax.vjp(scaled_norm, middle, gain_two_f)[1]
    d_mid_part, grad_ln2_gain = second_pull(d_hidden)
    d_middle = upstream + d_mid_part
    d_mid_low = d_middle.astype(jnp.bfloat16)
    grad_out_w = jnp.einsum("ti,td->id", attn_mix, d_mid_low, preferred_element_type=jnp.float32)
    grad_out_b = jnp.sum(d_mid_low.astype(jnp.float32), axis=0)
    d_mix = jnp.einsum("td,id->ti", d_mid_low, out_w, preferred_element_type=jnp.float32)
    d_mix = d_mix.astype(jnp.bfloat16).reshape(seq_count, length, HEADS, head_dim)
    d_probs = jnp.einsum("sqhd,skhd->shqk", d_mix, value_heads, preferred_element_type=jnp.float32)
    d_values = jnp.einsum("shqk,sqhd->skhd", probs_low, d_mix, preferred_element_type=jnp.float32)
    d_scores = (
        attn_probs * (d_probs - jnp.sum(d_probs * attn_probs, axis=-1, keepdims=True))
    ).astype(jnp.bfloat16)
    d_queries = (
        jnp.einsum("shqk,skhd->sqhd", d_scores, key_heads, preferred_element_type=jnp.float32)
        * factor
    )
    d_keys = (
        jnp.einsum("shqk,sqhd->skhd", d_scores, queries, preferred_element_type=jnp.float32)
        * factor
    )
    d_packed = (
        jnp.stack([d_queries, d_keys, d_values], axis=2)
        .astype(jnp.bfloat16)
        .reshape(row_count, 3 * model_width)
    )
    grad_qkv = jnp.einsum("ti,tf->if", scaled, d_packed, preferred_element_type=jnp.float32)
    d_scaled = jnp.einsum("tf,if->ti", d_packed, qkv_w, preferred_element_type=jnp.float32).reshape(
        seq_count, length, model_width
    )
    d_normed = d_scaled * scale_seq
    grad_ln1_bias = jnp.sum(d_normed, axis=(0, 1))
    d_embedding = jnp.sum(d_scaled * normed, axis=1)
    grad_table = jnp.einsum(
        "sn,sd->nd", one_hot.astype(jnp.float32), d_embedding, precision=lax.Precision.HIGHEST
    )
    first_pull = jax.vjp(scaled_norm, inputs, gain_one_f)[1]
    d_in_part, grad_ln1_gain = first_pull(d_normed.reshape(row_count, model_width))
    grad_tokens = (d_middle + d_in_part).astype(jnp.bfloat16)
    return (
        block_out,
        grad_tokens,
        (grad_table, grad_ln1_gain, grad_ln1_bias, grad_qkv, grad_out_w, grad_out_b, grad_ln2_gain,
         grad_ln2_bias, grad_up, grad_up_b, grad_down, grad_down_b),
    )


def plain(*args):
    dims = (None, None, 1, 0, 0, 0, 0, 0, 0, 0, 0, 0, 0, 0, None)
    whole = [
        item if dim is None else lax.all_gather(item, "fsdp", axis=dim, tiled=True)
        for item, dim in zip(args, dims, strict=True)
    ]
    block_out, grad_tokens, grads = layer(*whole)
    shares = [
        lax.psum_scatter(grad, "fsdp", scatter_dimension=1 if place == 0 else 0, tiled=True)
        for place, grad in enumerate(grads)
    ]
    return (block_out, grad_tokens, *lax.psum(tuple(shares), "dp"))


def eight_by_four(
    tokens, time_index, time_table, ln1_gain, ln1_bias, w_qkv, w_out, b_out, ln2_gain, ln2_bias,
    w_up, b_up, w_down, b_down, cotangent,
):
    where = jnp.stack(coords()).astype(jnp.int32)
    seqs = time_index.shape[0]
    length = tokens.shape[0] // seqs
    vec = jnp.concatenate(
        [v.reshape(-1, 128) for v in (ln1_gain, ln1_bias, b_out, ln2_gain, ln2_bias, b_down, b_up)]
        + [jnp.zeros((6, 128), LOW)]
    )
    times = time_index.reshape(seqs, 1)
    chain.clear()

    (parts_first,) = (
        simple(own_first_kernel, (w_qkv, w_out), [((2, 128, CW), LOW)], where=where)
    )
    small = jnp.concatenate([time_table, vec])
    small_side = swap(small, "y")
    pieces = [Piece(parts_first, (i,)) for i in range(2)]
    near = swap(parts_first, "z1")
    for piece in pieces:
        piece.move_z1(near, piece.index)

    def tick(*jobs, extra=(), passing=()):
        stages = {
            "z": ("two", "move_z2"), "y": ("four", "move_y"), "x": ("across_send", "move_x"), "c": ("core_send", "move_c"),
        }
        jobs = [(pieces[n], *stages[stage]) for stage, n in jobs]
        made = (move([getattr(p, make)() for p, make, _ in jobs] + list(extra), passing=passing))
        for (p, _, go), value in zip(jobs, made):
            getattr(p, go)(value)
        return made[len(jobs) :]

    extra = [((2, 144, 128), [(small, (), 0), (small_side, (), 1)])]
    (small_two,) = tick(("z", 0), ("z", 1), extra=extra)
    small_near = swap(small_two, "z1")
    (parts_other,) = simple(own_other_kernel, (w_up, w_down), [((4, 128, CW), LOW)], where=where)
    pieces += [Piece(parts_other, (i,), i >= 2) for i in range(4)]
    near_other = swap(parts_other, "z1")
    for i in range(4):
        pieces[2 + i].move_z1(near_other, (i,))
    everything = slice(None)
    owns = [
        [(w_qkv, [(everything, pl.ds(0, 2048))], [0], 2048)],
        [(w_qkv, [(everything, pl.ds(2048, 1024))], [0], 1024), (w_out, [(everything, everything)], [1024], 1024)],
    ]
    for half in range(2):
        reads = [(everything, pl.ds(s * 512 + half * 256, 256)) for s in range(8)]
        owns.append([(w_up, reads, [s * 256 for s in range(8)], 256)])
    for half in range(2):
        reads = [(pl.ds(half * 256 + i * 128, 128), everything) for i in range(2)]
        owns.append([(w_down, reads, [0, 1024], 1024)])

    def whole(n):
        return (assemble(where, pieces[n], owns[n]))

    extra = [((4, 144, 128), [(small_two, (), slice(0, 2)), (small_near, (), slice(2, 4))])]
    (small_four,) = tick(("y", 0), extra=extra)
    small_far = swap(small_four, "z2")
    table, vec, up_b, scale = (small_params(where, small_four, small_far, times))
    tick(("x", 0), ("y", 1), ("z", 2))
    tick(("c", 0), ("x", 1), ("y", 2), ("z", 3))
    gain_one, bias_one, out_b, gain_two, bias_two, down_b = (vec[i : i + 1] for i in range(6))
    scale = scale.reshape(seqs, 1, -1)
    scaled = (first_norm(tokens, gain_one, bias_one, scale))
    w_qk = whole(0)
    tick(("c", 1), ("x", 2), ("y", 3), ("z", 4))
    qk = (project(scaled, w_qk))
    vo = whole(1)
    begun = (attend(scaled, qk, vo, length, 0, 2))
    tick(("c", 2), ("x", 3), ("y", 4), ("z", 5))
    v, probs, mix = (attend(scaled, qk, vo, length, 2, 2, begun))
    middle, hidden = (second_norm(mix, tokens, vo, out_b, gain_two, bias_two))
    up_a = whole(2)
    tick(("c", 3), ("x", 4), ("y", 5))
    act_a, slope_a = (up(hidden, up_a, up_b[0:1]))
    up_b_w = whole(3)
    tick(("c", 4), ("x", 5))
    act_b, slope_b = (up(hidden, up_b_w, up_b[1:2]))
    def step(*jobs, passing=(), cost=0):
        lists = [getattr(r, stage)() for r, stage in jobs]
        made = add_up([item for items in lists for item in items], passing=passing, cost=cost)
        for (r, stage), items in zip(jobs, lists, strict=True):
            values, made = made[: len(items)], made[len(items) :]
            go = "go_last" if stage == "last_direct" else "go_" + stage
            getattr(r, go)(*values)
        return made

    acts = (act_a, act_b)
    downs = [whole(4)]
    away = (tall_away(where, acts, cotangent))
    (away,) = tick(("c", 5), passing=(away,))
    core_one = swap(away, "c")
    d_pre, up_sum_a = (pull(cotangent, downs[0], slope_a, 0))
    downs.append(whole(5))
    xa, yb, *keep = (tall_mine(where, acts, cotangent, core_one))
    one = Reduction(*keep)
    one.go_first(xa, yb)
    d_pre, up_sum_b = (pull(cotangent, downs[1], slope_b, 1, d_pre))
    pairs_two = [(hidden, d_pre, "layer")]
    core_two = swap((row_away(where, pairs_two)), "c")
    d_middle, d_low, d_mix, sums_two = (
        middle_back(d_pre, (up_a, up_b_w), middle, cotangent, gain_two, vo)
    )
    step((one, "second"), cost=42000000000)
    xa, yb, *keep = (row_mine(where, pairs_two, core_two))
    two = Reduction(*keep)
    two.go_first(xa, yb)
    d_packed = (attend_back(d_mix, probs, qk, v, length))
    step((one, "third"), cost=42000000000)
    pairs_three = [(scaled, d_packed, "layers"), (mix, d_low, "columns")]
    core_three = swap(row_away(where, pairs_three), "c")
    step((two, "second"), cost=38000000000)
    *sends, ka, kb = (row_mine(where, pairs_three, core_three))
    three = Reduction(ka, kb)
    three.go_first(*step((two, "third"), passing=sends))
    grad_tokens, sums_one, d_emb = (
        input_back(d_packed, w_qk, vo, tokens, d_middle, gain_one, bias_one, scale)
    )
    block_out = down(acts, downs, middle, down_b, 0, 2)
    step((one, "fourth"))
    simple(pause_kernel, (), [], cost=10000000000)
    step((three, "second"))
    (rows,) = (
        simple(
            rows_kernel,
            (d_emb, sums_one, sums_two, up_sum_a, up_sum_b, jnp.pad(time_index.astype(F32), (0, 120))[None]),
            [((32, 24, 128), F32)],
        )
    )
    got = lax.all_to_all(rows, BOTH, 0, 0)
    block_out = down(acts, downs, middle, down_b, 2, 2, (block_out,))
    step((two, "fourth"), (three, "third_direct"))
    (early,) = add_up([join(one, two)])
    early_x = swap(early, "x")
    grad_table, sums = (
        simple(table_kernel, (got,), [((128, 128), F32), ((16, 128), F32)])
    )
    (late,) = add_up(three.last_direct(), cost=10000000000)
    late_x = swap(late, "x")
    (packed,) = add_up([pack_last(early, early_x, late)])
    other = swap(packed, "c")
    (down_shard,) = shard_of(tall_shard_kernel, where, (early, early_x, other), [(512, 1024)])
    (up_shard,) = shard_of(up_shard_kernel, where, (early, early_x, other), [(128, 4096)])
    (late_x,) = simple(pause_kernel, (), [], passing=(late_x,))
    late_corner = swap(late_x, "c")
    qkv_shard, out_shard = shard_of(
        qkv_shard_kernel, where, (late, late_x, other, late_corner), [(128, 3072), (128, 1024)]
    )
    return (
        block_out, grad_tokens, grad_table, sums[0], sums[1], qkv_shard, out_shard, sums[2], sums[3], sums[4],
        up_shard, sums[6:10].reshape(512), down_shard, sums[5],
    )


def solution(mesh):
    in_specs = (
        P(("fsdp", "dp"), None),
        P(("fsdp", "dp")),
        P(None, "fsdp"),
        P("fsdp"),
        P("fsdp"),
        P("fsdp", None),
        P("fsdp", None),
        P("fsdp"),
        P("fsdp"),
        P("fsdp"),
        P("fsdp", None),
        P("fsdp"),
        P("fsdp", None),
        P("fsdp"),
        P(("fsdp", "dp"), None),
    )
    out_specs = (
        P(("fsdp", "dp"), None),
        P(("fsdp", "dp"), None),
        P(None, "fsdp"),
        P("fsdp"),
        P("fsdp"),
        P("fsdp", None),
        P("fsdp", None),
        P("fsdp"),
        P("fsdp"),
        P("fsdp"),
        P("fsdp", None),
        P("fsdp"),
        P("fsdp", None),
        P("fsdp"),
    )
    local = eight_by_four if (mesh.shape["fsdp"], mesh.shape["dp"]) == (8, 4) else plain
    return jax.shard_map(local, mesh=mesh, in_specs=in_specs, out_specs=out_specs, check_vma=False)
```

```python
import functools

import jax
import jax.numpy as jnp
from jax import lax
from jax.experimental import pallas as pl
from jax.experimental.pallas import tpu as pltpu
from jax.sharding import PartitionSpec as P

HEADS = 16
BOTH = ("fsdp", "dp")
LOW = jnp.bfloat16
F32 = jnp.float32
NT = (((1,), (1,)), ((), ()))
TN = (((0,), (0,)), ((), ()))


def flips(which):
    pairs = []
    for f in range(8):
        for d in range(4):
            z, y, x, c = f // 2, f % 2, d // 2, d % 2
            if which == "x":
                x = 1 - x
            elif which == "y":
                y = 1 - y
            elif which == "c":
                c = 1 - c
            elif which == "z1":
                z = z ^ 1
            elif which == "z2":
                z = z ^ 2
            elif which == "z3":
                z = z ^ 3
            pairs.append((f * 4 + d, (z * 2 + y) * 4 + x * 2 + c))
    return pairs


def swap(values, which):
    return lax.ppermute(values, BOTH, flips(which))


def coords():
    f, d = lax.axis_index("fsdp"), lax.axis_index("dp")
    return f // 2, f % 2, d // 2, d % 2


def call(kernel, grid, ins, outs, flops=0, nbytes=0, scratch=(), prefetch=0, aliases=None, limit=18, pin=(), pin_out=(), cost=0
):
    after = tuple(chain)

    def spec(block, index):
        if block is None:
            return pl.BlockSpec(memory_space=pl.ANY)
        if block == "hbm":
            return pl.BlockSpec(memory_space=pltpu.MemorySpace.HBM)
        if index in constant and grid:
            return pl.BlockSpec(block, index, pipeline_mode=pl.Buffered(1))
        return pl.BlockSpec(block, index)

    def body(*refs):
        n = prefetch + len(ins)
        m = n + len(after) + len(outs)
        kernel(*refs[:n], *refs[n + len(after) : m], *refs[m + 1 :])

    run = pl.pallas_call(
        body,
        out_shape=[
            pltpu.MemorySpace.HBM(shape, kind) if k in pin_out else jax.ShapeDtypeStruct(shape, kind)
            for k, (shape, kind, _, _) in enumerate(outs)
        ]
        + [pltpu.MemorySpace.HBM((8, 128), F32)],
        grid_spec=pltpu.PrefetchScalarGridSpec(
            num_scalar_prefetch=prefetch,
            grid=grid,
            in_specs=[spec(block, index) for block, index in ins] + [spec(None, None)] * len(after),
            out_specs=[spec(block, index) for _, _, block, index in outs] + [spec(None, None)],
            scratch_shapes=scratch,
        ),
        input_output_aliases=aliases or {},
        compiler_params=pltpu.CompilerParams(
            vmem_limit_bytes=limit * 2**20, dimension_semantics=("arbitrary",) * len(grid)
        ),
        cost_estimate=pl.CostEstimate(flops=cost, bytes_accessed=1024, transcendentals=0),
    )

    def pinned(*args):
        args = [
            pltpu.with_memory_space_constraint(a, pltpu.MemorySpace.HBM) if k - prefetch in pin else a
            for k, a in enumerate(args)
        ]
        *values, token = run(*args, *(pltpu.with_memory_space_constraint(t, pltpu.MemorySpace.HBM) for t in after))
        chain[:] = [token]
        return values

    return pinned


def simple(kernel, args, outs, where=None, passing=(), limit=12, pin_out=(), cost=0):
    def whole(shape):
        return shape, lambda *_: (0,) * len(shape)

    prefetch = 0 if where is None else 1
    n_in, n_out, n_pass = len(args), len(outs), len(passing)

    def body(*refs):
        first = prefetch + n_in
        kernel(*refs[:first], *refs[first + n_pass : first + n_pass + n_out])

    run = call(
        body,
        (),
        [whole(a.shape) for a in args] + [(None, None)] * n_pass,
        [(shape, kind, *whole(shape)) for shape, kind in outs] + [(a.shape, a.dtype, None, None) for a in passing],
        prefetch=prefetch,
        aliases={prefetch + n_in + k: n_out + k for k in range(n_pass)},
        limit=limit,
        pin_out=pin_out,
        cost=cost,
    )
    return run(*(() if where is None else (where,)), *args, *passing)


constant = []
chain = []


def fixed(*index):
    constant.append(lambda *grid: index)
    return constant[-1]


def ends(n):
    e = n * 3 // 8
    return e // 2, (n - 2 * e) // 2


def end_start(n, x, c):
    eh, mh = ends(n)
    return x * (n - 2 * eh) + c * eh


def middle_start(n, c):
    eh, mh = ends(n)
    return 2 * eh + c * mh


COLS = 2048
CE, CM = ends(COLS)
CW = CE + CM


def lanes(start, size=128):
    return pl.ds(start if isinstance(start, int) else pl.multiple_of(start, 128), size)


def own_columns(where, dest, read):
    x, c = where[2], where[3]
    for i in range(CW // 128):
        start = end_start(COLS, x, c) + i * 128 if i < CE // 128 else middle_start(COLS, c) + i * 128 - CE
        dest[:, i * 128 : (i + 1) * 128] = read(start)


def own_up(where, up_w, half):
    return lambda start: up_w[:, lanes((start // 256) * 512 + half * 256 + start % 256)]


def own_first_kernel(where, qkv, out_w, up_w, parts):
    own_columns(where, parts.at[0], lambda start: qkv[:, lanes(start)])
    own_columns(
        where,
        parts.at[1],
        lambda start: jnp.where(
            start < 1024, qkv[:, lanes(2048 + jnp.minimum(start, 896))], out_w[:, lanes(jnp.maximum(start - 1024, 0))]
        ),
    )
    own_columns(where, parts.at[2], own_up(where, up_w, 0))


def own_other_kernel(where, up_w, down_w, parts):
    own_columns(where, parts.at[0], own_up(where, up_w, 1))
    for half in range(2):
        own_columns(
            where,
            parts.at[1 + half],
            lambda start: down_w[
                pl.ds(pl.multiple_of(half * 256 + (start // 1024) * 128, 128), 128), lanes(start % 1024)
            ],
        )


def move(jobs, passing=()):
    args = []
    for _, copies in jobs:
        for array, _, _ in copies:
            if not any(array is a for a in args):
                args.append(array)

    def kernel(*refs):
        outs = refs[len(args) :]
        for out, (_, copies) in zip(outs, jobs, strict=True):
            for array, read, write in copies:
                ref = refs[[i for i, a in enumerate(args) if a is array][0]]
                out[write] = ref[read if read != () else ...]

    return simple(kernel, args, [(shape, LOW) for shape, _ in jobs], passing=passing)


class Piece:
    def __init__(self, part, index, tall=False):
        self.part, self.index, self.tall = part, index, tall
        self.shape = (128, CW)
        self.pair = None

    def two(self):
        return (2, *self.shape), [(self.part, self.index, 0), (self.near, self.near_index, 1)]

    def four(self):
        return (4, *self.shape), [
            (self.part, self.index, 0),
            (self.near, self.near_index, 1),
            (self.far, slice(None), slice(2, 4)),
        ]

    def blocks(self):
        found = [(self.near, self.near_index)] + [(self.far, (i,)) for i in range(2)]
        return found + [(self.beside, (i,)) for i in range(4)]

    def across_send(self):
        end = (slice(None), slice(0, CE))
        return (7, 128, CE), [(a, (*i, *end), j) for j, (a, i) in enumerate(self.blocks())]

    def core_send(self):
        first, last = (slice(None), slice(0, CW)), (slice(None), slice(CW, CW + CE))
        copies = [(a, i, (j, *first)) for j, (a, i) in enumerate(self.blocks())]
        return (7, 128, CW + CE), copies + [(self.across, j, (j, *last)) for j in range(7)]

    def move_z1(self, near, near_index):
        self.near, self.near_index = near, near_index

    def move_z2(self, two):
        self.far = swap(two, "z2")

    def move_y(self, four):
        self.beside = swap(four, "y")

    def move_x(self, send):
        self.across = swap(send, "x")

    def move_c(self, send):
        self.other = swap(send, "c")


def assemble_kernel(tall, own_copies, near_index, where, *refs):
    n_own = len(own_copies)
    owns = refs[:n_own]
    near, far, beside, across, other, out, sems = refs[n_own:]
    z, y, x, c = where[0], where[1], where[2], where[3]
    eh, mh = CE, CM

    def at(shard, start, count):
        if not tall:
            return out.at[pl.ds(pl.multiple_of(shard * 128, 128), 128), lanes(start, count)]
        row = shard * 256 + (start // 1024) * 128
        return out.at[pl.ds(pl.multiple_of(row, 128), 128), lanes(start % 1024, count)]

    def cut(block, start, count):
        return block.at[:, pl.ds(start, count)]

    copies = []
    for j in range(8):
        shard = (z ^ (j % 4)) * 2 + (y if j < 4 else 1 - y)
        if j == 0:
            for ref, (read, start, count) in zip(owns, own_copies, strict=True):
                for k in range(len(read)):
                    copies.append((ref.at[read[k]], at(shard, start[k], count)))
            continue
        close = near.at[near_index[0]] if near_index else near
        mine = (close, far.at[0], far.at[1], beside.at[0], beside.at[1], beside.at[2], beside.at[3])[j - 1]
        oc = 1 - c
        copies += [
            (cut(mine, 0, eh), at(shard, end_start(COLS, x, c), eh)),
            (cut(mine, eh, mh), at(shard, middle_start(COLS, c), mh)),
            (cut(across.at[j - 1], 0, eh), at(shard, end_start(COLS, 1 - x, c), eh)),
            (cut(other.at[j - 1], 0, eh), at(shard, end_start(COLS, x, oc), eh)),
            (cut(other.at[j - 1], eh, mh), at(shard, middle_start(COLS, oc), mh)),
            (cut(other.at[j - 1], eh + mh, eh), at(shard, end_start(COLS, 1 - x, oc), eh)),
        ]
    copies = [pltpu.make_async_copy(s, d, sems.at[k]) for k, (s, d) in enumerate(copies)]
    for copy in copies:
        copy.start()
    for copy in copies:
        copy.wait()


def assemble(where, piece, owns):
    shape = (2048, 1024) if piece.tall else (1024, COLS)
    args = [o[0] for o in owns] + [piece.near, piece.far, piece.beside, piece.across, piece.other]
    n_copies = 42 + sum(len(o[1]) for o in owns)
    return call(
        functools.partial(assemble_kernel, piece.tall, [o[1:] for o in owns], piece.near_index),
        (),
        [(None, None)] * len(args),
        [(shape, LOW, shape, lambda *_: (0, 0))],
        prefetch=1,
        scratch=[pltpu.SemaphoreType.DMA((n_copies,))],
        limit=8,
    )(where, *args)[0]


def small_kernel(where, four, beside, time_index, table, vec, up_b, scale):
    z, y = where[0], where[1]
    for j in range(8):
        block = four.at[j] if j < 4 else beside.at[j - 4]
        shard = (z ^ (j // 4 + j // 2 % 2 * 2)) * 2 + (y ^ (j % 2))
        table[:, lanes(shard * 128)] = block[:128, :]
        vec[:, lanes(shard * 128)] = block[128:, :].astype(F32)
        for row in range(4):
            unit = lanes(shard * 256 + (row % 2) * 128)
            up_b[row // 2 : row // 2 + 1, unit] = block[134 + row : 135 + row, :].astype(F32)
    numbers = lax.broadcasted_iota(jnp.int32, (time_index.shape[0], 128), 1)
    one_hot = (numbers == time_index[...]).astype(F32).astype(LOW)
    scale[...] = 1.0 + jnp.dot(one_hot, table[...], preferred_element_type=F32)


def small_params(where, four, beside, time_index):
    return simple(
        small_kernel,
        (four, beside, time_index),
        [((128, 1024), LOW), ((16, 1024), F32), ((2, 2048), F32), ((time_index.shape[0], 1024), F32)],
        where=where,
    )


def rows_kernel(d_emb, sums_one, sums_two, up_a, up_b, times, out):
    for s in range(8):
        here = slice(s * 128, (s + 1) * 128)
        rows = [d_emb[i, :, here] for i in range(8)]
        rows += [sums_one[0:2, here], sums_two[2:3, here], sums_two[0:2, here], sums_two[3:4, here]]
        for sums in (up_a, up_b):
            rows += [sums[:, s * 256 + j * 128 : s * 256 + (j + 1) * 128] for j in range(2)]
        rows += [times[...], jnp.zeros((5, 128), F32)]
        block = jnp.concatenate(rows, axis=0)
        for copy in range(4):
            out[s * 4 + copy] = block


def mm(a, b):
    return jnp.dot(a, b, preferred_element_type=F32)


def mm_nt(a, b):
    return lax.dot_general(a, b, NT, preferred_element_type=F32)


def mm_tn(a, b):
    return lax.dot_general(a, b, TN, preferred_element_type=F32)


def centre(values):
    mean = jnp.mean(values, axis=-1, keepdims=True)
    centred = values - mean
    scale = lax.rsqrt(jnp.mean(centred * centred, axis=-1, keepdims=True) + 1e-05)
    return centred * scale, scale


def first_norm_kernel(tokens, gain, bias, scale, scaled):
    hat, _ = centre(tokens[...].astype(F32))
    scaled[...] = ((hat * gain[...] + bias[...]) * scale[0]).astype(LOW)


def first_norm(tokens, gain, bias, scale):
    rows, width = tokens.shape
    seqs = scale.shape[0]
    length = rows // seqs
    return call(
        first_norm_kernel,
        (seqs,),
        [
            ((length, width), lambda i: (i, 0)),
            ((1, width), fixed(0, 0)),
            ((1, width), fixed(0, 0)),
            ((1, 1, width), lambda i: (i, 0, 0)),
        ],
        [((rows, width), LOW, (length, width), lambda i: (i, 0))],
    )(tokens, gain, bias, scale)[0]


def halves(values):
    lane = lax.broadcasted_iota(jnp.int32, values.shape, 1)
    zero = jnp.zeros_like(values)
    return jnp.concatenate([jnp.where(lane < 64, values, zero), jnp.where(lane < 64, zero, values)], axis=0)


def side(values):
    n = values.shape[0] // 2
    return jnp.concatenate([values[:n], values[n:]], axis=1)


def project_kernel(x, w, out):
    out[...] = mm(x[...], w[...]).astype(LOW)


def project(x, w, tile=512):
    rows, width = x.shape
    n = w.shape[1]
    return call(
        project_kernel,
        (n // tile,),
        [((rows, width), fixed(0, 0)), ((width, tile), lambda i: (0, i))],
        [((rows, n), LOW, (rows, tile), lambda i: (0, i))],
    )(x, w)[0]


def units_of(rows, length, at_once=8):
    units = []
    for seq in range(rows // length):
        for pair in range(2):
            units.append((seq, pair, (slice(seq * length, (seq + 1) * length), slice(pair * 128, (pair + 1) * 128))))
    return [units[i : i + at_once] for i in range(0, len(units), at_once)]


def attend_kernel(length, scaled, wv, q_in, k_in, *refs):
    v_out, probs_out, mix_out = refs[-3:]
    factor = 64 ** (-0.5) * 1.4426950408889634
    v_out[...] = mm(scaled[...], wv[...]).astype(LOW)
    for units in units_of(scaled.shape[0], length):
        scores = [mm_nt(halves(q_in[here]), k_in[here]) for _, _, here in units]
        found = []
        for s in scores:
            e = jnp.exp2((s - jnp.max(s, axis=-1, keepdims=True)) * factor)
            found.append((e * (1.0 / jnp.sum(e, axis=-1, keepdims=True))).astype(LOW))
        for (seq, pair, here), probs in zip(units, found, strict=True):
            probs_out[0, seq, pair] = probs
            mix_out[here] = mm(side(probs), halves(v_out[here])).astype(LOW)


def attend(scaled, qk, vo, length, first=0, count=None, earlier=()):
    rows, width = scaled.shape
    groups = width // 256
    seqs = rows // length
    count = groups if count is None else count
    column = lambda i: (0, first + i)
    wide = ((rows, width), LOW, (rows, 256), column)
    probs = (groups, seqs, 2, 2 * length, length)
    return call(
        functools.partial(attend_kernel, length),
        (count,),
        [
            ((rows, width), fixed(0, 0)),
            ((width, 256), column),
            ((rows, 256), column),
            ((rows, 256), lambda i: (0, groups + first + i)),
        ]
        + [(None, None)] * len(earlier),
        [wide, (probs, LOW, (1, *probs[1:]), lambda i: (first + i, 0, 0, 0, 0)), wide],
        aliases={4 + i: i for i in range(len(earlier))},
    )(scaled, vo, qk, qk, *earlier)


def middle_kernel(mix, tokens, w, out_b, gain, bias, middle_out, hidden_out):
    middle = tokens[...].astype(F32) + mm(mix[...], w[...]) + out_b[...]
    middle_out[...] = middle
    hat, _ = centre(middle)
    hidden_out[...] = (hat * gain[...] + bias[...]).astype(LOW)


def second_norm(mix, tokens, vo, out_b, gain, bias):
    rows, width = tokens.shape
    row = lambda i: (i, 0)
    vec = ((1, width), fixed(0, 0))
    return call(
        middle_kernel,
        (rows // 256,),
        [((256, width), row), ((256, width), row), ((width, width), fixed(0, 1)), vec, vec, vec],
        [((rows, width), F32, (256, width), row), ((rows, width), LOW, (256, width), row)],
    )(mix, tokens, vo, out_b, gain, bias)


def gelu_parts(v):
    cdf = 0.5 + 0.5 * lax.erf(v * 0.5**0.5)
    bell = jnp.exp(-0.5 * v * v)
    return v * cdf, cdf + (v * 0.3989422804014327) * bell


def up_kernel(hidden, w, bias, act, slope):
    value, pull = gelu_parts(mm(hidden[...], w[...]) + bias[...])
    act[...] = value.astype(LOW)
    slope[...] = pull.astype(LOW)


def up(hidden, w, bias, tile=512):
    rows, width = hidden.shape
    n = w.shape[1]
    column = lambda i: (0, i)
    return call(
        up_kernel,
        (n // tile,),
        [((rows, width), fixed(0, 0)), ((width, tile), column), ((1, tile), column)],
        [((rows, n), LOW, (rows, tile), column)] * 2,
        limit=22,
        pin_out=(1,),
    )(hidden, w, bias)


def down_kernel(act_a, act_b, first, second, middle, bias, *refs):
    total = middle[...] + bias[...]
    total += mm(act_a[...], first[...])
    total += mm(act_b[...], second[...])
    refs[-1][...] = total.astype(LOW)


def down(acts, ws, middle, bias, start, count, earlier=(), tile=256):
    rows, width = middle.shape
    k = ws[0].shape[0]
    row = lambda i: (start + i, 0)
    return call(
        down_kernel,
        (count,),
        [((tile, k), row)] * 2
        + [((k, width), fixed(0, 0))] * 2
        + [((tile, width), row), ((1, width), fixed(0, 0))]
        + [(None, None)] * len(earlier),
        [((rows, width), LOW, (tile, width), row)],
        aliases={6 + i: i for i in range(len(earlier))},
        limit=56,
    )(*acts, *ws, middle, bias, *earlier)[0]


def pull_kernel(cot, w, slope, *refs):
    d_pre, sums = refs[-2:]
    value = (mm_nt(cot[...], w[...]) * slope[...].astype(F32)).astype(LOW)
    d_pre[0] = value
    sums[...] = jnp.sum(value.astype(F32), axis=0, keepdims=True)


def pull(cot, w, slope, half, earlier=None, tile=512):
    rows, width = cot.shape
    n = w.shape[0]
    column = lambda i: (0, i)
    ins = [((rows, width), fixed(0, 0)), ((tile, width), lambda i: (i, 0)), ((rows, tile), column)]
    return call(
        pull_kernel,
        (n // tile,),
        ins + ([] if earlier is None else [(None, None)]),
        [((2, rows, n), LOW, (1, rows, tile), lambda i: (half, 0, i)), ((1, n), F32, (1, tile), column)],
        aliases={} if earlier is None else {3: 0},
        pin=(2,),
    )(cot, w, slope, *(() if earlier is None else (earlier,)))


def norm_back(d_out, hat, scale, gain):
    e = d_out * gain
    mean = jnp.mean(e, axis=-1, keepdims=True)
    slant = jnp.mean(e * hat, axis=-1, keepdims=True)
    return (e - mean - hat * slant) * scale


def fold(*rows_of):
    sums = [jnp.sum(v, axis=0, keepdims=True) for v in rows_of]
    return jnp.concatenate(sums + [jnp.zeros_like(sums[0])] * (8 - len(sums)), axis=0)


def middle_back_kernel(d_pre, wa, wb, middle, cot, gain, w_out, d_middle_out, d_low_out, d_mix_out, sums):
    d_hidden = mm_nt(d_pre[0], wa[...]) + mm_nt(d_pre[1], wb[...])
    hat, scale = centre(middle[...])
    d_middle = cot[...].astype(F32) + norm_back(d_hidden, hat, scale, gain[...])
    d_middle_out[...] = d_middle
    d_low = d_middle.astype(LOW)
    d_low_out[...] = d_low
    d_mix_out[...] = mm_nt(d_low, w_out[...]).astype(LOW)

    @pl.when(pl.program_id(0) == 0)
    def _():
        sums[...] = jnp.zeros_like(sums)

    sums[...] += fold(d_hidden * hat, d_hidden, d_low.astype(F32), cot[...].astype(F32))


def middle_back(d_pre, ws, middle, cot, gain, vo, tile=256):
    rows, width = middle.shape
    row = lambda i: (i, 0)
    return call(
        middle_back_kernel,
        (rows // tile,),
        [
            ((2, tile, d_pre.shape[2]), lambda i: (0, i, 0)),
            (ws[0].shape, fixed(0, 0)),
            (ws[1].shape, fixed(0, 0)),
            ((tile, width), row),
            ((tile, width), row),
            ((1, width), fixed(0, 0)),
            ((width, width), fixed(0, 1)),
        ],
        [
            ((rows, width), F32, (tile, width), row),
            ((rows, width), LOW, (tile, width), row),
            ((rows, width), LOW, (tile, width), row),
            ((8, width), F32, (8, width), fixed(0, 0)),
        ],
        limit=32,
    )(d_pre, *ws, middle, cot, gain, vo)


def attend_back_kernel(length, d_mix, probs, q_in, k_in, v_in, *refs):
    out = refs[-1]
    factor = 64 ** (-0.5)
    for units in units_of(d_mix.shape[0], length, 8):
        dms = [halves(d_mix[here]) for _, _, here in units]
        d_probs = [mm_nt(dm, v_in[here]) for dm, (_, _, here) in zip(dms, units, strict=True)]
        found = []
        for d, (seq, pair, _) in zip(d_probs, units, strict=True):
            high = probs[0, seq, pair].astype(F32)
            found.append((high * (d - jnp.sum(d * high, axis=-1, keepdims=True))).astype(LOW))
        for dm, d_scores, (seq, pair, here) in zip(dms, found, units, strict=True):
            out[(2, *here)] = mm_tn(probs[0, seq, pair], dm).astype(LOW)
            out[(0, *here)] = (mm(side(d_scores), halves(k_in[here])) * factor).astype(LOW)
            out[(1, *here)] = (mm_tn(d_scores, halves(q_in[here])) * factor).astype(LOW)


def attend_back(d_mix, probs, qk, v, length, first=0, count=None, earlier=()):
    rows, width = d_mix.shape
    count = width // 256 if count is None else count
    wide = ((rows, 256), lambda i: (0, first + i))
    return call(
        functools.partial(attend_back_kernel, length),
        (count,),
        [
            wide,
            ((1,) + probs.shape[1:], lambda i: (first + i, 0, 0, 0, 0)),
            wide,
            ((rows, 256), lambda i: (0, width // 256 + first + i)),
            wide,
        ]
        + [(None, None)] * len(earlier),
        [((3, rows, width), LOW, (3, rows, 256), lambda i: (0, 0, first + i))],
        aliases={5 + i: i for i in range(len(earlier))},
    )(d_mix, probs, qk, qk, v, *earlier)[0]


def input_back_kernel(length, d, wq, wk, wv, tokens, d_middle, gain, bias, scale, out, sums, d_emb):
    d_scaled = mm_nt(d[0], wq[...]) + mm_nt(d[1], wk[...]) + mm_nt(d[2], wv[...])
    hat, spread = centre(tokens[...].astype(F32))
    normed = hat * gain[...] + bias[...]
    count = tokens.shape[0] // length
    parts = []
    for i in range(count):
        here = slice(i * length, (i + 1) * length)
        d_emb[i] = jnp.sum(d_scaled[here] * normed[here], axis=0, keepdims=True)
        parts.append(d_scaled[here] * scale[i])
    d_normed = jnp.concatenate(parts, axis=0)
    out[...] = (d_middle[...] + norm_back(d_normed, hat, spread, gain[...])).astype(LOW)

    @pl.when(pl.program_id(0) == 0)
    def _():
        sums[...] = jnp.zeros_like(sums)

    sums[...] += fold(d_normed * hat, d_normed)


def input_back(d_packed, qk, vo, tokens, d_middle, gain, bias, scale, tile=256, cost=0):
    rows, width = tokens.shape
    seqs = scale.shape[0]
    length = rows // seqs
    row = lambda i: (i, 0)
    wide = ((tile, width), row)
    vec = ((1, width), fixed(0, 0))
    some = ((tile // length, 1, width), lambda i: (i, 0, 0))
    return call(
        functools.partial(input_back_kernel, length),
        (rows // tile,),
        [
            ((3, tile, width), lambda i: (0, i, 0)),
            ((width, width), fixed(0, 0)),
            ((width, width), fixed(0, 1)),
            ((width, width), fixed(0, 0)),
            wide, wide, vec, vec, some,
        ],
        [
            ((rows, width), LOW, (tile, width), row),
            ((8, width), F32, (8, width), fixed(0, 0)),
            ((seqs, 1, width), F32) + some,
        ],
        cost=cost,
        limit=26,
    )(d_packed, qk, qk, vo, tokens, d_middle, gain, bias, scale)


def tall_parts(where, a, b, cot, yy):
    here = slice(yy * 256, (yy + 1) * 256)
    value = mm_tn(jnp.concatenate([a[:, here], b[:, here]], axis=1), cot[...])
    x = where[2]
    found = []
    for xr in range(2):
        pair = []
        for half in range(2):
            low, high = value[half * 256 : half * 256 + 128], value[half * 256 + 128 : half * 256 + 256]
            pair.append(jnp.where((x ^ xr) == 0, low, high))
        found.append(pair)
    return found


def tall_away_kernel(where, a, b, cot, away):
    for yy in range(2):
        found = tall_parts(where, a, b, cot, yy)
        for xr in range(2):
            for half in range(2):
                away[xr, yy ^ where[1], 0, half] = found[xr][half].astype(LOW)


def tall_ins(acts, cot, core):
    rows, width = cot.shape
    act = ((rows, 512), lambda zr, where: (0, zr ^ where[0]))
    return [act, act, ((rows, width // 2), lambda zr, where: (0, where[3] ^ core))]


def tall_away(where, acts, cot):
    n = cot.shape[1] // 2
    return call(
        tall_away_kernel,
        (4,),
        tall_ins(acts, cot, 1),
        [((2, 2, 4, 2, 128, n), LOW, (2, 2, 1, 2, 128, n), lambda zr, where: (0, 0, zr, 0, 0, 0))],
        prefetch=1,
    )(where, *acts, cot)[0]


def tall_mine_kernel(where, a, b, cot, core, xa, yb, ka, kb):
    far = pl.program_id(0) >= 2
    for yy in range(2):
        found = tall_parts(where, a, b, cot, yy)
        yr = yy ^ where[1]
        sums = []
        for xr in range(2):
            sums.append([(found[xr][h] + core[xr, yr, 0, h].astype(F32)).astype(LOW) for h in range(2)])

        @pl.when(jnp.logical_not(far))
        def _(sums=sums, yr=yr):
            for half in range(2):
                ka[yr, 0, half] = sums[0][half]
                xa[yr, 0, half] = sums[1][half]

        @pl.when(far & (yr == 0))
        def _(sums=sums):
            for xr in range(2):
                for half in range(2):
                    kb[xr, 0, half] = sums[xr][half]

        @pl.when(far & (yr == 1))
        def _(sums=sums):
            for xr in range(2):
                for half in range(2):
                    yb[xr, 0, half] = sums[xr][half]


def tall_mine(where, acts, cot, core):
    n = cot.shape[1] // 2
    shape = (2, 2, 2, 128, n)
    block = (2, 1, 2, 128, n)
    close = (shape, LOW, block, lambda zr, where: (0, jnp.minimum(zr, 1), 0, 0, 0))
    far = (shape, LOW, block, lambda zr, where: (0, jnp.maximum(zr - 2, 0), 0, 0, 0))
    return call(
        tall_mine_kernel,
        (4,),
        tall_ins(acts, cot, 0) + [((2, 2, 1, 2, 128, n), lambda zr, where: (0, 0, zr, 0, 0, 0))],
        [close, far, close, far],
        prefetch=1,
        pin=(3,),
    )(where, *acts, cot, core)


def row_value(step, lefts, rights, counts, hold):
    first = 0
    for left, right, count in zip(lefts, rights, counts, strict=True):

        def put(left=left, right=right):
            b = right[0] if len(right.shape) == 3 else right[...]
            hold[...] = mm_tn(left[...], b)

        if len(lefts) == 1:
            put()
        else:
            pl.when((step >= first) & (step < first + count))(put)
        first += count


def row_from(where, xr, yr, zr):
    start = ((where[0] ^ zr) * 2 + (where[1] ^ yr)) * 128 + (where[2] ^ xr) * 64
    return pl.ds(pl.multiple_of(start, 64), 64)


def row_away_kernel(counts, where, *refs):
    n = len(counts)
    lefts, rights, away, hold = refs[:n], refs[n : 2 * n], refs[2 * n], refs[2 * n + 1]
    row_value(pl.program_id(0), lefts, rights, counts, hold)
    for xr in range(2):
        for yr in range(2):
            for zr in range(4):
                away[xr, yr, zr] = hold[row_from(where, xr, yr, zr), :].astype(LOW)


def row_mine_kernel(counts, where, *refs):
    n = len(counts)
    lefts, rights = refs[:n], refs[n : 2 * n]
    core, xa, yb, ka, kb, hold = refs[2 * n :]
    row_value(pl.program_id(0), lefts, rights, counts, hold)
    for xr in range(2):
        for yr in range(2):
            for zr in range(4):
                total = hold[row_from(where, xr, yr, zr), :] + core[xr, yr, zr].astype(F32)
                total = total.astype(LOW)
                if zr < 2:
                    (ka if xr == 0 else xa)[yr, zr] = total
                else:
                    (kb if yr == 0 else yb)[xr, zr - 2] = total


def row_specs(pairs, core, tile):
    ins, counts = [], []
    for a, _, _ in pairs:
        ins.append((a.shape, lambda j, where: (0, 0)))
    first = 0
    for _, b, kind in pairs:
        tokens = b.shape[-2]
        if kind == "layers":
            count = b.shape[0] * (b.shape[2] // 2 // tile)
            each = b.shape[2] // 2 // tile
            spec = (
                (1, tokens, tile),
                lambda j, where, f=first, m=count, e=each: (
                    jnp.clip(j - f, 0, m - 1) // e,
                    0,
                    (where[3] ^ core) * e + jnp.clip(j - f, 0, m - 1) % e,
                ),
            )
        elif kind == "layer":
            count = b.shape[2] // tile
            spec = (
                (1, tokens, tile),
                lambda j, where, f=first, m=count: (where[3] ^ core, 0, jnp.clip(j - f, 0, m - 1)),
            )
        else:
            count = b.shape[1] // 2 // tile
            spec = (
                (tokens, tile),
                lambda j, where, f=first, m=count: (0, (where[3] ^ core) * m + jnp.clip(j - f, 0, m - 1)),
            )
        ins.append(spec)
        counts.append(count)
        first += count
    return ins, counts


def row_away(where, pairs, tile=512):
    ins, counts = row_specs(pairs, 1, tile)
    steps = sum(counts)
    return call(
        functools.partial(row_away_kernel, counts),
        (steps,),
        ins,
        [((2, 2, 4, 64, steps * tile), LOW, (2, 2, 4, 64, tile), lambda j, where: (0, 0, 0, 0, j))],
        prefetch=1,
        scratch=[pltpu.VMEM((1024, tile), F32)],
    )(where, *[a for a, _, _ in pairs], *[b for _, b, _ in pairs])[0]


def row_mine(where, pairs, core, tile=512):
    ins, counts = row_specs(pairs, 0, tile)
    steps = sum(counts)
    out = ((2, 2, 64, steps * tile), LOW, (2, 2, 64, tile), lambda j, where: (0, 0, 0, j))
    return call(
        functools.partial(row_mine_kernel, counts),
        (steps,),
        ins + [((2, 2, 4, 64, tile), lambda j, where: (0, 0, 0, 0, j))],
        [out] * 4,
        prefetch=1,
        scratch=[pltpu.VMEM((1024, tile), F32)],
        pin=(2 * len(pairs),),
    )(where, *[a for a, _, _ in pairs], *[b for _, b, _ in pairs], core)


def add_up(jobs, passing=(), cost=0):
    args, pieces = [], []
    parts = [job[1] if isinstance(job[1][0][0], list) else [(job[1], ...)] for job in jobs]

    def number(array, index):
        here = [k for k, a in enumerate(args) if a is array]
        if not here:
            args.append(array)
            here = [len(args) - 1]
        if (here[0], index) not in pieces:
            pieces.append((here[0], index))
        return pieces.index((here[0], index))

    parts = [[([number(*term) for term in terms], write) for terms, write in part] for part in parts]
    shapes = [jax.eval_shape(lambda a, index=index: a[index], args[k]).shape for k, index in pieces]
    n_in, n_out, n_pass = len(args), len(jobs), len(passing)

    def kernel(*refs):
        ins, outs = refs[:n_in], refs[n_in + n_pass : n_in + n_pass + n_out]
        *held, sems = refs[n_in + 2 * n_pass + n_out :]
        copies = []
        for k, (at, index) in enumerate(pieces):
            copies.append(pltpu.make_async_copy(ins[at].at[index], held[k], sems.at[k]))
            copies[-1].start()
        waited = set()
        for out, part in zip(outs, parts, strict=True):
            for terms, write in part:
                total = None
                for k in terms:
                    if k not in waited:
                        copies[k].wait()
                        waited.add(k)
                    value = held[k][...].astype(F32)
                    total = value if total is None else total + value
                out[write] = total.astype(LOW)

    def whole(shape):
        return shape, lambda *_: (0,) * len(shape)

    return call(
        kernel,
        (),
        [("hbm", None)] * n_in + [(None, None)] * n_pass,
        [(job[0], LOW, *whole(job[0])) for job in jobs] + [(a.shape, a.dtype, None, None) for a in passing],
        aliases={n_in + k: n_out + k for k in range(n_pass)},
        scratch=[pltpu.VMEM(shape, LOW) for shape in shapes] + [pltpu.SemaphoreType.DMA((len(pieces),))],
        cost=cost,
        limit=12,
    )(*args, *passing)


class Reduction:
    def __init__(self, ka, kb):
        self.ka, self.kb = ka, kb
        self.tail = ka.shape[2:]

    def go_first(self, xa, yb):
        self.xa, self.yb = swap(xa, "x"), swap(yb, "y")

    def second(self):
        shape = (2, *self.tail)
        return [(shape, [(self.ka, 1), (self.xa, 1)]), (shape, [(self.kb, 1), (self.yb, 1)])]

    def go_second(self, ya, xb):
        self.ya, self.xb = swap(ya, "y"), swap(xb, "x")

    def kept(self, i):
        return self.tail, [(self.ka, (0, i)), (self.xa, (0, i)), (self.ya, i)]

    def sent(self, i):
        return self.tail, [(self.kb, (0, i)), (self.yb, (0, i)), (self.xb, i)]

    def third(self):
        two = [((2, *self.tail), [(self.kb, 0), (self.yb, 0), (self.xb, slice(None))])]
        return two + [self.kept(0), self.kept(1)]

    def go_third(self, far, mine, next_one):
        self.far, self.mine, self.next_one = swap(far, "z2"), mine, next_one

    def fourth(self):
        return [(self.tail, [(self.next_one, slice(None)), (self.far, 1)])]

    def go_fourth(self, near):
        self.near = swap(near, "z1")

    def last(self):
        return [(self.tail, [(self.mine, slice(None)), (self.far, 0), (self.near, slice(None))])]

    def third_direct(self):
        return [self.kept(1), self.sent(0), self.sent(1), self.kept(0)]

    def go_third_direct(self, *blocks):
        self.got = [swap(block, name) for block, name in zip(blocks, ("z1", "z2", "z3"))]
        self.mine = blocks[3]

    def last_direct(self):
        return [(self.tail, [(self.mine, slice(None))] + [(got, slice(None)) for got in self.got])]


def join(first, second):
    (_, terms), = first.last()
    parts = []
    for half in range(2):
        cut = [(array, (0, half) if index == 0 else half) for array, index in terms]
        parts.append((cut, slice(half * 128, half * 128 + 128)))
    (_, terms), = second.last()
    for k in range(4):
        here = (slice(None), slice(k * 512, k * 512 + 512))
        cut = [(array, (0, *here) if index == 0 else here) for array, index in terms]
        parts.append((cut, slice(256 + k * 64, 320 + k * 64)))
    return (512, 512), parts


def pack_last(early, early_x, late):
    whole = slice(None)
    parts = [([(early, whole)], slice(0, 512)), ([(early_x, whole)], slice(512, 1024))]
    for k in range(4):
        here = (slice(None), slice(k * 512, k * 512 + 512))
        parts.append(([(late, here)], slice(1024 + k * 64, 1088 + k * 64)))
    return (1280, 512), parts


def pause_kernel(*_):
    pass


def early_blocks(where, early, early_x, other):
    x, c = where[2], where[3]
    return (
        (early, 0, x, c), (early_x, 0, 1 - x, c), (other, 0, x, 1 - c), (other, 512, 1 - x, 1 - c),
    )


def tall_shard_kernel(where, early, early_x, other, out):
    for block, first, xx, cc in early_blocks(where, early, early_x, other):
        for half in range(2):
            rows = pl.ds(pl.multiple_of(half * 256 + xx * 128, 128), 128)
            out[rows, lanes(cc * 512, 512)] = block[first + half * 128 : first + half * 128 + 128, :].astype(F32)


def up_shard_kernel(where, early, early_x, other, up_out):
    for block, first, xx, cc in early_blocks(where, early, early_x, other):
        rows = pl.ds(pl.multiple_of(xx * 64, 64), 64)
        for s in range(8):
            start = first + 256 + (s // 2) * 64
            value = block[start : start + 64, (s % 2) * 256 : (s % 2) * 256 + 256]
            up_out[rows, lanes(s * 512 + cc * 256, 256)] = value.astype(F32)


def qkv_shard_kernel(where, late, late_x, other, corner, out, out_out):
    x, c = where[2], where[3]
    for block, packed, xx, cc in (
        (late, False, x, c), (late_x, False, 1 - x, c), (other, True, x, 1 - c), (corner, False, 1 - x, 1 - c),
    ):
        rows = pl.ds(pl.multiple_of(xx * 64, 64), 64)
        for k in range(4):
            if packed:
                value = block[1024 + k * 64 : 1088 + k * 64, :]
            else:
                value = block[:, k * 512 : (k + 1) * 512]
            if k < 3:
                out[rows, lanes(k * 1024 + cc * 512, 512)] = value.astype(F32)
            else:
                out_out[rows, lanes(cc * 512, 512)] = value.astype(F32)


def shard_of(kernel, where, blocks, shapes):
    return simple(kernel, blocks, [(s, F32) for s in shapes], where=where, pin_out=range(len(shapes)))


def table_kernel(got, table, vec):
    n = got.shape[0]
    times = lax.broadcasted_iota(jnp.int32, (128, 8), 0).astype(F32)
    total = jnp.zeros(table.shape, F32)
    sums = jnp.zeros(vec.shape, F32)
    for i in range(n):
        hot = (times == got[i, 18:19, 0:8]).astype(F32)
        total += lax.dot_general(hot, got[i, 0:8, :], (((1,), (0,)), ((), ())), precision=lax.Precision.HIGHEST)
        sums += got[i, 8:24, :]
    table[...] = total
    vec[...] = sums


def normalize(values):
    centred = values - jnp.mean(values, axis=-1, keepdims=True)
    spread = jnp.mean(centred * centred, axis=-1, keepdims=True)
    return centred * lax.rsqrt(spread + 1e-05)


def scaled_norm(values, gain):
    return normalize(values) * gain


def exact_gelu(values):
    return jax.nn.gelu(values, approximate=False)


def layer(
    tokens,
    time_index,
    table_all,
    gain_one,
    bias_one,
    qkv_w,
    out_w,
    out_b,
    gain_two,
    bias_two,
    up_w,
    up_b,
    down_w,
    down_b,
    cotangent,
):
    row_count, model_width = tokens.shape
    seq_count = time_index.shape[0]
    length = row_count // seq_count
    head_dim = model_width // HEADS
    factor = head_dim ** (-0.5)
    levels = table_all.shape[0]
    gain_one_f = gain_one.astype(jnp.float32)
    gain_two_f = gain_two.astype(jnp.float32)
    one_hot = time_index[:, None] == jnp.arange(levels, dtype=jnp.int32)[None, :]
    embedding = jnp.dot(one_hot.astype(jnp.bfloat16), table_all, preferred_element_type=jnp.float32)
    scale_seq = (1.0 + embedding)[:, None, :]
    inputs = tokens.astype(jnp.float32)
    normed = (normalize(inputs) * gain_one_f + bias_one.astype(jnp.float32)).reshape(
        seq_count, length, model_width
    )
    scaled = (normed * scale_seq).astype(jnp.bfloat16).reshape(row_count, model_width)
    packed = jnp.dot(scaled, qkv_w, preferred_element_type=jnp.float32).astype(jnp.bfloat16)
    packed = packed.reshape(seq_count, length, 3, HEADS, head_dim)
    queries = packed[:, :, 0]
    key_heads = packed[:, :, 1]
    value_heads = packed[:, :, 2]
    scores = (
        jnp.einsum("sqhd,skhd->shqk", queries, key_heads, preferred_element_type=jnp.float32)
        * factor
    )
    attn_probs = jax.nn.softmax(scores, axis=-1)
    probs_low = attn_probs.astype(jnp.bfloat16)
    attn_mix = jnp.einsum(
        "shqk,skhd->sqhd", probs_low, value_heads, preferred_element_type=jnp.float32
    )
    attn_mix = attn_mix.astype(jnp.bfloat16).reshape(row_count, model_width)
    middle = (
        inputs
        + jnp.dot(attn_mix, out_w, preferred_element_type=jnp.float32)
        + out_b.astype(jnp.float32)
    )
    hidden_in = (normalize(middle) * gain_two_f + bias_two.astype(jnp.float32)).astype(jnp.bfloat16)
    pre_act = jnp.dot(hidden_in, up_w, preferred_element_type=jnp.float32) + up_b.astype(
        jnp.float32
    )
    activated = exact_gelu(pre_act).astype(jnp.bfloat16)
    block_out = (
        middle
        + jnp.dot(activated, down_w, preferred_element_type=jnp.float32)
        + down_b.astype(jnp.float32)
    ).astype(jnp.bfloat16)
    upstream = cotangent.astype(jnp.float32)
    grad_down = jnp.einsum("ti,td->id", activated, cotangent, preferred_element_type=jnp.float32)
    grad_down_b = jnp.sum(upstream, axis=0)
    d_act = jnp.einsum("td,id->ti", cotangent, down_w, preferred_element_type=jnp.float32)
    gelu_pull = jax.vjp(exact_gelu, pre_act)[1]
    d_pre = gelu_pull(d_act)[0].astype(jnp.bfloat16)
    grad_up = jnp.einsum("ti,tf->if", hidden_in, d_pre, preferred_element_type=jnp.float32)
    grad_up_b = jnp.sum(d_pre.astype(jnp.float32), axis=0)
    d_hidden = jnp.einsum("tf,if->ti", d_pre, up_w, preferred_element_type=jnp.float32)
    grad_ln2_bias = jnp.sum(d_hidden, axis=0)
    second_pull = jax.vjp(scaled_norm, middle, gain_two_f)[1]
    d_mid_part, grad_ln2_gain = second_pull(d_hidden)
    d_middle = upstream + d_mid_part
    d_mid_low = d_middle.astype(jnp.bfloat16)
    grad_out_w = jnp.einsum("ti,td->id", attn_mix, d_mid_low, preferred_element_type=jnp.float32)
    grad_out_b = jnp.sum(d_mid_low.astype(jnp.float32), axis=0)
    d_mix = jnp.einsum("td,id->ti", d_mid_low, out_w, preferred_element_type=jnp.float32)
    d_mix = d_mix.astype(jnp.bfloat16).reshape(seq_count, length, HEADS, head_dim)
    d_probs = jnp.einsum("sqhd,skhd->shqk", d_mix, value_heads, preferred_element_type=jnp.float32)
    d_values = jnp.einsum("shqk,sqhd->skhd", probs_low, d_mix, preferred_element_type=jnp.float32)
    d_scores = (
        attn_probs * (d_probs - jnp.sum(d_probs * attn_probs, axis=-1, keepdims=True))
    ).astype(jnp.bfloat16)
    d_queries = (
        jnp.einsum("shqk,skhd->sqhd", d_scores, key_heads, preferred_element_type=jnp.float32)
        * factor
    )
    d_keys = (
        jnp.einsum("shqk,sqhd->skhd", d_scores, queries, preferred_element_type=jnp.float32)
        * factor
    )
    d_packed = (
        jnp.stack([d_queries, d_keys, d_values], axis=2)
        .astype(jnp.bfloat16)
        .reshape(row_count, 3 * model_width)
    )
    grad_qkv = jnp.einsum("ti,tf->if", scaled, d_packed, preferred_element_type=jnp.float32)
    d_scaled = jnp.einsum("tf,if->ti", d_packed, qkv_w, preferred_element_type=jnp.float32).reshape(
        seq_count, length, model_width
    )
    d_normed = d_scaled * scale_seq
    grad_ln1_bias = jnp.sum(d_normed, axis=(0, 1))
    d_embedding = jnp.sum(d_scaled * normed, axis=1)
    grad_table = jnp.einsum(
        "sn,sd->nd", one_hot.astype(jnp.float32), d_embedding, precision=lax.Precision.HIGHEST
    )
    first_pull = jax.vjp(scaled_norm, inputs, gain_one_f)[1]
    d_in_part, grad_ln1_gain = first_pull(d_normed.reshape(row_count, model_width))
    grad_tokens = (d_middle + d_in_part).astype(jnp.bfloat16)
    return (
        block_out,
        grad_tokens,
        (grad_table, grad_ln1_gain, grad_ln1_bias, grad_qkv, grad_out_w, grad_out_b, grad_ln2_gain,
         grad_ln2_bias, grad_up, grad_up_b, grad_down, grad_down_b),
    )


def plain(*args):
    dims = (None, None, 1, 0, 0, 0, 0, 0, 0, 0, 0, 0, 0, 0, None)
    whole = [
        item if dim is None else lax.all_gather(item, "fsdp", axis=dim, tiled=True)
        for item, dim in zip(args, dims, strict=True)
    ]
    block_out, grad_tokens, grads = layer(*whole)
    shares = [
        lax.psum_scatter(grad, "fsdp", scatter_dimension=1 if place == 0 else 0, tiled=True)
        for place, grad in enumerate(grads)
    ]
    return (block_out, grad_tokens, *lax.psum(tuple(shares), "dp"))


def eight_by_four(
    tokens, time_index, time_table, ln1_gain, ln1_bias, w_qkv, w_out, b_out, ln2_gain, ln2_bias,
    w_up, b_up, w_down, b_down, cotangent,
):
    where = jnp.stack(coords()).astype(jnp.int32)
    seqs = time_index.shape[0]
    length = tokens.shape[0] // seqs
    vec = jnp.concatenate(
        [v.reshape(-1, 128) for v in (ln1_gain, ln1_bias, b_out, ln2_gain, ln2_bias, b_down, b_up)]
        + [jnp.zeros((6, 128), LOW)]
    )
    times = time_index.reshape(seqs, 1)
    chain.clear()

    (parts_first,) = simple(own_first_kernel, (w_qkv, w_out, w_up), [((3, 128, CW), LOW)], where=where)
    small = jnp.concatenate([time_table, vec])
    small_side = swap(small, "y")
    (small_two,) = move([((2, 144, 128), [(small, (), 0), (small_side, (), 1)])])
    small_far = swap(small_two, "z2")
    pieces = [Piece(parts_first, (i,)) for i in range(3)]
    near = swap(parts_first, "z1")
    for piece in pieces:
        piece.move_z1(near, piece.index)

    def tick(*jobs, extra=(), passing=()):
        stages = {
            "z": ("two", "move_z2"), "y": ("four", "move_y"), "x": ("across_send", "move_x"), "c": ("core_send", "move_c"),
        }
        ready = [pieces[n] for stage, n in jobs if stage == "z" and pieces[n].pair is not None]
        jobs = [(pieces[n], *stages[stage]) for stage, n in jobs if stage != "z" or pieces[n].pair is None]
        made = move([getattr(p, make)() for p, make, _ in jobs] + list(extra), passing=passing)
        for (p, _, go), value in zip(jobs, made):
            getattr(p, go)(value)
        for p in ready:
            p.move_z2(p.pair)
        return made[len(jobs) :]

    tick(("z", 0), ("z", 1))
    (small_four,) = move([((4, 144, 128), [(small_two, (), slice(0, 2)), (small_far, (), slice(2, 4))])])
    small_near = swap(small_four, "z1")
    table, vec, up_b, scale = small_params(where, small_four, small_near, times)
    gain_one, bias_one, out_b, gain_two, bias_two, down_b = (vec[i : i + 1] for i in range(6))
    scale = scale.reshape(seqs, 1, -1)
    scaled = first_norm(tokens, gain_one, bias_one, scale)
    everything = slice(None)
    owns = [
        [(w_qkv, [(everything, pl.ds(0, 2048))], [0], 2048)],
        [(w_qkv, [(everything, pl.ds(2048, 1024))], [0], 1024), (w_out, [(everything, everything)], [1024], 1024)],
    ]
    for half in range(2):
        reads = [(everything, pl.ds(s * 512 + half * 256, 256)) for s in range(8)]
        owns.append([(w_up, reads, [s * 256 for s in range(8)], 256)])
    for half in range(2):
        reads = [(pl.ds(half * 256 + i * 128, 128), everything) for i in range(2)]
        owns.append([(w_down, reads, [0, 1024], 1024)])

    def whole(n):
        return (assemble(where, pieces[n], owns[n]))

    tick(("y", 0))
    (parts_other,) = simple(own_other_kernel, (w_up, w_down), [((3, 128, CW), LOW)], where=where)
    pieces += [Piece(parts_other, (i,), i >= 1) for i in range(3)]
    near_other = swap(parts_other, "z1")
    for i in range(3):
        pieces[3 + i].move_z1(near_other, (i,))
    pairs = tick(("x", 0), ("y", 1), ("z", 2), extra=[pieces[i].two() for i in range(3, 6)])
    for i in range(3):
        pieces[3 + i].pair = pairs[i]
    tick(("c", 0), ("x", 1), ("y", 2), ("z", 3))
    w_qk = whole(0)
    tick(("c", 1), ("x", 2), ("y", 3), ("z", 4))
    qk = (project(scaled, w_qk))
    vo = whole(1)
    begun = (attend(scaled, qk, vo, length, 0, 2))
    tick(("c", 2), ("x", 3), ("y", 4), ("z", 5))
    v, probs, mix = (attend(scaled, qk, vo, length, 2, 2, begun))
    middle, hidden = (second_norm(mix, tokens, vo, out_b, gain_two, bias_two))
    up_a = whole(2)
    tick(("c", 3), ("x", 4), ("y", 5))
    act_a, slope_a = (up(hidden, up_a, up_b[0:1]))
    up_b_w = whole(3)
    tick(("c", 4), ("x", 5))
    act_b, slope_b = (up(hidden, up_b_w, up_b[1:2]))
    def step(*jobs, passing=(), cost=0):
        lists = [getattr(r, stage)() for r, stage in jobs]
        made = add_up([item for items in lists for item in items], passing=passing, cost=cost)
        for (r, stage), items in zip(jobs, lists, strict=True):
            values, made = made[: len(items)], made[len(items) :]
            go = "go_last" if stage == "last_direct" else "go_" + stage
            getattr(r, go)(*values)
        return made

    acts = (act_a, act_b)
    downs = [whole(4)]
    away = (tall_away(where, acts, cotangent))
    (away,) = tick(("c", 5), passing=(away,))
    core_one = swap(away, "c")
    d_pre, up_sum_a = (pull(cotangent, downs[0], slope_a, 0))
    downs.append(whole(5))
    xa, yb, *keep = (tall_mine(where, acts, cotangent, core_one))
    one = Reduction(*keep)
    one.go_first(xa, yb)
    d_pre, up_sum_b = (pull(cotangent, downs[1], slope_b, 1, d_pre))
    pairs_two = [(hidden, d_pre, "layer")]
    core_two = swap((row_away(where, pairs_two)), "c")
    d_middle, d_low, d_mix, sums_two = (
        middle_back(d_pre, (up_a, up_b_w), middle, cotangent, gain_two, vo)
    )
    step((one, "second"), cost=42000000000)
    xa, yb, *keep = (row_mine(where, pairs_two, core_two))
    two = Reduction(*keep)
    two.go_first(xa, yb)
    d_packed = (attend_back(d_mix, probs, qk, v, length))
    step((one, "third"), cost=42000000000)
    pairs_three = [(scaled, d_packed, "layers"), (mix, d_low, "columns")]
    core_three = swap(row_away(where, pairs_three), "c")
    step((two, "second"), cost=38000000000)
    *sends, ka, kb = (row_mine(where, pairs_three, core_three))
    three = Reduction(ka, kb)
    three.go_first(*step((two, "third"), passing=sends))
    grad_tokens, sums_one, d_emb = (
        input_back(d_packed, w_qk, vo, tokens, d_middle, gain_one, bias_one, scale)
    )
    block_out = down(acts, downs, middle, down_b, 0, 2)
    step((one, "fourth"))
    simple(pause_kernel, (), [], cost=10000000000)
    step((three, "second"))
    (rows,) = (
        simple(
            rows_kernel,
            (d_emb, sums_one, sums_two, up_sum_a, up_sum_b, jnp.pad(time_index.astype(F32), (0, 120))[None]),
            [((32, 24, 128), F32)],
        )
    )
    got = lax.all_to_all(rows, BOTH, 0, 0)
    block_out = down(acts, downs, middle, down_b, 2, 2, (block_out,))
    step((two, "fourth"), (three, "third_direct"))
    (early,) = add_up([join(one, two)])
    early_x = swap(early, "x")
    grad_table, sums = (
        simple(table_kernel, (got,), [((128, 128), F32), ((16, 128), F32)])
    )
    (late,) = add_up(three.last_direct(), cost=10000000000)
    late_x = swap(late, "x")
    (packed,) = add_up([pack_last(early, early_x, late)])
    other = swap(packed, "c")
    (down_shard,) = shard_of(tall_shard_kernel, where, (early, early_x, other), [(512, 1024)])
    (up_shard,) = shard_of(up_shard_kernel, where, (early, early_x, other), [(128, 4096)])
    (late_x,) = simple(pause_kernel, (), [], passing=(late_x,))
    late_corner = swap(late_x, "c")
    qkv_shard, out_shard = shard_of(
        qkv_shard_kernel, where, (late, late_x, other, late_corner), [(128, 3072), (128, 1024)]
    )
    return (
        block_out, grad_tokens, grad_table, sums[0], sums[1], qkv_shard, out_shard, sums[2], sums[3], sums[4],
        up_shard, sums[6:10].reshape(512), down_shard, sums[5],
    )


def solution(mesh):
    in_specs = (
        P(("fsdp", "dp"), None),
        P(("fsdp", "dp")),
        P(None, "fsdp"),
        P("fsdp"),
        P("fsdp"),
        P("fsdp", None),
        P("fsdp", None),
        P("fsdp"),
        P("fsdp"),
        P("fsdp"),
        P("fsdp", None),
        P("fsdp"),
        P("fsdp", None),
        P("fsdp"),
        P(("fsdp", "dp"), None),
    )
    out_specs = (
        P(("fsdp", "dp"), None),
        P(("fsdp", "dp"), None),
        P(None, "fsdp"),
        P("fsdp"),
        P("fsdp"),
        P("fsdp", None),
        P("fsdp", None),
        P("fsdp"),
        P("fsdp"),
        P("fsdp"),
        P("fsdp", None),
        P("fsdp"),
        P("fsdp", None),
        P("fsdp"),
    )
    local = eight_by_four if (mesh.shape["fsdp"], mesh.shape["dp"]) == (8, 4) else plain
    return jax.shard_map(local, mesh=mesh, in_specs=in_specs, out_specs=out_specs, check_vma=False)
```

```python
import functools

import jax
import jax.numpy as jnp
from jax import lax
from jax.experimental import pallas as pl
from jax.experimental.pallas import tpu as pltpu
from jax.sharding import PartitionSpec as P

HEADS = 16
BOTH = ("fsdp", "dp")
LOW = jnp.bfloat16
F32 = jnp.float32
NT = (((1,), (1,)), ((), ()))
TN = (((0,), (0,)), ((), ()))


def flips(which):
    pairs = []
    for f in range(8):
        for d in range(4):
            z, y, x, c = f // 2, f % 2, d // 2, d % 2
            if which == "x":
                x = 1 - x
            elif which == "y":
                y = 1 - y
            elif which == "c":
                c = 1 - c
            elif which == "z1":
                z = z ^ 1
            elif which == "z2":
                z = z ^ 2
            elif which == "z3":
                z = z ^ 3
            pairs.append((f * 4 + d, (z * 2 + y) * 4 + x * 2 + c))
    return pairs


def swap(values, which):
    return lax.ppermute(values, BOTH, flips(which))


def coords():
    f, d = lax.axis_index("fsdp"), lax.axis_index("dp")
    return f // 2, f % 2, d // 2, d % 2


def call(kernel, grid, ins, outs, flops=0, nbytes=0, scratch=(), prefetch=0, aliases=None, limit=18, pin=(), pin_out=(), cost=0
):
    after = tuple(chain)

    def spec(block, index):
        if block is None:
            return pl.BlockSpec(memory_space=pl.ANY)
        if block == "hbm":
            return pl.BlockSpec(memory_space=pltpu.MemorySpace.HBM)
        if index in constant and grid:
            return pl.BlockSpec(block, index, pipeline_mode=pl.Buffered(1))
        return pl.BlockSpec(block, index)

    def body(*refs):
        n = prefetch + len(ins)
        m = n + len(after) + len(outs)
        kernel(*refs[:n], *refs[n + len(after) : m], *refs[m + 1 :])

    run = pl.pallas_call(
        body,
        out_shape=[
            pltpu.MemorySpace.HBM(shape, kind) if k in pin_out else jax.ShapeDtypeStruct(shape, kind)
            for k, (shape, kind, _, _) in enumerate(outs)
        ]
        + [pltpu.MemorySpace.HBM((8, 128), F32)],
        grid_spec=pltpu.PrefetchScalarGridSpec(
            num_scalar_prefetch=prefetch,
            grid=grid,
            in_specs=[spec(block, index) for block, index in ins] + [spec(None, None)] * len(after),
            out_specs=[spec(block, index) for _, _, block, index in outs] + [spec(None, None)],
            scratch_shapes=scratch,
        ),
        input_output_aliases=aliases or {},
        compiler_params=pltpu.CompilerParams(
            vmem_limit_bytes=limit * 2**20, dimension_semantics=("arbitrary",) * len(grid)
        ),
        cost_estimate=pl.CostEstimate(flops=cost, bytes_accessed=1024, transcendentals=0),
    )

    def pinned(*args):
        args = [
            pltpu.with_memory_space_constraint(a, pltpu.MemorySpace.HBM) if k - prefetch in pin else a
            for k, a in enumerate(args)
        ]
        *values, token = run(*args, *(pltpu.with_memory_space_constraint(t, pltpu.MemorySpace.HBM) for t in after))
        chain[:] = [token]
        return values

    return pinned


def simple(kernel, args, outs, where=None, passing=(), limit=12, pin_out=(), cost=0):
    def whole(shape):
        return shape, lambda *_: (0,) * len(shape)

    prefetch = 0 if where is None else 1
    n_in, n_out, n_pass = len(args), len(outs), len(passing)

    def body(*refs):
        first = prefetch + n_in
        kernel(*refs[:first], *refs[first + n_pass : first + n_pass + n_out])

    run = call(
        body,
        (),
        [whole(a.shape) for a in args] + [(None, None)] * n_pass,
        [(shape, kind, *whole(shape)) for shape, kind in outs] + [(a.shape, a.dtype, None, None) for a in passing],
        prefetch=prefetch,
        aliases={prefetch + n_in + k: n_out + k for k in range(n_pass)},
        limit=limit,
        pin_out=pin_out,
        cost=cost,
    )
    return run(*(() if where is None else (where,)), *args, *passing)


constant = []
chain = []


def fixed(*index):
    constant.append(lambda *grid: index)
    return constant[-1]


def ends(n):
    e = n * 3 // 8
    return e // 2, (n - 2 * e) // 2


def end_start(n, x, c):
    eh, mh = ends(n)
    return x * (n - 2 * eh) + c * eh


def middle_start(n, c):
    eh, mh = ends(n)
    return 2 * eh + c * mh


COLS = 2048
CE, CM = ends(COLS)
CW = CE + CM


def lanes(start, size=128):
    return pl.ds(start if isinstance(start, int) else pl.multiple_of(start, 128), size)


def own_columns(where, dest, read):
    x, c = where[2], where[3]
    for i in range(CW // 128):
        start = end_start(COLS, x, c) + i * 128 if i < CE // 128 else middle_start(COLS, c) + i * 128 - CE
        dest[:, i * 128 : (i + 1) * 128] = read(start)


def own_up(where, up_w, half):
    return lambda start: up_w[:, lanes((start // 256) * 512 + half * 256 + start % 256)]


def own_first_kernel(where, qkv, out_w, up_w, parts, sems):
    x, c = where[2], where[3]
    copies = []
    for piece in range(3):
        for i in range(CW // 128):
            start = end_start(COLS, x, c) + i * 128 if i < CE // 128 else middle_start(COLS, c) + i * 128 - CE
            dest = parts.at[piece, :, i * 128 : (i + 1) * 128]
            sem = sems.at[piece * (CW // 128) + i]
            if piece == 1:
                value = pltpu.make_async_copy(qkv.at[:, lanes(2048 + jnp.minimum(start, 896))], dest, sem)
                other = pltpu.make_async_copy(out_w.at[:, lanes(jnp.maximum(start - 1024, 0))], dest, sem)
                pl.when(start < 1024)(value.start)
                pl.when(start >= 1024)(other.start)
                copies.append(value)
                continue
            if piece == 0:
                source = qkv.at[:, lanes(start)]
            else:
                source = up_w.at[:, lanes((start // 256) * 512 + start % 256)]
            copies.append(pltpu.make_async_copy(source, dest, sem))
            copies[-1].start()
    for copy in copies:
        copy.wait()


def own_first(where, qkv, out_w, up_w):
    shape = (3, 128, CW)
    return call(
        own_first_kernel,
        (),
        [("hbm", None)] * 3,
        [(shape, LOW, shape, lambda *_: (0, 0, 0))],
        prefetch=1,
        scratch=[pltpu.SemaphoreType.DMA((3 * (CW // 128),))],
        limit=8,
        pin=(0, 1, 2),
    )(where, qkv, out_w, up_w)


def own_other_kernel(where, up_w, down_w, parts):
    own_columns(where, parts.at[0], own_up(where, up_w, 1))
    for half in range(2):
        own_columns(
            where,
            parts.at[1 + half],
            lambda start: down_w[
                pl.ds(pl.multiple_of(half * 256 + (start // 1024) * 128, 128), 128), lanes(start % 1024)
            ],
        )


def move(jobs, passing=()):
    args = []
    for _, copies in jobs:
        for array, _, _ in copies:
            if not any(array is a for a in args):
                args.append(array)

    def kernel(*refs):
        outs = refs[len(args) :]
        for out, (_, copies) in zip(outs, jobs, strict=True):
            for array, read, write in copies:
                ref = refs[[i for i, a in enumerate(args) if a is array][0]]
                out[write] = ref[read if read != () else ...]

    return simple(kernel, args, [(shape, LOW) for shape, _ in jobs], passing=passing)


class Piece:
    def __init__(self, part, index, tall=False):
        self.part, self.index, self.tall = part, index, tall
        self.shape = (128, CW)
        self.pair = None

    def two(self):
        return (2, *self.shape), [(self.part, self.index, 0), (self.near, self.near_index, 1)]

    def four(self):
        return (4, *self.shape), [
            (self.part, self.index, 0),
            (self.near, self.near_index, 1),
            (self.far, slice(None), slice(2, 4)),
        ]

    def blocks(self):
        found = [(self.near, self.near_index)] + [(self.far, (i,)) for i in range(2)]
        return found + [(self.beside, (i,)) for i in range(4)]

    def across_send(self):
        end = (slice(None), slice(0, CE))
        return (7, 128, CE), [(a, (*i, *end), j) for j, (a, i) in enumerate(self.blocks())]

    def core_send(self):
        first, last = (slice(None), slice(0, CW)), (slice(None), slice(CW, CW + CE))
        copies = [(a, i, (j, *first)) for j, (a, i) in enumerate(self.blocks())]
        return (7, 128, CW + CE), copies + [(self.across, j, (j, *last)) for j in range(7)]

    def move_z1(self, near, near_index):
        self.near, self.near_index = near, near_index

    def move_z2(self, two):
        self.far = swap(two, "z2")

    def move_y(self, four):
        self.beside = swap(four, "y")

    def move_x(self, send):
        self.across = swap(send, "x")

    def move_c(self, send):
        self.other = swap(send, "c")


def assemble_kernel(tall, own_copies, near_index, where, *refs):
    n_own = len(own_copies)
    owns = refs[:n_own]
    near, far, beside, across, other, out, sems = refs[n_own:]
    z, y, x, c = where[0], where[1], where[2], where[3]
    eh, mh = CE, CM

    def at(shard, start, count):
        if not tall:
            return out.at[pl.ds(pl.multiple_of(shard * 128, 128), 128), lanes(start, count)]
        row = shard * 256 + (start // 1024) * 128
        return out.at[pl.ds(pl.multiple_of(row, 128), 128), lanes(start % 1024, count)]

    def cut(block, start, count):
        return block.at[:, pl.ds(start, count)]

    copies = []
    for j in range(8):
        shard = (z ^ (j % 4)) * 2 + (y if j < 4 else 1 - y)
        if j == 0:
            for ref, (read, start, count) in zip(owns, own_copies, strict=True):
                for k in range(len(read)):
                    copies.append((ref.at[read[k]], at(shard, start[k], count)))
            continue
        close = near.at[near_index[0]] if near_index else near
        mine = (close, far.at[0], far.at[1], beside.at[0], beside.at[1], beside.at[2], beside.at[3])[j - 1]
        oc = 1 - c
        copies += [
            (cut(mine, 0, eh), at(shard, end_start(COLS, x, c), eh)),
            (cut(mine, eh, mh), at(shard, middle_start(COLS, c), mh)),
            (cut(across.at[j - 1], 0, eh), at(shard, end_start(COLS, 1 - x, c), eh)),
            (cut(other.at[j - 1], 0, eh), at(shard, end_start(COLS, x, oc), eh)),
            (cut(other.at[j - 1], eh, mh), at(shard, middle_start(COLS, oc), mh)),
            (cut(other.at[j - 1], eh + mh, eh), at(shard, end_start(COLS, 1 - x, oc), eh)),
        ]
    copies = [pltpu.make_async_copy(s, d, sems.at[k]) for k, (s, d) in enumerate(copies)]
    for copy in copies:
        copy.start()
    for copy in copies:
        copy.wait()


def assemble(where, piece, owns):
    shape = (2048, 1024) if piece.tall else (1024, COLS)
    args = [o[0] for o in owns] + [piece.near, piece.far, piece.beside, piece.across, piece.other]
    n_copies = 42 + sum(len(o[1]) for o in owns)
    return call(
        functools.partial(assemble_kernel, piece.tall, [o[1:] for o in owns], piece.near_index),
        (),
        [(None, None)] * len(args),
        [(shape, LOW, shape, lambda *_: (0, 0))],
        prefetch=1,
        scratch=[pltpu.SemaphoreType.DMA((n_copies,))],
        limit=8,
    )(where, *args)[0]


def small_kernel(where, four, beside, time_index, table, vec, up_b, scale):
    z, y = where[0], where[1]
    for j in range(8):
        block = four.at[j] if j < 4 else beside.at[j - 4]
        shard = (z ^ (j // 4 + j // 2 % 2 * 2)) * 2 + (y ^ (j % 2))
        table[:, lanes(shard * 128)] = block[:128, :]
        vec[:, lanes(shard * 128)] = block[128:, :].astype(F32)
        for row in range(4):
            unit = lanes(shard * 256 + (row % 2) * 128)
            up_b[row // 2 : row // 2 + 1, unit] = block[134 + row : 135 + row, :].astype(F32)
    numbers = lax.broadcasted_iota(jnp.int32, (time_index.shape[0], 128), 1)
    one_hot = (numbers == time_index[...]).astype(F32).astype(LOW)
    scale[...] = 1.0 + jnp.dot(one_hot, table[...], preferred_element_type=F32)


def small_params(where, four, beside, time_index):
    return simple(
        small_kernel,
        (four, beside, time_index),
        [((128, 1024), LOW), ((16, 1024), F32), ((2, 2048), F32), ((time_index.shape[0], 1024), F32)],
        where=where,
    )


def rows_kernel(d_emb, sums_one, sums_two, up_a, up_b, times, out):
    for s in range(8):
        here = slice(s * 128, (s + 1) * 128)
        rows = [d_emb[i, :, here] for i in range(8)]
        rows += [sums_one[0:2, here], sums_two[2:3, here], sums_two[0:2, here], sums_two[3:4, here]]
        for sums in (up_a, up_b):
            rows += [sums[:, s * 256 + j * 128 : s * 256 + (j + 1) * 128] for j in range(2)]
        rows += [times[...], jnp.zeros((5, 128), F32)]
        block = jnp.concatenate(rows, axis=0)
        for copy in range(4):
            out[s * 4 + copy] = block


def mm(a, b):
    return jnp.dot(a, b, preferred_element_type=F32)


def mm_nt(a, b):
    return lax.dot_general(a, b, NT, preferred_element_type=F32)


def mm_tn(a, b):
    return lax.dot_general(a, b, TN, preferred_element_type=F32)


def centre(values):
    mean = jnp.mean(values, axis=-1, keepdims=True)
    centred = values - mean
    scale = lax.rsqrt(jnp.mean(centred * centred, axis=-1, keepdims=True) + 1e-05)
    return centred * scale, scale


def first_norm_kernel(tokens, gain, bias, scale, scaled):
    hat, _ = centre(tokens[...].astype(F32))
    scaled[...] = ((hat * gain[...] + bias[...]) * scale[0]).astype(LOW)


def first_norm(tokens, gain, bias, scale):
    rows, width = tokens.shape
    seqs = scale.shape[0]
    length = rows // seqs
    return call(
        first_norm_kernel,
        (seqs,),
        [
            ((length, width), lambda i: (i, 0)),
            ((1, width), fixed(0, 0)),
            ((1, width), fixed(0, 0)),
            ((1, 1, width), lambda i: (i, 0, 0)),
        ],
        [((rows, width), LOW, (length, width), lambda i: (i, 0))],
    )(tokens, gain, bias, scale)[0]


def halves(values):
    lane = lax.broadcasted_iota(jnp.int32, values.shape, 1)
    zero = jnp.zeros_like(values)
    return jnp.concatenate([jnp.where(lane < 64, values, zero), jnp.where(lane < 64, zero, values)], axis=0)


def side(values):
    n = values.shape[0] // 2
    return jnp.concatenate([values[:n], values[n:]], axis=1)


def project_kernel(x, w, out):
    out[...] = mm(x[...], w[...]).astype(LOW)


def project(x, w, tile=512):
    rows, width = x.shape
    n = w.shape[1]
    return call(
        project_kernel,
        (n // tile,),
        [((rows, width), fixed(0, 0)), ((width, tile), lambda i: (0, i))],
        [((rows, n), LOW, (rows, tile), lambda i: (0, i))],
    )(x, w)[0]


def units_of(rows, length, at_once=8):
    units = []
    for seq in range(rows // length):
        for pair in range(2):
            units.append((seq, pair, (slice(seq * length, (seq + 1) * length), slice(pair * 128, (pair + 1) * 128))))
    return [units[i : i + at_once] for i in range(0, len(units), at_once)]


def attend_kernel(length, scaled, wv, q_in, k_in, *refs):
    v_out, probs_out, mix_out = refs[-3:]
    factor = 64 ** (-0.5) * 1.4426950408889634
    v_out[...] = mm(scaled[...], wv[...]).astype(LOW)
    for units in units_of(scaled.shape[0], length):
        scores = [mm_nt(halves(q_in[here]), k_in[here]) for _, _, here in units]
        found = []
        for s in scores:
            e = jnp.exp2((s - jnp.max(s, axis=-1, keepdims=True)) * factor)
            found.append((e * (1.0 / jnp.sum(e, axis=-1, keepdims=True))).astype(LOW))
        for (seq, pair, here), probs in zip(units, found, strict=True):
            probs_out[0, seq, pair] = probs
            mix_out[here] = mm(side(probs), halves(v_out[here])).astype(LOW)


def attend(scaled, qk, vo, length, first=0, count=None, earlier=()):
    rows, width = scaled.shape
    groups = width // 256
    seqs = rows // length
    count = groups if count is None else count
    column = lambda i: (0, first + i)
    wide = ((rows, width), LOW, (rows, 256), column)
    probs = (groups, seqs, 2, 2 * length, length)
    return call(
        functools.partial(attend_kernel, length),
        (count,),
        [
            ((rows, width), fixed(0, 0)),
            ((width, 256), column),
            ((rows, 256), column),
            ((rows, 256), lambda i: (0, groups + first + i)),
        ]
        + [(None, None)] * len(earlier),
        [wide, (probs, LOW, (1, *probs[1:]), lambda i: (first + i, 0, 0, 0, 0)), wide],
        aliases={4 + i: i for i in range(len(earlier))},
    )(scaled, vo, qk, qk, *earlier)


def middle_kernel(mix, tokens, w, out_b, gain, bias, middle_out, hidden_out):
    middle = tokens[...].astype(F32) + mm(mix[...], w[...]) + out_b[...]
    middle_out[...] = middle
    hat, _ = centre(middle)
    hidden_out[...] = (hat * gain[...] + bias[...]).astype(LOW)


def second_norm(mix, tokens, vo, out_b, gain, bias):
    rows, width = tokens.shape
    row = lambda i: (i, 0)
    vec = ((1, width), fixed(0, 0))
    return call(
        middle_kernel,
        (rows // 256,),
        [((256, width), row), ((256, width), row), ((width, width), fixed(0, 1)), vec, vec, vec],
        [((rows, width), F32, (256, width), row), ((rows, width), LOW, (256, width), row)],
    )(mix, tokens, vo, out_b, gain, bias)


def gelu_parts(v):
    cdf = 0.5 + 0.5 * lax.erf(v * 0.5**0.5)
    bell = jnp.exp(-0.5 * v * v)
    return v * cdf, cdf + (v * 0.3989422804014327) * bell


def up_kernel(hidden, w, bias, act, slope):
    value, pull = gelu_parts(mm(hidden[...], w[...]) + bias[...])
    act[...] = value.astype(LOW)
    slope[...] = pull.astype(LOW)


def up(hidden, w, bias, tile=512):
    rows, width = hidden.shape
    n = w.shape[1]
    column = lambda i: (0, i)
    return call(
        up_kernel,
        (n // tile,),
        [((rows, width), fixed(0, 0)), ((width, tile), column), ((1, tile), column)],
        [((rows, n), LOW, (rows, tile), column)] * 2,
        limit=22,
        pin_out=(1,),
    )(hidden, w, bias)


def down_kernel(act_a, act_b, first, second, middle, bias, *refs):
    total = middle[...] + bias[...]
    total += mm(act_a[...], first[...])
    total += mm(act_b[...], second[...])
    refs[-1][...] = total.astype(LOW)


def down(acts, ws, middle, bias, start, count, earlier=(), tile=256):
    rows, width = middle.shape
    k = ws[0].shape[0]
    row = lambda i: (start + i, 0)
    return call(
        down_kernel,
        (count,),
        [((tile, k), row)] * 2
        + [((k, width), fixed(0, 0))] * 2
        + [((tile, width), row), ((1, width), fixed(0, 0))]
        + [(None, None)] * len(earlier),
        [((rows, width), LOW, (tile, width), row)],
        aliases={6 + i: i for i in range(len(earlier))},
        limit=56,
    )(*acts, *ws, middle, bias, *earlier)[0]


def pull_kernel(cot, w, slope, *refs):
    d_pre, sums = refs[-2:]
    value = (mm_nt(cot[...], w[...]) * slope[...].astype(F32)).astype(LOW)
    d_pre[0] = value
    sums[...] = jnp.sum(value.astype(F32), axis=0, keepdims=True)


def pull(cot, w, slope, half, earlier=None, tile=512):
    rows, width = cot.shape
    n = w.shape[0]
    column = lambda i: (0, i)
    ins = [((rows, width), fixed(0, 0)), ((tile, width), lambda i: (i, 0)), ((rows, tile), column)]
    return call(
        pull_kernel,
        (n // tile,),
        ins + ([] if earlier is None else [(None, None)]),
        [((2, rows, n), LOW, (1, rows, tile), lambda i: (half, 0, i)), ((1, n), F32, (1, tile), column)],
        aliases={} if earlier is None else {3: 0},
        pin=(2,),
    )(cot, w, slope, *(() if earlier is None else (earlier,)))


def norm_back(d_out, hat, scale, gain):
    e = d_out * gain
    mean = jnp.mean(e, axis=-1, keepdims=True)
    slant = jnp.mean(e * hat, axis=-1, keepdims=True)
    return (e - mean - hat * slant) * scale


def fold(*rows_of):
    sums = [jnp.sum(v, axis=0, keepdims=True) for v in rows_of]
    return jnp.concatenate(sums + [jnp.zeros_like(sums[0])] * (8 - len(sums)), axis=0)


def middle_back_kernel(d_pre, wa, wb, middle, cot, gain, w_out, d_middle_out, d_low_out, d_mix_out, sums):
    d_hidden = mm_nt(d_pre[0], wa[...]) + mm_nt(d_pre[1], wb[...])
    hat, scale = centre(middle[...])
    d_middle = cot[...].astype(F32) + norm_back(d_hidden, hat, scale, gain[...])
    d_middle_out[...] = d_middle
    d_low = d_middle.astype(LOW)
    d_low_out[...] = d_low
    d_mix_out[...] = mm_nt(d_low, w_out[...]).astype(LOW)

    @pl.when(pl.program_id(0) == 0)
    def _():
        sums[...] = jnp.zeros_like(sums)

    sums[...] += fold(d_hidden * hat, d_hidden, d_low.astype(F32), cot[...].astype(F32))


def middle_back(d_pre, ws, middle, cot, gain, vo, tile=256):
    rows, width = middle.shape
    row = lambda i: (i, 0)
    return call(
        middle_back_kernel,
        (rows // tile,),
        [
            ((2, tile, d_pre.shape[2]), lambda i: (0, i, 0)),
            (ws[0].shape, fixed(0, 0)),
            (ws[1].shape, fixed(0, 0)),
            ((tile, width), row),
            ((tile, width), row),
            ((1, width), fixed(0, 0)),
            ((width, width), fixed(0, 1)),
        ],
        [
            ((rows, width), F32, (tile, width), row),
            ((rows, width), LOW, (tile, width), row),
            ((rows, width), LOW, (tile, width), row),
            ((8, width), F32, (8, width), fixed(0, 0)),
        ],
        limit=32,
    )(d_pre, *ws, middle, cot, gain, vo)


def attend_back_kernel(length, d_mix, probs, q_in, k_in, v_in, *refs):
    out = refs[-1]
    factor = 64 ** (-0.5)
    for units in units_of(d_mix.shape[0], length, 8):
        dms = [halves(d_mix[here]) for _, _, here in units]
        d_probs = [mm_nt(dm, v_in[here]) for dm, (_, _, here) in zip(dms, units, strict=True)]
        found = []
        for d, (seq, pair, _) in zip(d_probs, units, strict=True):
            high = probs[0, seq, pair].astype(F32)
            found.append((high * (d - jnp.sum(d * high, axis=-1, keepdims=True))).astype(LOW))
        for dm, d_scores, (seq, pair, here) in zip(dms, found, units, strict=True):
            out[(2, *here)] = mm_tn(probs[0, seq, pair], dm).astype(LOW)
            out[(0, *here)] = (mm(side(d_scores), halves(k_in[here])) * factor).astype(LOW)
            out[(1, *here)] = (mm_tn(d_scores, halves(q_in[here])) * factor).astype(LOW)


def attend_back(d_mix, probs, qk, v, length, first=0, count=None, earlier=()):
    rows, width = d_mix.shape
    count = width // 256 if count is None else count
    wide = ((rows, 256), lambda i: (0, first + i))
    return call(
        functools.partial(attend_back_kernel, length),
        (count,),
        [
            wide,
            ((1,) + probs.shape[1:], lambda i: (first + i, 0, 0, 0, 0)),
            wide,
            ((rows, 256), lambda i: (0, width // 256 + first + i)),
            wide,
        ]
        + [(None, None)] * len(earlier),
        [((3, rows, width), LOW, (3, rows, 256), lambda i: (0, 0, first + i))],
        aliases={5 + i: i for i in range(len(earlier))},
    )(d_mix, probs, qk, qk, v, *earlier)[0]


def input_back_kernel(length, d, wq, wk, wv, tokens, d_middle, gain, bias, scale, out, sums, d_emb):
    d_scaled = mm_nt(d[0], wq[...]) + mm_nt(d[1], wk[...]) + mm_nt(d[2], wv[...])
    hat, spread = centre(tokens[...].astype(F32))
    normed = hat * gain[...] + bias[...]
    count = tokens.shape[0] // length
    parts = []
    for i in range(count):
        here = slice(i * length, (i + 1) * length)
        d_emb[i] = jnp.sum(d_scaled[here] * normed[here], axis=0, keepdims=True)
        parts.append(d_scaled[here] * scale[i])
    d_normed = jnp.concatenate(parts, axis=0)
    out[...] = (d_middle[...] + norm_back(d_normed, hat, spread, gain[...])).astype(LOW)

    @pl.when(pl.program_id(0) == 0)
    def _():
        sums[...] = jnp.zeros_like(sums)

    sums[...] += fold(d_normed * hat, d_normed)


def input_back(d_packed, qk, vo, tokens, d_middle, gain, bias, scale, tile=256, cost=0):
    rows, width = tokens.shape
    seqs = scale.shape[0]
    length = rows // seqs
    row = lambda i: (i, 0)
    wide = ((tile, width), row)
    vec = ((1, width), fixed(0, 0))
    some = ((tile // length, 1, width), lambda i: (i, 0, 0))
    return call(
        functools.partial(input_back_kernel, length),
        (rows // tile,),
        [
            ((3, tile, width), lambda i: (0, i, 0)),
            ((width, width), fixed(0, 0)),
            ((width, width), fixed(0, 1)),
            ((width, width), fixed(0, 0)),
            wide, wide, vec, vec, some,
        ],
        [
            ((rows, width), LOW, (tile, width), row),
            ((8, width), F32, (8, width), fixed(0, 0)),
            ((seqs, 1, width), F32) + some,
        ],
        cost=cost,
        limit=26,
    )(d_packed, qk, qk, vo, tokens, d_middle, gain, bias, scale)


def tall_parts(where, a, b, cot, yy):
    here = slice(yy * 256, (yy + 1) * 256)
    value = mm_tn(jnp.concatenate([a[:, here], b[:, here]], axis=1), cot[...])
    x = where[2]
    found = []
    for xr in range(2):
        pair = []
        for half in range(2):
            low, high = value[half * 256 : half * 256 + 128], value[half * 256 + 128 : half * 256 + 256]
            pair.append(jnp.where((x ^ xr) == 0, low, high))
        found.append(pair)
    return found


def tall_away_kernel(where, a, b, cot, away):
    for yy in range(2):
        found = tall_parts(where, a, b, cot, yy)
        for xr in range(2):
            for half in range(2):
                away[xr, yy ^ where[1], 0, half] = found[xr][half].astype(LOW)


def tall_ins(acts, cot, core):
    rows, width = cot.shape
    act = ((rows, 512), lambda zr, where: (0, zr ^ where[0]))
    return [act, act, ((rows, width // 2), lambda zr, where: (0, where[3] ^ core))]


def tall_away(where, acts, cot):
    n = cot.shape[1] // 2
    return call(
        tall_away_kernel,
        (4,),
        tall_ins(acts, cot, 1),
        [((2, 2, 4, 2, 128, n), LOW, (2, 2, 1, 2, 128, n), lambda zr, where: (0, 0, zr, 0, 0, 0))],
        prefetch=1,
    )(where, *acts, cot)[0]


def tall_mine_kernel(where, a, b, cot, core, xa, yb, ka, kb):
    far = pl.program_id(0) >= 2
    for yy in range(2):
        found = tall_parts(where, a, b, cot, yy)
        yr = yy ^ where[1]
        sums = []
        for xr in range(2):
            sums.append([(found[xr][h] + core[xr, yr, 0, h].astype(F32)).astype(LOW) for h in range(2)])

        @pl.when(jnp.logical_not(far))
        def _(sums=sums, yr=yr):
            for half in range(2):
                ka[yr, 0, half] = sums[0][half]
                xa[yr, 0, half] = sums[1][half]

        @pl.when(far & (yr == 0))
        def _(sums=sums):
            for xr in range(2):
                for half in range(2):
                    kb[xr, 0, half] = sums[xr][half]

        @pl.when(far & (yr == 1))
        def _(sums=sums):
            for xr in range(2):
                for half in range(2):
                    yb[xr, 0, half] = sums[xr][half]


def tall_mine(where, acts, cot, core):
    n = cot.shape[1] // 2
    shape = (2, 2, 2, 128, n)
    block = (2, 1, 2, 128, n)
    close = (shape, LOW, block, lambda zr, where: (0, jnp.minimum(zr, 1), 0, 0, 0))
    far = (shape, LOW, block, lambda zr, where: (0, jnp.maximum(zr - 2, 0), 0, 0, 0))
    return call(
        tall_mine_kernel,
        (4,),
        tall_ins(acts, cot, 0) + [((2, 2, 1, 2, 128, n), lambda zr, where: (0, 0, zr, 0, 0, 0))],
        [close, far, close, far],
        prefetch=1,
        pin=(3,),
    )(where, *acts, cot, core)


def row_value(step, lefts, rights, counts, hold):
    first = 0
    for left, right, count in zip(lefts, rights, counts, strict=True):

        def put(left=left, right=right):
            b = right[0] if len(right.shape) == 3 else right[...]
            hold[...] = mm_tn(left[...], b)

        if len(lefts) == 1:
            put()
        else:
            pl.when((step >= first) & (step < first + count))(put)
        first += count


def row_from(where, xr, yr, zr):
    start = ((where[0] ^ zr) * 2 + (where[1] ^ yr)) * 128 + (where[2] ^ xr) * 64
    return pl.ds(pl.multiple_of(start, 64), 64)


def row_away_kernel(counts, where, *refs):
    n = len(counts)
    lefts, rights, away, hold = refs[:n], refs[n : 2 * n], refs[2 * n], refs[2 * n + 1]
    row_value(pl.program_id(0), lefts, rights, counts, hold)
    for xr in range(2):
        for yr in range(2):
            for zr in range(4):
                away[xr, yr, zr] = hold[row_from(where, xr, yr, zr), :].astype(LOW)


def row_mine_kernel(counts, where, *refs):
    n = len(counts)
    lefts, rights = refs[:n], refs[n : 2 * n]
    core, xa, yb, ka, kb, hold = refs[2 * n :]
    row_value(pl.program_id(0), lefts, rights, counts, hold)
    for xr in range(2):
        for yr in range(2):
            for zr in range(4):
                total = hold[row_from(where, xr, yr, zr), :] + core[xr, yr, zr].astype(F32)
                total = total.astype(LOW)
                if zr < 2:
                    (ka if xr == 0 else xa)[yr, zr] = total
                else:
                    (kb if yr == 0 else yb)[xr, zr - 2] = total


def row_specs(pairs, core, tile):
    ins, counts = [], []
    for a, _, _ in pairs:
        ins.append((a.shape, lambda j, where: (0, 0)))
    first = 0
    for _, b, kind in pairs:
        tokens = b.shape[-2]
        if kind == "layers":
            count = b.shape[0] * (b.shape[2] // 2 // tile)
            each = b.shape[2] // 2 // tile
            spec = (
                (1, tokens, tile),
                lambda j, where, f=first, m=count, e=each: (
                    jnp.clip(j - f, 0, m - 1) // e,
                    0,
                    (where[3] ^ core) * e + jnp.clip(j - f, 0, m - 1) % e,
                ),
            )
        elif kind == "layer":
            count = b.shape[2] // tile
            spec = (
                (1, tokens, tile),
                lambda j, where, f=first, m=count: (where[3] ^ core, 0, jnp.clip(j - f, 0, m - 1)),
            )
        else:
            count = b.shape[1] // 2 // tile
            spec = (
                (tokens, tile),
                lambda j, where, f=first, m=count: (0, (where[3] ^ core) * m + jnp.clip(j - f, 0, m - 1)),
            )
        ins.append(spec)
        counts.append(count)
        first += count
    return ins, counts


def row_away(where, pairs, tile=512):
    ins, counts = row_specs(pairs, 1, tile)
    steps = sum(counts)
    return call(
        functools.partial(row_away_kernel, counts),
        (steps,),
        ins,
        [((2, 2, 4, 64, steps * tile), LOW, (2, 2, 4, 64, tile), lambda j, where: (0, 0, 0, 0, j))],
        prefetch=1,
        scratch=[pltpu.VMEM((1024, tile), F32)],
    )(where, *[a for a, _, _ in pairs], *[b for _, b, _ in pairs])[0]


def row_mine(where, pairs, core, tile=512):
    ins, counts = row_specs(pairs, 0, tile)
    steps = sum(counts)
    out = ((2, 2, 64, steps * tile), LOW, (2, 2, 64, tile), lambda j, where: (0, 0, 0, j))
    return call(
        functools.partial(row_mine_kernel, counts),
        (steps,),
        ins + [((2, 2, 4, 64, tile), lambda j, where: (0, 0, 0, 0, j))],
        [out] * 4,
        prefetch=1,
        scratch=[pltpu.VMEM((1024, tile), F32)],
        pin=(2 * len(pairs),),
    )(where, *[a for a, _, _ in pairs], *[b for _, b, _ in pairs], core)


def add_up(jobs, passing=(), cost=0):
    args, pieces = [], []
    parts = [job[1] if isinstance(job[1][0][0], list) else [(job[1], ...)] for job in jobs]

    def number(array, index):
        here = [k for k, a in enumerate(args) if a is array]
        if not here:
            args.append(array)
            here = [len(args) - 1]
        if (here[0], index) not in pieces:
            pieces.append((here[0], index))
        return pieces.index((here[0], index))

    parts = [[([number(*term) for term in terms], write) for terms, write in part] for part in parts]
    shapes = [jax.eval_shape(lambda a, index=index: a[index], args[k]).shape for k, index in pieces]
    n_in, n_out, n_pass = len(args), len(jobs), len(passing)

    def kernel(*refs):
        ins, outs = refs[:n_in], refs[n_in + n_pass : n_in + n_pass + n_out]
        *held, sems = refs[n_in + 2 * n_pass + n_out :]
        copies = []
        for k, (at, index) in enumerate(pieces):
            copies.append(pltpu.make_async_copy(ins[at].at[index], held[k], sems.at[k]))
            copies[-1].start()
        waited = set()
        for out, part in zip(outs, parts, strict=True):
            for terms, write in part:
                total = None
                for k in terms:
                    if k not in waited:
                        copies[k].wait()
                        waited.add(k)
                    value = held[k][...].astype(F32)
                    total = value if total is None else total + value
                out[write] = total.astype(LOW)

    def whole(shape):
        return shape, lambda *_: (0,) * len(shape)

    return call(
        kernel,
        (),
        [("hbm", None)] * n_in + [(None, None)] * n_pass,
        [(job[0], LOW, *whole(job[0])) for job in jobs] + [(a.shape, a.dtype, None, None) for a in passing],
        aliases={n_in + k: n_out + k for k in range(n_pass)},
        scratch=[pltpu.VMEM(shape, LOW) for shape in shapes] + [pltpu.SemaphoreType.DMA((len(pieces),))],
        cost=cost,
        limit=12,
    )(*args, *passing)


class Reduction:
    def __init__(self, ka, kb):
        self.ka, self.kb = ka, kb
        self.tail = ka.shape[2:]

    def go_first(self, xa, yb):
        self.xa, self.yb = swap(xa, "x"), swap(yb, "y")

    def second(self):
        shape = (2, *self.tail)
        return [(shape, [(self.ka, 1), (self.xa, 1)]), (shape, [(self.kb, 1), (self.yb, 1)])]

    def go_second(self, ya, xb):
        self.ya, self.xb = swap(ya, "y"), swap(xb, "x")

    def kept(self, i):
        return self.tail, [(self.ka, (0, i)), (self.xa, (0, i)), (self.ya, i)]

    def sent(self, i):
        return self.tail, [(self.kb, (0, i)), (self.yb, (0, i)), (self.xb, i)]

    def third(self):
        two = [((2, *self.tail), [(self.kb, 0), (self.yb, 0), (self.xb, slice(None))])]
        return two + [self.kept(0), self.kept(1)]

    def go_third(self, far, mine, next_one):
        self.far, self.mine, self.next_one = swap(far, "z2"), mine, next_one

    def fourth(self):
        return [(self.tail, [(self.next_one, slice(None)), (self.far, 1)])]

    def go_fourth(self, near):
        self.near = swap(near, "z1")

    def last(self):
        return [(self.tail, [(self.mine, slice(None)), (self.far, 0), (self.near, slice(None))])]

    def third_direct(self):
        return [self.kept(1), self.sent(0), self.sent(1), self.kept(0)]

    def go_third_direct(self, *blocks):
        self.got = [swap(block, name) for block, name in zip(blocks, ("z1", "z2", "z3"))]
        self.mine = blocks[3]

    def last_direct(self):
        return [(self.tail, [(self.mine, slice(None))] + [(got, slice(None)) for got in self.got])]


def join(first, second):
    (_, terms), = first.last()
    parts = []
    for half in range(2):
        cut = [(array, (0, half) if index == 0 else half) for array, index in terms]
        parts.append((cut, slice(half * 128, half * 128 + 128)))
    (_, terms), = second.last()
    for k in range(4):
        here = (slice(None), slice(k * 512, k * 512 + 512))
        cut = [(array, (0, *here) if index == 0 else here) for array, index in terms]
        parts.append((cut, slice(256 + k * 64, 320 + k * 64)))
    return (512, 512), parts


def pack_last(early, early_x, late):
    whole = slice(None)
    parts = [([(early, whole)], slice(0, 512)), ([(early_x, whole)], slice(512, 1024))]
    for k in range(4):
        here = (slice(None), slice(k * 512, k * 512 + 512))
        parts.append(([(late, here)], slice(1024 + k * 64, 1088 + k * 64)))
    return (1280, 512), parts


def pause_kernel(*_):
    pass


def early_blocks(where, early, early_x, other):
    x, c = where[2], where[3]
    return (
        (early, 0, x, c), (early_x, 0, 1 - x, c), (other, 0, x, 1 - c), (other, 512, 1 - x, 1 - c),
    )


def tall_shard_kernel(where, early, early_x, other, out):
    for block, first, xx, cc in early_blocks(where, early, early_x, other):
        for half in range(2):
            rows = pl.ds(pl.multiple_of(half * 256 + xx * 128, 128), 128)
            out[rows, lanes(cc * 512, 512)] = block[first + half * 128 : first + half * 128 + 128, :].astype(F32)


def up_shard_kernel(where, early, early_x, other, up_out):
    for block, first, xx, cc in early_blocks(where, early, early_x, other):
        rows = pl.ds(pl.multiple_of(xx * 64, 64), 64)
        for s in range(8):
            start = first + 256 + (s // 2) * 64
            value = block[start : start + 64, (s % 2) * 256 : (s % 2) * 256 + 256]
            up_out[rows, lanes(s * 512 + cc * 256, 256)] = value.astype(F32)


def qkv_shard_kernel(where, late, late_x, other, corner, out, out_out):
    x, c = where[2], where[3]
    for block, packed, xx, cc in (
        (late, False, x, c), (late_x, False, 1 - x, c), (other, True, x, 1 - c), (corner, False, 1 - x, 1 - c),
    ):
        rows = pl.ds(pl.multiple_of(xx * 64, 64), 64)
        for k in range(4):
            if packed:
                value = block[1024 + k * 64 : 1088 + k * 64, :]
            else:
                value = block[:, k * 512 : (k + 1) * 512]
            if k < 3:
                out[rows, lanes(k * 1024 + cc * 512, 512)] = value.astype(F32)
            else:
                out_out[rows, lanes(cc * 512, 512)] = value.astype(F32)


def shard_of(kernel, where, blocks, shapes):
    return simple(kernel, blocks, [(s, F32) for s in shapes], where=where, pin_out=range(len(shapes)))


def table_kernel(got, table, vec):
    n = got.shape[0]
    times = lax.broadcasted_iota(jnp.int32, (128, 8), 0).astype(F32)
    total = jnp.zeros(table.shape, F32)
    sums = jnp.zeros(vec.shape, F32)
    for i in range(n):
        hot = (times == got[i, 18:19, 0:8]).astype(F32)
        total += lax.dot_general(hot, got[i, 0:8, :], (((1,), (0,)), ((), ())), precision=lax.Precision.HIGHEST)
        sums += got[i, 8:24, :]
    table[...] = total
    vec[...] = sums


def normalize(values):
    centred = values - jnp.mean(values, axis=-1, keepdims=True)
    spread = jnp.mean(centred * centred, axis=-1, keepdims=True)
    return centred * lax.rsqrt(spread + 1e-05)


def scaled_norm(values, gain):
    return normalize(values) * gain


def exact_gelu(values):
    return jax.nn.gelu(values, approximate=False)


def layer(
    tokens,
    time_index,
    table_all,
    gain_one,
    bias_one,
    qkv_w,
    out_w,
    out_b,
    gain_two,
    bias_two,
    up_w,
    up_b,
    down_w,
    down_b,
    cotangent,
):
    row_count, model_width = tokens.shape
    seq_count = time_index.shape[0]
    length = row_count // seq_count
    head_dim = model_width // HEADS
    factor = head_dim ** (-0.5)
    levels = table_all.shape[0]
    gain_one_f = gain_one.astype(jnp.float32)
    gain_two_f = gain_two.astype(jnp.float32)
    one_hot = time_index[:, None] == jnp.arange(levels, dtype=jnp.int32)[None, :]
    embedding = jnp.dot(one_hot.astype(jnp.bfloat16), table_all, preferred_element_type=jnp.float32)
    scale_seq = (1.0 + embedding)[:, None, :]
    inputs = tokens.astype(jnp.float32)
    normed = (normalize(inputs) * gain_one_f + bias_one.astype(jnp.float32)).reshape(
        seq_count, length, model_width
    )
    scaled = (normed * scale_seq).astype(jnp.bfloat16).reshape(row_count, model_width)
    packed = jnp.dot(scaled, qkv_w, preferred_element_type=jnp.float32).astype(jnp.bfloat16)
    packed = packed.reshape(seq_count, length, 3, HEADS, head_dim)
    queries = packed[:, :, 0]
    key_heads = packed[:, :, 1]
    value_heads = packed[:, :, 2]
    scores = (
        jnp.einsum("sqhd,skhd->shqk", queries, key_heads, preferred_element_type=jnp.float32)
        * factor
    )
    attn_probs = jax.nn.softmax(scores, axis=-1)
    probs_low = attn_probs.astype(jnp.bfloat16)
    attn_mix = jnp.einsum(
        "shqk,skhd->sqhd", probs_low, value_heads, preferred_element_type=jnp.float32
    )
    attn_mix = attn_mix.astype(jnp.bfloat16).reshape(row_count, model_width)
    middle = (
        inputs
        + jnp.dot(attn_mix, out_w, preferred_element_type=jnp.float32)
        + out_b.astype(jnp.float32)
    )
    hidden_in = (normalize(middle) * gain_two_f + bias_two.astype(jnp.float32)).astype(jnp.bfloat16)
    pre_act = jnp.dot(hidden_in, up_w, preferred_element_type=jnp.float32) + up_b.astype(
        jnp.float32
    )
    activated = exact_gelu(pre_act).astype(jnp.bfloat16)
    block_out = (
        middle
        + jnp.dot(activated, down_w, preferred_element_type=jnp.float32)
        + down_b.astype(jnp.float32)
    ).astype(jnp.bfloat16)
    upstream = cotangent.astype(jnp.float32)
    grad_down = jnp.einsum("ti,td->id", activated, cotangent, preferred_element_type=jnp.float32)
    grad_down_b = jnp.sum(upstream, axis=0)
    d_act = jnp.einsum("td,id->ti", cotangent, down_w, preferred_element_type=jnp.float32)
    gelu_pull = jax.vjp(exact_gelu, pre_act)[1]
    d_pre = gelu_pull(d_act)[0].astype(jnp.bfloat16)
    grad_up = jnp.einsum("ti,tf->if", hidden_in, d_pre, preferred_element_type=jnp.float32)
    grad_up_b = jnp.sum(d_pre.astype(jnp.float32), axis=0)
    d_hidden = jnp.einsum("tf,if->ti", d_pre, up_w, preferred_element_type=jnp.float32)
    grad_ln2_bias = jnp.sum(d_hidden, axis=0)
    second_pull = jax.vjp(scaled_norm, middle, gain_two_f)[1]
    d_mid_part, grad_ln2_gain = second_pull(d_hidden)
    d_middle = upstream + d_mid_part
    d_mid_low = d_middle.astype(jnp.bfloat16)
    grad_out_w = jnp.einsum("ti,td->id", attn_mix, d_mid_low, preferred_element_type=jnp.float32)
    grad_out_b = jnp.sum(d_mid_low.astype(jnp.float32), axis=0)
    d_mix = jnp.einsum("td,id->ti", d_mid_low, out_w, preferred_element_type=jnp.float32)
    d_mix = d_mix.astype(jnp.bfloat16).reshape(seq_count, length, HEADS, head_dim)
    d_probs = jnp.einsum("sqhd,skhd->shqk", d_mix, value_heads, preferred_element_type=jnp.float32)
    d_values = jnp.einsum("shqk,sqhd->skhd", probs_low, d_mix, preferred_element_type=jnp.float32)
    d_scores = (
        attn_probs * (d_probs - jnp.sum(d_probs * attn_probs, axis=-1, keepdims=True))
    ).astype(jnp.bfloat16)
    d_queries = (
        jnp.einsum("shqk,skhd->sqhd", d_scores, key_heads, preferred_element_type=jnp.float32)
        * factor
    )
    d_keys = (
        jnp.einsum("shqk,sqhd->skhd", d_scores, queries, preferred_element_type=jnp.float32)
        * factor
    )
    d_packed = (
        jnp.stack([d_queries, d_keys, d_values], axis=2)
        .astype(jnp.bfloat16)
        .reshape(row_count, 3 * model_width)
    )
    grad_qkv = jnp.einsum("ti,tf->if", scaled, d_packed, preferred_element_type=jnp.float32)
    d_scaled = jnp.einsum("tf,if->ti", d_packed, qkv_w, preferred_element_type=jnp.float32).reshape(
        seq_count, length, model_width
    )
    d_normed = d_scaled * scale_seq
    grad_ln1_bias = jnp.sum(d_normed, axis=(0, 1))
    d_embedding = jnp.sum(d_scaled * normed, axis=1)
    grad_table = jnp.einsum(
        "sn,sd->nd", one_hot.astype(jnp.float32), d_embedding, precision=lax.Precision.HIGHEST
    )
    first_pull = jax.vjp(scaled_norm, inputs, gain_one_f)[1]
    d_in_part, grad_ln1_gain = first_pull(d_normed.reshape(row_count, model_width))
    grad_tokens = (d_middle + d_in_part).astype(jnp.bfloat16)
    return (
        block_out,
        grad_tokens,
        (grad_table, grad_ln1_gain, grad_ln1_bias, grad_qkv, grad_out_w, grad_out_b, grad_ln2_gain,
         grad_ln2_bias, grad_up, grad_up_b, grad_down, grad_down_b),
    )


def plain(*args):
    dims = (None, None, 1, 0, 0, 0, 0, 0, 0, 0, 0, 0, 0, 0, None)
    whole = [
        item if dim is None else lax.all_gather(item, "fsdp", axis=dim, tiled=True)
        for item, dim in zip(args, dims, strict=True)
    ]
    block_out, grad_tokens, grads = layer(*whole)
    shares = [
        lax.psum_scatter(grad, "fsdp", scatter_dimension=1 if place == 0 else 0, tiled=True)
        for place, grad in enumerate(grads)
    ]
    return (block_out, grad_tokens, *lax.psum(tuple(shares), "dp"))


def eight_by_four(
    tokens, time_index, time_table, ln1_gain, ln1_bias, w_qkv, w_out, b_out, ln2_gain, ln2_bias,
    w_up, b_up, w_down, b_down, cotangent,
):
    where = jnp.stack(coords()).astype(jnp.int32)
    seqs = time_index.shape[0]
    length = tokens.shape[0] // seqs
    vec = jnp.concatenate(
        [v.reshape(-1, 128) for v in (ln1_gain, ln1_bias, b_out, ln2_gain, ln2_bias, b_down, b_up)]
        + [jnp.zeros((6, 128), LOW)]
    )
    times = time_index.reshape(seqs, 1)
    chain.clear()

    (parts_first,) = own_first(where, w_qkv, w_out, w_up)
    small = jnp.concatenate([time_table, vec])
    small_side = swap(small, "y")
    (small_two,) = move([((2, 144, 128), [(small, (), 0), (small_side, (), 1)])])
    small_far = swap(small_two, "z2")
    pieces = [Piece(parts_first, (i,)) for i in range(3)]
    near = swap(parts_first, "z1")
    for piece in pieces:
        piece.move_z1(near, piece.index)

    def tick(*jobs, extra=(), passing=()):
        stages = {
            "z": ("two", "move_z2"), "y": ("four", "move_y"), "x": ("across_send", "move_x"), "c": ("core_send", "move_c"),
        }
        ready = [pieces[n] for stage, n in jobs if stage == "z" and pieces[n].pair is not None]
        jobs = [(pieces[n], *stages[stage]) for stage, n in jobs if stage != "z" or pieces[n].pair is None]
        made = move([getattr(p, make)() for p, make, _ in jobs] + list(extra), passing=passing)
        for (p, _, go), value in zip(jobs, made):
            getattr(p, go)(value)
        for p in ready:
            p.move_z2(p.pair)
        return made[len(jobs) :]

    extra = [((4, 144, 128), [(small_two, (), slice(0, 2)), (small_far, (), slice(2, 4))])]
    (small_four,) = tick(("z", 0), ("z", 1), extra=extra)
    small_near = swap(small_four, "z1")
    table, vec, up_b, scale = small_params(where, small_four, small_near, times)
    gain_one, bias_one, out_b, gain_two, bias_two, down_b = (vec[i : i + 1] for i in range(6))
    scale = scale.reshape(seqs, 1, -1)
    scaled = first_norm(tokens, gain_one, bias_one, scale)
    everything = slice(None)
    owns = [
        [(w_qkv, [(everything, pl.ds(0, 2048))], [0], 2048)],
        [(w_qkv, [(everything, pl.ds(2048, 1024))], [0], 1024), (w_out, [(everything, everything)], [1024], 1024)],
    ]
    for half in range(2):
        reads = [(everything, pl.ds(s * 512 + half * 256, 256)) for s in range(8)]
        owns.append([(w_up, reads, [s * 256 for s in range(8)], 256)])
    for half in range(2):
        reads = [(pl.ds(half * 256 + i * 128, 128), everything) for i in range(2)]
        owns.append([(w_down, reads, [0, 1024], 1024)])

    def whole(n):
        return (assemble(where, pieces[n], owns[n]))

    tick(("y", 0))
    (parts_other,) = simple(own_other_kernel, (w_up, w_down), [((3, 128, CW), LOW)], where=where)
    pieces += [Piece(parts_other, (i,), i >= 1) for i in range(3)]
    near_other = swap(parts_other, "z1")
    for i in range(3):
        pieces[3 + i].move_z1(near_other, (i,))
    pairs = tick(("x", 0), ("y", 1), ("z", 2), extra=[pieces[i].two() for i in range(3, 6)])
    for i in range(3):
        pieces[3 + i].pair = pairs[i]
    tick(("c", 0), ("x", 1), ("y", 2), ("z", 3))
    w_qk = whole(0)
    tick(("c", 1), ("x", 2), ("y", 3), ("z", 4))
    qk = (project(scaled, w_qk))
    vo = whole(1)
    begun = (attend(scaled, qk, vo, length, 0, 2))
    tick(("c", 2), ("x", 3), ("y", 4), ("z", 5))
    v, probs, mix = (attend(scaled, qk, vo, length, 2, 2, begun))
    middle, hidden = (second_norm(mix, tokens, vo, out_b, gain_two, bias_two))
    up_a = whole(2)
    tick(("c", 3), ("x", 4), ("y", 5))
    act_a, slope_a = (up(hidden, up_a, up_b[0:1]))
    up_b_w = whole(3)
    tick(("c", 4), ("x", 5))
    act_b, slope_b = (up(hidden, up_b_w, up_b[1:2]))
    def step(*jobs, passing=(), cost=0):
        lists = [getattr(r, stage)() for r, stage in jobs]
        made = add_up([item for items in lists for item in items], passing=passing, cost=cost)
        for (r, stage), items in zip(jobs, lists, strict=True):
            values, made = made[: len(items)], made[len(items) :]
            go = "go_last" if stage == "last_direct" else "go_" + stage
            getattr(r, go)(*values)
        return made

    acts = (act_a, act_b)
    downs = [whole(4)]
    away = (tall_away(where, acts, cotangent))
    (away,) = tick(("c", 5), passing=(away,))
    core_one = swap(away, "c")
    d_pre, up_sum_a = (pull(cotangent, downs[0], slope_a, 0))
    downs.append(whole(5))
    xa, yb, *keep = (tall_mine(where, acts, cotangent, core_one))
    one = Reduction(*keep)
    one.go_first(xa, yb)
    d_pre, up_sum_b = (pull(cotangent, downs[1], slope_b, 1, d_pre))
    pairs_two = [(hidden, d_pre, "layer")]
    core_two = swap((row_away(where, pairs_two)), "c")
    d_middle, d_low, d_mix, sums_two = (
        middle_back(d_pre, (up_a, up_b_w), middle, cotangent, gain_two, vo)
    )
    step((one, "second"), cost=42000000000)
    xa, yb, *keep = (row_mine(where, pairs_two, core_two))
    two = Reduction(*keep)
    two.go_first(xa, yb)
    d_packed = (attend_back(d_mix, probs, qk, v, length))
    step((one, "third"), cost=42000000000)
    pairs_three = [(scaled, d_packed, "layers"), (mix, d_low, "columns")]
    core_three = swap(row_away(where, pairs_three), "c")
    step((two, "second"), cost=38000000000)
    *sends, ka, kb = (row_mine(where, pairs_three, core_three))
    three = Reduction(ka, kb)
    three.go_first(*step((two, "third"), passing=sends))
    grad_tokens, sums_one, d_emb = (
        input_back(d_packed, w_qk, vo, tokens, d_middle, gain_one, bias_one, scale)
    )
    block_out = down(acts, downs, middle, down_b, 0, 2)
    step((one, "fourth"))
    simple(pause_kernel, (), [], cost=10000000000)
    step((three, "second"))
    (rows,) = (
        simple(
            rows_kernel,
            (d_emb, sums_one, sums_two, up_sum_a, up_sum_b, jnp.pad(time_index.astype(F32), (0, 120))[None]),
            [((32, 24, 128), F32)],
        )
    )
    got = lax.all_to_all(rows, BOTH, 0, 0)
    step((two, "fourth"), (three, "third_direct"))
    block_out = down(acts, downs, middle, down_b, 2, 2, (block_out,))
    (early,) = add_up([join(one, two)])
    early_x = swap(early, "x")
    grad_table, sums = (
        simple(table_kernel, (got,), [((128, 128), F32), ((16, 128), F32)])
    )
    (late,) = add_up(three.last_direct(), cost=10000000000)
    late_x = swap(late, "x")
    (packed,) = add_up([pack_last(early, early_x, late)])
    other = swap(packed, "c")
    (down_shard,) = shard_of(tall_shard_kernel, where, (early, early_x, other), [(512, 1024)])
    (up_shard,) = shard_of(up_shard_kernel, where, (early, early_x, other), [(128, 4096)])
    (late_x,) = simple(pause_kernel, (), [], passing=(late_x,))
    late_corner = swap(late_x, "c")
    qkv_shard, out_shard = shard_of(
        qkv_shard_kernel, where, (late, late_x, other, late_corner), [(128, 3072), (128, 1024)]
    )
    return (
        block_out, grad_tokens, grad_table, sums[0], sums[1], qkv_shard, out_shard, sums[2], sums[3], sums[4],
        up_shard, sums[6:10].reshape(512), down_shard, sums[5],
    )


def solution(mesh):
    in_specs = (
        P(("fsdp", "dp"), None),
        P(("fsdp", "dp")),
        P(None, "fsdp"),
        P("fsdp"),
        P("fsdp"),
        P("fsdp", None),
        P("fsdp", None),
        P("fsdp"),
        P("fsdp"),
        P("fsdp"),
        P("fsdp", None),
        P("fsdp"),
        P("fsdp", None),
        P("fsdp"),
        P(("fsdp", "dp"), None),
    )
    out_specs = (
        P(("fsdp", "dp"), None),
        P(("fsdp", "dp"), None),
        P(None, "fsdp"),
        P("fsdp"),
        P("fsdp"),
        P("fsdp", None),
        P("fsdp", None),
        P("fsdp"),
        P("fsdp"),
        P("fsdp"),
        P("fsdp", None),
        P("fsdp"),
        P("fsdp", None),
        P("fsdp"),
    )
    local = eight_by_four if (mesh.shape["fsdp"], mesh.shape["dp"]) == (8, 4) else plain
    return jax.shard_map(local, mesh=mesh, in_specs=in_specs, out_specs=out_specs, check_vma=False)
```

```python
import functools

import jax
import jax.numpy as jnp
from jax import lax
from jax.experimental import pallas as pl
from jax.experimental.pallas import tpu as pltpu
from jax.sharding import PartitionSpec as P

HEADS = 16
BOTH = ("fsdp", "dp")
LOW = jnp.bfloat16
F32 = jnp.float32
NT = (((1,), (1,)), ((), ()))
TN = (((0,), (0,)), ((), ()))


def flips(which):
    pairs = []
    for f in range(8):
        for d in range(4):
            z, y, x, c = f // 2, f % 2, d // 2, d % 2
            if which == "x":
                x = 1 - x
            elif which == "y":
                y = 1 - y
            elif which == "c":
                c = 1 - c
            elif which == "z1":
                z = z ^ 1
            elif which == "z2":
                z = z ^ 2
            elif which == "z3":
                z = z ^ 3
            pairs.append((f * 4 + d, (z * 2 + y) * 4 + x * 2 + c))
    return pairs


def swap(values, which):
    return lax.ppermute(values, BOTH, flips(which))


def coords():
    f, d = lax.axis_index("fsdp"), lax.axis_index("dp")
    return f // 2, f % 2, d // 2, d % 2


def call(kernel, grid, ins, outs, flops=0, nbytes=0, scratch=(), prefetch=0, aliases=None, limit=18, pin=(), pin_out=(), cost=0
):
    after = tuple(chain)

    def spec(block, index):
        if block is None:
            return pl.BlockSpec(memory_space=pl.ANY)
        if block == "hbm":
            return pl.BlockSpec(memory_space=pltpu.MemorySpace.HBM)
        if index in constant and grid:
            return pl.BlockSpec(block, index, pipeline_mode=pl.Buffered(1))
        return pl.BlockSpec(block, index)

    def body(*refs):
        n = prefetch + len(ins)
        m = n + len(after) + len(outs)
        kernel(*refs[:n], *refs[n + len(after) : m], *refs[m + 1 :])

    run = pl.pallas_call(
        body,
        out_shape=[
            pltpu.MemorySpace.HBM(shape, kind) if k in pin_out else jax.ShapeDtypeStruct(shape, kind)
            for k, (shape, kind, _, _) in enumerate(outs)
        ]
        + [pltpu.MemorySpace.HBM((8, 128), F32)],
        grid_spec=pltpu.PrefetchScalarGridSpec(
            num_scalar_prefetch=prefetch,
            grid=grid,
            in_specs=[spec(block, index) for block, index in ins] + [spec(None, None)] * len(after),
            out_specs=[spec(block, index) for _, _, block, index in outs] + [spec(None, None)],
            scratch_shapes=scratch,
        ),
        input_output_aliases=aliases or {},
        compiler_params=pltpu.CompilerParams(
            vmem_limit_bytes=limit * 2**20, dimension_semantics=("arbitrary",) * len(grid)
        ),
        cost_estimate=pl.CostEstimate(flops=cost, bytes_accessed=1024, transcendentals=0),
    )

    def pinned(*args):
        args = [
            pltpu.with_memory_space_constraint(a, pltpu.MemorySpace.HBM) if k - prefetch in pin else a
            for k, a in enumerate(args)
        ]
        *values, token = run(*args, *(pltpu.with_memory_space_constraint(t, pltpu.MemorySpace.HBM) for t in after))
        chain[:] = [token]
        return values

    return pinned


def simple(kernel, args, outs, where=None, passing=(), limit=12, pin_out=(), cost=0):
    def whole(shape):
        return shape, lambda *_: (0,) * len(shape)

    prefetch = 0 if where is None else 1
    n_in, n_out, n_pass = len(args), len(outs), len(passing)

    def body(*refs):
        first = prefetch + n_in
        kernel(*refs[:first], *refs[first + n_pass : first + n_pass + n_out])

    run = call(
        body,
        (),
        [whole(a.shape) for a in args] + [(None, None)] * n_pass,
        [(shape, kind, *whole(shape)) for shape, kind in outs] + [(a.shape, a.dtype, None, None) for a in passing],
        prefetch=prefetch,
        aliases={prefetch + n_in + k: n_out + k for k in range(n_pass)},
        limit=limit,
        pin_out=pin_out,
        cost=cost,
    )
    return run(*(() if where is None else (where,)), *args, *passing)


constant = []
chain = []


def fixed(*index):
    constant.append(lambda *grid: index)
    return constant[-1]


def ends(n):
    e = n * 3 // 8
    return e // 2, (n - 2 * e) // 2


def end_start(n, x, c):
    eh, mh = ends(n)
    return x * (n - 2 * eh) + c * eh


def middle_start(n, c):
    eh, mh = ends(n)
    return 2 * eh + c * mh


COLS = 2048
CE, CM = ends(COLS)
CW = CE + CM


def lanes(start, size=128):
    return pl.ds(start if isinstance(start, int) else pl.multiple_of(start, 128), size)


def own_columns(where, dest, read):
    x, c = where[2], where[3]
    for i in range(CW // 128):
        start = end_start(COLS, x, c) + i * 128 if i < CE // 128 else middle_start(COLS, c) + i * 128 - CE
        dest[:, i * 128 : (i + 1) * 128] = read(start)


def own_up(where, up_w, half):
    return lambda start: up_w[:, lanes((start // 256) * 512 + half * 256 + start % 256)]


def own_first_kernel(where, qkv, out_w, up_w, parts, sems):
    x, c = where[2], where[3]
    copies = []
    for piece in range(3):
        for i in range(CW // 128):
            start = end_start(COLS, x, c) + i * 128 if i < CE // 128 else middle_start(COLS, c) + i * 128 - CE
            dest = parts.at[piece, :, i * 128 : (i + 1) * 128]
            sem = sems.at[piece * (CW // 128) + i]
            if piece == 1:
                value = pltpu.make_async_copy(qkv.at[:, lanes(2048 + jnp.minimum(start, 896))], dest, sem)
                other = pltpu.make_async_copy(out_w.at[:, lanes(jnp.maximum(start - 1024, 0))], dest, sem)
                pl.when(start < 1024)(value.start)
                pl.when(start >= 1024)(other.start)
                copies.append(value)
                continue
            if piece == 0:
                source = qkv.at[:, lanes(start)]
            else:
                source = up_w.at[:, lanes((start // 256) * 512 + start % 256)]
            copies.append(pltpu.make_async_copy(source, dest, sem))
            copies[-1].start()
    for copy in copies:
        copy.wait()


def own_first(where, qkv, out_w, up_w):
    shape = (3, 128, CW)
    return call(
        own_first_kernel,
        (),
        [("hbm", None)] * 3,
        [(shape, LOW, shape, lambda *_: (0, 0, 0))],
        prefetch=1,
        scratch=[pltpu.SemaphoreType.DMA((3 * (CW // 128),))],
        limit=8,
        pin=(0, 1, 2),
    )(where, qkv, out_w, up_w)


def own_other_kernel(where, up_w, down_w, parts):
    own_columns(where, parts.at[0], own_up(where, up_w, 1))
    for half in range(2):
        own_columns(
            where,
            parts.at[1 + half],
            lambda start: down_w[
                pl.ds(pl.multiple_of(half * 256 + (start // 1024) * 128, 128), 128), lanes(start % 1024)
            ],
        )


def move(jobs, passing=()):
    args = []
    for _, copies in jobs:
        for array, _, _ in copies:
            if not any(array is a for a in args):
                args.append(array)

    def kernel(*refs):
        outs = refs[len(args) :]
        for out, (_, copies) in zip(outs, jobs, strict=True):
            for array, read, write in copies:
                ref = refs[[i for i, a in enumerate(args) if a is array][0]]
                out[write] = ref[read if read != () else ...]

    return simple(kernel, args, [(shape, LOW) for shape, _ in jobs], passing=passing)


class Piece:
    def __init__(self, part, index, tall=False):
        self.part, self.index, self.tall = part, index, tall
        self.shape = (128, CW)
        self.pair = None

    def two(self):
        return (2, *self.shape), [(self.part, self.index, 0), (self.near, self.near_index, 1)]

    def four(self):
        return (4, *self.shape), [
            (self.part, self.index, 0),
            (self.near, self.near_index, 1),
            (self.far, slice(None), slice(2, 4)),
        ]

    def blocks(self):
        found = [(self.near, self.near_index)] + [(self.far, (i,)) for i in range(2)]
        return found + [(self.beside, (i,)) for i in range(4)]

    def across_send(self):
        end = (slice(None), slice(0, CE))
        return (7, 128, CE), [(a, (*i, *end), j) for j, (a, i) in enumerate(self.blocks())]

    def core_send(self):
        first, last = (slice(None), slice(0, CW)), (slice(None), slice(CW, CW + CE))
        copies = [(a, i, (j, *first)) for j, (a, i) in enumerate(self.blocks())]
        return (7, 128, CW + CE), copies + [(self.across, j, (j, *last)) for j in range(7)]

    def move_z1(self, near, near_index):
        self.near, self.near_index = near, near_index

    def move_z2(self, two):
        self.far = swap(two, "z2")

    def move_y(self, four):
        self.beside = swap(four, "y")

    def move_x(self, send):
        self.across = swap(send, "x")

    def move_c(self, send):
        self.other = swap(send, "c")


def assemble_kernel(tall, own_copies, near_index, where, *refs):
    n_own = len(own_copies)
    owns = refs[:n_own]
    near, far, beside, across, other, out, sems = refs[n_own:]
    z, y, x, c = where[0], where[1], where[2], where[3]
    eh, mh = CE, CM

    def at(shard, start, count):
        if not tall:
            return out.at[pl.ds(pl.multiple_of(shard * 128, 128), 128), lanes(start, count)]
        row = shard * 256 + (start // 1024) * 128
        return out.at[pl.ds(pl.multiple_of(row, 128), 128), lanes(start % 1024, count)]

    def cut(block, start, count):
        return block.at[:, pl.ds(start, count)]

    copies = []
    for j in range(8):
        shard = (z ^ (j % 4)) * 2 + (y if j < 4 else 1 - y)
        if j == 0:
            for ref, (read, start, count) in zip(owns, own_copies, strict=True):
                for k in range(len(read)):
                    copies.append((ref.at[read[k]], at(shard, start[k], count)))
            continue
        close = near.at[near_index[0]] if near_index else near
        mine = (close, far.at[0], far.at[1], beside.at[0], beside.at[1], beside.at[2], beside.at[3])[j - 1]
        oc = 1 - c
        copies += [
            (cut(mine, 0, eh), at(shard, end_start(COLS, x, c), eh)),
            (cut(mine, eh, mh), at(shard, middle_start(COLS, c), mh)),
            (cut(across.at[j - 1], 0, eh), at(shard, end_start(COLS, 1 - x, c), eh)),
            (cut(other.at[j - 1], 0, eh), at(shard, end_start(COLS, x, oc), eh)),
            (cut(other.at[j - 1], eh, mh), at(shard, middle_start(COLS, oc), mh)),
            (cut(other.at[j - 1], eh + mh, eh), at(shard, end_start(COLS, 1 - x, oc), eh)),
        ]
    copies = [pltpu.make_async_copy(s, d, sems.at[k]) for k, (s, d) in enumerate(copies)]
    for copy in copies:
        copy.start()
    for copy in copies:
        copy.wait()


def assemble(where, piece, owns):
    shape = (2048, 1024) if piece.tall else (1024, COLS)
    args = [o[0] for o in owns] + [piece.near, piece.far, piece.beside, piece.across, piece.other]
    n_copies = 42 + sum(len(o[1]) for o in owns)
    return call(
        functools.partial(assemble_kernel, piece.tall, [o[1:] for o in owns], piece.near_index),
        (),
        [(None, None)] * len(args),
        [(shape, LOW, shape, lambda *_: (0, 0))],
        prefetch=1,
        scratch=[pltpu.SemaphoreType.DMA((n_copies,))],
        limit=8,
    )(where, *args)[0]


def small_kernel(where, four, beside, time_index, table, vec, up_b, scale):
    z, y = where[0], where[1]
    for j in range(8):
        block = four.at[j] if j < 4 else beside.at[j - 4]
        shard = (z ^ (j // 4 + j // 2 % 2 * 2)) * 2 + (y ^ (j % 2))
        table[:, lanes(shard * 128)] = block[:128, :]
        vec[:, lanes(shard * 128)] = block[128:, :].astype(F32)
        for row in range(4):
            unit = lanes(shard * 256 + (row % 2) * 128)
            up_b[row // 2 : row // 2 + 1, unit] = block[134 + row : 135 + row, :].astype(F32)
    numbers = lax.broadcasted_iota(jnp.int32, (time_index.shape[0], 128), 1)
    one_hot = (numbers == time_index[...]).astype(F32).astype(LOW)
    scale[...] = 1.0 + jnp.dot(one_hot, table[...], preferred_element_type=F32)


def small_params(where, four, beside, time_index):
    return simple(
        small_kernel,
        (four, beside, time_index),
        [((128, 1024), LOW), ((16, 1024), F32), ((2, 2048), F32), ((time_index.shape[0], 1024), F32)],
        where=where,
    )


def rows_kernel(d_emb, sums_one, sums_two, up_a, up_b, times, out):
    for s in range(8):
        here = slice(s * 128, (s + 1) * 128)
        rows = [d_emb[i, :, here] for i in range(8)]
        rows += [sums_one[0:2, here], sums_two[2:3, here], sums_two[0:2, here], sums_two[3:4, here]]
        for sums in (up_a, up_b):
            rows += [sums[:, s * 256 + j * 128 : s * 256 + (j + 1) * 128] for j in range(2)]
        rows += [times[...], jnp.zeros((5, 128), F32)]
        block = jnp.concatenate(rows, axis=0)
        for copy in range(4):
            out[s * 4 + copy] = block


def mm(a, b):
    return jnp.dot(a, b, preferred_element_type=F32)


def mm_nt(a, b):
    return lax.dot_general(a, b, NT, preferred_element_type=F32)


def mm_tn(a, b):
    return lax.dot_general(a, b, TN, preferred_element_type=F32)


def centre(values):
    mean = jnp.mean(values, axis=-1, keepdims=True)
    centred = values - mean
    scale = lax.rsqrt(jnp.mean(centred * centred, axis=-1, keepdims=True) + 1e-05)
    return centred * scale, scale


def first_norm_kernel(tokens, gain, bias, scale, scaled):
    hat, _ = centre(tokens[...].astype(F32))
    scaled[...] = ((hat * gain[...] + bias[...]) * scale[0]).astype(LOW)


def first_norm(tokens, gain, bias, scale):
    rows, width = tokens.shape
    seqs = scale.shape[0]
    length = rows // seqs
    return call(
        first_norm_kernel,
        (seqs,),
        [
            ((length, width), lambda i: (i, 0)),
            ((1, width), fixed(0, 0)),
            ((1, width), fixed(0, 0)),
            ((1, 1, width), lambda i: (i, 0, 0)),
        ],
        [((rows, width), LOW, (length, width), lambda i: (i, 0))],
    )(tokens, gain, bias, scale)[0]


def halves(values):
    lane = lax.broadcasted_iota(jnp.int32, values.shape, 1)
    zero = jnp.zeros_like(values)
    return jnp.concatenate([jnp.where(lane < 64, values, zero), jnp.where(lane < 64, zero, values)], axis=0)


def side(values):
    n = values.shape[0] // 2
    return jnp.concatenate([values[:n], values[n:]], axis=1)


def project_kernel(x, w, out):
    out[...] = mm(x[...], w[...]).astype(LOW)


def project(x, w, tile=512):
    rows, width = x.shape
    n = w.shape[1]
    return call(
        project_kernel,
        (n // tile,),
        [((rows, width), fixed(0, 0)), ((width, tile), lambda i: (0, i))],
        [((rows, n), LOW, (rows, tile), lambda i: (0, i))],
    )(x, w)[0]


def units_of(rows, length, at_once=8):
    units = []
    for seq in range(rows // length):
        for pair in range(2):
            units.append((seq, pair, (slice(seq * length, (seq + 1) * length), slice(pair * 128, (pair + 1) * 128))))
    return [units[i : i + at_once] for i in range(0, len(units), at_once)]


def attend_kernel(length, scaled, wv, q_in, k_in, *refs):
    v_out, probs_out, mix_out = refs[-3:]
    factor = 64 ** (-0.5) * 1.4426950408889634
    v_out[...] = mm(scaled[...], wv[...]).astype(LOW)
    for units in units_of(scaled.shape[0], length):
        scores = [mm_nt(halves(q_in[here]), k_in[here]) for _, _, here in units]
        found = []
        for s in scores:
            e = jnp.exp2((s - jnp.max(s, axis=-1, keepdims=True)) * factor)
            found.append((e * (1.0 / jnp.sum(e, axis=-1, keepdims=True))).astype(LOW))
        for (seq, pair, here), probs in zip(units, found, strict=True):
            probs_out[0, seq, pair] = probs
            mix_out[here] = mm(side(probs), halves(v_out[here])).astype(LOW)


def attend(scaled, qk, vo, length, first=0, count=None, earlier=()):
    rows, width = scaled.shape
    groups = width // 256
    seqs = rows // length
    count = groups if count is None else count
    column = lambda i: (0, first + i)
    wide = ((rows, width), LOW, (rows, 256), column)
    probs = (groups, seqs, 2, 2 * length, length)
    return call(
        functools.partial(attend_kernel, length),
        (count,),
        [
            ((rows, width), fixed(0, 0)),
            ((width, 256), column),
            ((rows, 256), column),
            ((rows, 256), lambda i: (0, groups + first + i)),
        ]
        + [(None, None)] * len(earlier),
        [wide, (probs, LOW, (1, *probs[1:]), lambda i: (first + i, 0, 0, 0, 0)), wide],
        aliases={4 + i: i for i in range(len(earlier))},
    )(scaled, vo, qk, qk, *earlier)


def middle_kernel(mix, tokens, w, out_b, gain, bias, middle_out, hidden_out):
    middle = tokens[...].astype(F32) + mm(mix[...], w[...]) + out_b[...]
    middle_out[...] = middle
    hat, _ = centre(middle)
    hidden_out[...] = (hat * gain[...] + bias[...]).astype(LOW)


def second_norm(mix, tokens, vo, out_b, gain, bias):
    rows, width = tokens.shape
    row = lambda i: (i, 0)
    vec = ((1, width), fixed(0, 0))
    return call(
        middle_kernel,
        (rows // 256,),
        [((256, width), row), ((256, width), row), ((width, width), fixed(0, 1)), vec, vec, vec],
        [((rows, width), F32, (256, width), row), ((rows, width), LOW, (256, width), row)],
    )(mix, tokens, vo, out_b, gain, bias)


def gelu_parts(v):
    cdf = 0.5 + 0.5 * lax.erf(v * 0.5**0.5)
    bell = jnp.exp(-0.5 * v * v)
    return v * cdf, cdf + (v * 0.3989422804014327) * bell


def up_kernel(hidden, w, bias, act, slope):
    value, pull = gelu_parts(mm(hidden[...], w[...]) + bias[...])
    act[...] = value.astype(LOW)
    slope[...] = pull.astype(LOW)


def up(hidden, w, bias, tile=512):
    rows, width = hidden.shape
    n = w.shape[1]
    column = lambda i: (0, i)
    return call(
        up_kernel,
        (n // tile,),
        [((rows, width), fixed(0, 0)), ((width, tile), column), ((1, tile), column)],
        [((rows, n), LOW, (rows, tile), column)] * 2,
        limit=22,
        pin_out=(1,),
    )(hidden, w, bias)


def down_kernel(act_a, act_b, first, second, middle, bias, *refs):
    total = middle[...] + bias[...]
    total += mm(act_a[...], first[...])
    total += mm(act_b[...], second[...])
    refs[-1][...] = total.astype(LOW)


def down(acts, ws, middle, bias, start, count, earlier=(), tile=256):
    rows, width = middle.shape
    k = ws[0].shape[0]
    row = lambda i: (start + i, 0)
    return call(
        down_kernel,
        (count,),
        [((tile, k), row)] * 2
        + [((k, width), fixed(0, 0))] * 2
        + [((tile, width), row), ((1, width), fixed(0, 0))]
        + [(None, None)] * len(earlier),
        [((rows, width), LOW, (tile, width), row)],
        aliases={6 + i: i for i in range(len(earlier))},
        limit=56,
    )(*acts, *ws, middle, bias, *earlier)[0]


def pull_kernel(cot, w, slope, *refs):
    d_pre, sums = refs[-2:]
    value = (mm_nt(cot[...], w[...]) * slope[...].astype(F32)).astype(LOW)
    d_pre[0] = value
    sums[...] = jnp.sum(value.astype(F32), axis=0, keepdims=True)


def pull(cot, w, slope, half, earlier=None, tile=512):
    rows, width = cot.shape
    n = w.shape[0]
    column = lambda i: (0, i)
    ins = [((rows, width), fixed(0, 0)), ((tile, width), lambda i: (i, 0)), ((rows, tile), column)]
    return call(
        pull_kernel,
        (n // tile,),
        ins + ([] if earlier is None else [(None, None)]),
        [((2, rows, n), LOW, (1, rows, tile), lambda i: (half, 0, i)), ((1, n), F32, (1, tile), column)],
        aliases={} if earlier is None else {3: 0},
        pin=(2,),
    )(cot, w, slope, *(() if earlier is None else (earlier,)))


def norm_back(d_out, hat, scale, gain):
    e = d_out * gain
    mean = jnp.mean(e, axis=-1, keepdims=True)
    slant = jnp.mean(e * hat, axis=-1, keepdims=True)
    return (e - mean - hat * slant) * scale


def fold(*rows_of):
    sums = [jnp.sum(v, axis=0, keepdims=True) for v in rows_of]
    return jnp.concatenate(sums + [jnp.zeros_like(sums[0])] * (8 - len(sums)), axis=0)


def middle_back_kernel(d_pre, wa, wb, middle, cot, gain, w_out, d_middle_out, d_low_out, d_mix_out, sums):
    d_hidden = mm_nt(d_pre[0], wa[...]) + mm_nt(d_pre[1], wb[...])
    hat, scale = centre(middle[...])
    d_middle = cot[...].astype(F32) + norm_back(d_hidden, hat, scale, gain[...])
    d_middle_out[...] = d_middle
    d_low = d_middle.astype(LOW)
    d_low_out[...] = d_low
    d_mix_out[...] = mm_nt(d_low, w_out[...]).astype(LOW)

    @pl.when(pl.program_id(0) == 0)
    def _():
        sums[...] = jnp.zeros_like(sums)

    sums[...] += fold(d_hidden * hat, d_hidden, d_low.astype(F32), cot[...].astype(F32))


def middle_back(d_pre, ws, middle, cot, gain, vo, tile=256):
    rows, width = middle.shape
    row = lambda i: (i, 0)
    return call(
        middle_back_kernel,
        (rows // tile,),
        [
            ((2, tile, d_pre.shape[2]), lambda i: (0, i, 0)),
            (ws[0].shape, fixed(0, 0)),
            (ws[1].shape, fixed(0, 0)),
            ((tile, width), row),
            ((tile, width), row),
            ((1, width), fixed(0, 0)),
            ((width, width), fixed(0, 1)),
        ],
        [
            ((rows, width), F32, (tile, width), row),
            ((rows, width), LOW, (tile, width), row),
            ((rows, width), LOW, (tile, width), row),
            ((8, width), F32, (8, width), fixed(0, 0)),
        ],
        limit=32,
    )(d_pre, *ws, middle, cot, gain, vo)


def attend_back_kernel(length, d_mix, probs, q_in, k_in, v_in, *refs):
    out = refs[-1]
    factor = 64 ** (-0.5)
    for units in units_of(d_mix.shape[0], length, 8):
        dms = [halves(d_mix[here]) for _, _, here in units]
        d_probs = [mm_nt(dm, v_in[here]) for dm, (_, _, here) in zip(dms, units, strict=True)]
        found = []
        for d, (seq, pair, _) in zip(d_probs, units, strict=True):
            high = probs[0, seq, pair].astype(F32)
            found.append((high * (d - jnp.sum(d * high, axis=-1, keepdims=True))).astype(LOW))
        for dm, d_scores, (seq, pair, here) in zip(dms, found, units, strict=True):
            out[(2, *here)] = mm_tn(probs[0, seq, pair], dm).astype(LOW)
            out[(0, *here)] = (mm(side(d_scores), halves(k_in[here])) * factor).astype(LOW)
            out[(1, *here)] = (mm_tn(d_scores, halves(q_in[here])) * factor).astype(LOW)


def attend_back(d_mix, probs, qk, v, length, first=0, count=None, earlier=()):
    rows, width = d_mix.shape
    count = width // 256 if count is None else count
    wide = ((rows, 256), lambda i: (0, first + i))
    return call(
        functools.partial(attend_back_kernel, length),
        (count,),
        [
            wide,
            ((1,) + probs.shape[1:], lambda i: (first + i, 0, 0, 0, 0)),
            wide,
            ((rows, 256), lambda i: (0, width // 256 + first + i)),
            wide,
        ]
        + [(None, None)] * len(earlier),
        [((3, rows, width), LOW, (3, rows, 256), lambda i: (0, 0, first + i))],
        aliases={5 + i: i for i in range(len(earlier))},
    )(d_mix, probs, qk, qk, v, *earlier)[0]


def input_back_kernel(length, d, wq, wk, wv, tokens, d_middle, gain, bias, scale, out, sums, d_emb):
    d_scaled = mm_nt(d[0], wq[...]) + mm_nt(d[1], wk[...]) + mm_nt(d[2], wv[...])
    hat, spread = centre(tokens[...].astype(F32))
    normed = hat * gain[...] + bias[...]
    count = tokens.shape[0] // length
    parts = []
    for i in range(count):
        here = slice(i * length, (i + 1) * length)
        d_emb[i] = jnp.sum(d_scaled[here] * normed[here], axis=0, keepdims=True)
        parts.append(d_scaled[here] * scale[i])
    d_normed = jnp.concatenate(parts, axis=0)
    out[...] = (d_middle[...] + norm_back(d_normed, hat, spread, gain[...])).astype(LOW)

    @pl.when(pl.program_id(0) == 0)
    def _():
        sums[...] = jnp.zeros_like(sums)

    sums[...] += fold(d_normed * hat, d_normed)


def input_back(d_packed, qk, vo, tokens, d_middle, gain, bias, scale, tile=256, cost=0):
    rows, width = tokens.shape
    seqs = scale.shape[0]
    length = rows // seqs
    row = lambda i: (i, 0)
    wide = ((tile, width), row)
    vec = ((1, width), fixed(0, 0))
    some = ((tile // length, 1, width), lambda i: (i, 0, 0))
    return call(
        functools.partial(input_back_kernel, length),
        (rows // tile,),
        [
            ((3, tile, width), lambda i: (0, i, 0)),
            ((width, width), fixed(0, 0)),
            ((width, width), fixed(0, 1)),
            ((width, width), fixed(0, 0)),
            wide, wide, vec, vec, some,
        ],
        [
            ((rows, width), LOW, (tile, width), row),
            ((8, width), F32, (8, width), fixed(0, 0)),
            ((seqs, 1, width), F32) + some,
        ],
        cost=cost,
        limit=26,
    )(d_packed, qk, qk, vo, tokens, d_middle, gain, bias, scale)


def tall_parts(where, a, b, cot, yy):
    here = slice(yy * 256, (yy + 1) * 256)
    value = mm_tn(jnp.concatenate([a[:, here], b[:, here]], axis=1), cot[...])
    x = where[2]
    found = []
    for xr in range(2):
        pair = []
        for half in range(2):
            low, high = value[half * 256 : half * 256 + 128], value[half * 256 + 128 : half * 256 + 256]
            pair.append(jnp.where((x ^ xr) == 0, low, high))
        found.append(pair)
    return found


def tall_away_kernel(where, a, b, cot, away):
    for yy in range(2):
        found = tall_parts(where, a, b, cot, yy)
        for xr in range(2):
            for half in range(2):
                away[xr, yy ^ where[1], 0, half] = found[xr][half].astype(LOW)


def tall_ins(acts, cot, core):
    rows, width = cot.shape
    act = ((rows, 512), lambda zr, where: (0, zr ^ where[0]))
    return [act, act, ((rows, width // 2), lambda zr, where: (0, where[3] ^ core))]


def tall_away(where, acts, cot):
    n = cot.shape[1] // 2
    return call(
        tall_away_kernel,
        (4,),
        tall_ins(acts, cot, 1),
        [((2, 2, 4, 2, 128, n), LOW, (2, 2, 1, 2, 128, n), lambda zr, where: (0, 0, zr, 0, 0, 0))],
        prefetch=1,
    )(where, *acts, cot)[0]


def tall_mine_kernel(where, a, b, cot, core, xa, yb, ka, kb):
    far = pl.program_id(0) >= 2
    for yy in range(2):
        found = tall_parts(where, a, b, cot, yy)
        yr = yy ^ where[1]
        sums = []
        for xr in range(2):
            sums.append([(found[xr][h] + core[xr, yr, 0, h].astype(F32)).astype(LOW) for h in range(2)])

        @pl.when(jnp.logical_not(far))
        def _(sums=sums, yr=yr):
            for half in range(2):
                ka[yr, 0, half] = sums[0][half]
                xa[yr, 0, half] = sums[1][half]

        @pl.when(far & (yr == 0))
        def _(sums=sums):
            for xr in range(2):
                for half in range(2):
                    kb[xr, 0, half] = sums[xr][half]

        @pl.when(far & (yr == 1))
        def _(sums=sums):
            for xr in range(2):
                for half in range(2):
                    yb[xr, 0, half] = sums[xr][half]


def tall_mine(where, acts, cot, core):
    n = cot.shape[1] // 2
    shape = (2, 2, 2, 128, n)
    block = (2, 1, 2, 128, n)
    close = (shape, LOW, block, lambda zr, where: (0, jnp.minimum(zr, 1), 0, 0, 0))
    far = (shape, LOW, block, lambda zr, where: (0, jnp.maximum(zr - 2, 0), 0, 0, 0))
    return call(
        tall_mine_kernel,
        (4,),
        tall_ins(acts, cot, 0) + [((2, 2, 1, 2, 128, n), lambda zr, where: (0, 0, zr, 0, 0, 0))],
        [close, far, close, far],
        prefetch=1,
        pin=(3,),
    )(where, *acts, cot, core)


def row_value(step, lefts, rights, counts, hold):
    first = 0
    for left, right, count in zip(lefts, rights, counts, strict=True):

        def put(left=left, right=right):
            b = right[0] if len(right.shape) == 3 else right[...]
            hold[...] = mm_tn(left[...], b)

        if len(lefts) == 1:
            put()
        else:
            pl.when((step >= first) & (step < first + count))(put)
        first += count


def row_from(where, xr, yr, zr):
    start = ((where[0] ^ zr) * 2 + (where[1] ^ yr)) * 128 + (where[2] ^ xr) * 64
    return pl.ds(pl.multiple_of(start, 64), 64)


def row_away_kernel(counts, where, *refs):
    n = len(counts)
    lefts, rights, away, hold = refs[:n], refs[n : 2 * n], refs[2 * n], refs[2 * n + 1]
    row_value(pl.program_id(0), lefts, rights, counts, hold)
    for xr in range(2):
        for yr in range(2):
            for zr in range(4):
                away[xr, yr, zr] = hold[row_from(where, xr, yr, zr), :].astype(LOW)


def row_mine_kernel(counts, where, *refs):
    n = len(counts)
    lefts, rights = refs[:n], refs[n : 2 * n]
    core, xa, yb, ka, kb, hold = refs[2 * n :]
    row_value(pl.program_id(0), lefts, rights, counts, hold)
    for xr in range(2):
        for yr in range(2):
            for zr in range(4):
                total = hold[row_from(where, xr, yr, zr), :] + core[xr, yr, zr].astype(F32)
                total = total.astype(LOW)
                if zr < 2:
                    (ka if xr == 0 else xa)[yr, zr] = total
                else:
                    (kb if yr == 0 else yb)[xr, zr - 2] = total


def row_specs(pairs, core, tile):
    ins, counts = [], []
    for a, _, _ in pairs:
        ins.append((a.shape, lambda j, where: (0, 0)))
    first = 0
    for _, b, kind in pairs:
        tokens = b.shape[-2]
        if kind == "layers":
            count = b.shape[0] * (b.shape[2] // 2 // tile)
            each = b.shape[2] // 2 // tile
            spec = (
                (1, tokens, tile),
                lambda j, where, f=first, m=count, e=each: (
                    jnp.clip(j - f, 0, m - 1) // e,
                    0,
                    (where[3] ^ core) * e + jnp.clip(j - f, 0, m - 1) % e,
                ),
            )
        elif kind == "layer":
            count = b.shape[2] // tile
            spec = (
                (1, tokens, tile),
                lambda j, where, f=first, m=count: (where[3] ^ core, 0, jnp.clip(j - f, 0, m - 1)),
            )
        else:
            count = b.shape[1] // 2 // tile
            spec = (
                (tokens, tile),
                lambda j, where, f=first, m=count: (0, (where[3] ^ core) * m + jnp.clip(j - f, 0, m - 1)),
            )
        ins.append(spec)
        counts.append(count)
        first += count
    return ins, counts


def row_away(where, pairs, tile=512):
    ins, counts = row_specs(pairs, 1, tile)
    steps = sum(counts)
    return call(
        functools.partial(row_away_kernel, counts),
        (steps,),
        ins,
        [((2, 2, 4, 64, steps * tile), LOW, (2, 2, 4, 64, tile), lambda j, where: (0, 0, 0, 0, j))],
        prefetch=1,
        scratch=[pltpu.VMEM((1024, tile), F32)],
    )(where, *[a for a, _, _ in pairs], *[b for _, b, _ in pairs])[0]


def row_mine(where, pairs, core, tile=512):
    ins, counts = row_specs(pairs, 0, tile)
    steps = sum(counts)
    out = ((2, 2, 64, steps * tile), LOW, (2, 2, 64, tile), lambda j, where: (0, 0, 0, j))
    return call(
        functools.partial(row_mine_kernel, counts),
        (steps,),
        ins + [((2, 2, 4, 64, tile), lambda j, where: (0, 0, 0, 0, j))],
        [out] * 4,
        prefetch=1,
        scratch=[pltpu.VMEM((1024, tile), F32)],
        pin=(2 * len(pairs),),
    )(where, *[a for a, _, _ in pairs], *[b for _, b, _ in pairs], core)


def add_up(jobs, passing=(), cost=0):
    args, pieces = [], []
    parts = [job[1] if isinstance(job[1][0][0], list) else [(job[1], ...)] for job in jobs]

    def number(array, index):
        here = [k for k, a in enumerate(args) if a is array]
        if not here:
            args.append(array)
            here = [len(args) - 1]
        if (here[0], index) not in pieces:
            pieces.append((here[0], index))
        return pieces.index((here[0], index))

    parts = [[([number(*term) for term in terms], write) for terms, write in part] for part in parts]
    shapes = [jax.eval_shape(lambda a, index=index: a[index], args[k]).shape for k, index in pieces]
    n_in, n_out, n_pass = len(args), len(jobs), len(passing)

    def kernel(*refs):
        ins, outs = refs[:n_in], refs[n_in + n_pass : n_in + n_pass + n_out]
        *held, sems = refs[n_in + 2 * n_pass + n_out :]
        copies = []
        for k, (at, index) in enumerate(pieces):
            copies.append(pltpu.make_async_copy(ins[at].at[index], held[k], sems.at[k]))
            copies[-1].start()
        waited = set()
        for out, part in zip(outs, parts, strict=True):
            for terms, write in part:
                total = None
                for k in terms:
                    if k not in waited:
                        copies[k].wait()
                        waited.add(k)
                    value = held[k][...].astype(F32)
                    total = value if total is None else total + value
                out[write] = total.astype(LOW)

    def whole(shape):
        return shape, lambda *_: (0,) * len(shape)

    return call(
        kernel,
        (),
        [("hbm", None)] * n_in + [(None, None)] * n_pass,
        [(job[0], LOW, *whole(job[0])) for job in jobs] + [(a.shape, a.dtype, None, None) for a in passing],
        aliases={n_in + k: n_out + k for k in range(n_pass)},
        scratch=[pltpu.VMEM(shape, LOW) for shape in shapes] + [pltpu.SemaphoreType.DMA((len(pieces),))],
        cost=cost,
        limit=12,
    )(*args, *passing)


class Reduction:
    def __init__(self, ka, kb):
        self.ka, self.kb = ka, kb
        self.tail = ka.shape[2:]

    def go_first(self, xa, yb):
        self.xa, self.yb = swap(xa, "x"), swap(yb, "y")

    def second(self):
        shape = (2, *self.tail)
        return [(shape, [(self.ka, 1), (self.xa, 1)]), (shape, [(self.kb, 1), (self.yb, 1)])]

    def go_second(self, ya, xb):
        self.ya, self.xb = swap(ya, "y"), swap(xb, "x")

    def kept(self, i):
        return self.tail, [(self.ka, (0, i)), (self.xa, (0, i)), (self.ya, i)]

    def sent(self, i):
        return self.tail, [(self.kb, (0, i)), (self.yb, (0, i)), (self.xb, i)]

    def third(self):
        two = [((2, *self.tail), [(self.kb, 0), (self.yb, 0), (self.xb, slice(None))])]
        return two + [self.kept(0), self.kept(1)]

    def go_third(self, far, mine, next_one):
        self.far, self.mine, self.next_one = swap(far, "z2"), mine, next_one

    def fourth(self):
        return [(self.tail, [(self.next_one, slice(None)), (self.far, 1)])]

    def go_fourth(self, near):
        self.near = swap(near, "z1")

    def last(self):
        return [(self.tail, [(self.mine, slice(None)), (self.far, 0), (self.near, slice(None))])]

    def third_direct(self):
        return [self.kept(1), self.sent(0), self.sent(1), self.kept(0)]

    def go_third_direct(self, *blocks):
        self.got = [swap(block, name) for block, name in zip(blocks, ("z1", "z2", "z3"))]
        self.mine = blocks[3]

    def last_direct(self):
        return [(self.tail, [(self.mine, slice(None))] + [(got, slice(None)) for got in self.got])]


def join(first, second):
    (_, terms), = first.last()
    parts = []
    for half in range(2):
        cut = [(array, (0, half) if index == 0 else half) for array, index in terms]
        parts.append((cut, slice(half * 128, half * 128 + 128)))
    (_, terms), = second.last()
    for k in range(4):
        here = (slice(None), slice(k * 512, k * 512 + 512))
        cut = [(array, (0, *here) if index == 0 else here) for array, index in terms]
        parts.append((cut, slice(256 + k * 64, 320 + k * 64)))
    return (512, 512), parts


def pack_last(early, early_x, late):
    whole = slice(None)
    parts = [([(early, whole)], slice(0, 512)), ([(early_x, whole)], slice(512, 1024))]
    for k in range(4):
        here = (slice(None), slice(k * 512, k * 512 + 512))
        parts.append(([(late, here)], slice(1024 + k * 64, 1088 + k * 64)))
    return (1280, 512), parts


def pause_kernel(*_):
    pass


def early_blocks(where, early, early_x, other):
    x, c = where[2], where[3]
    return (
        (early, 0, x, c), (early_x, 0, 1 - x, c), (other, 0, x, 1 - c), (other, 512, 1 - x, 1 - c),
    )


def tall_shard_kernel(where, early, early_x, other, out):
    for block, first, xx, cc in early_blocks(where, early, early_x, other):
        for half in range(2):
            rows = pl.ds(pl.multiple_of(half * 256 + xx * 128, 128), 128)
            out[rows, lanes(cc * 512, 512)] = block[first + half * 128 : first + half * 128 + 128, :].astype(F32)


def up_shard_kernel(where, early, early_x, other, up_out):
    for block, first, xx, cc in early_blocks(where, early, early_x, other):
        rows = pl.ds(pl.multiple_of(xx * 64, 64), 64)
        for s in range(8):
            start = first + 256 + (s // 2) * 64
            value = block[start : start + 64, (s % 2) * 256 : (s % 2) * 256 + 256]
            up_out[rows, lanes(s * 512 + cc * 256, 256)] = value.astype(F32)


def qkv_shard_kernel(where, late, late_x, other, corner, out, out_out):
    x, c = where[2], where[3]
    for block, packed, xx, cc in (
        (late, False, x, c), (late_x, False, 1 - x, c), (other, True, x, 1 - c), (corner, False, 1 - x, 1 - c),
    ):
        rows = pl.ds(pl.multiple_of(xx * 64, 64), 64)
        for k in range(4):
            if packed:
                value = block[1024 + k * 64 : 1088 + k * 64, :]
            else:
                value = block[:, k * 512 : (k + 1) * 512]
            if k < 3:
                out[rows, lanes(k * 1024 + cc * 512, 512)] = value.astype(F32)
            else:
                out_out[rows, lanes(cc * 512, 512)] = value.astype(F32)


def shard_of(kernel, where, blocks, shapes):
    return simple(kernel, blocks, [(s, F32) for s in shapes], where=where, pin_out=range(len(shapes)))


def table_kernel(got, table, *vectors):
    n = got.shape[0]
    times = lax.broadcasted_iota(jnp.int32, (128, 8), 0).astype(F32)
    total = jnp.zeros(table.shape, F32)
    sums = jnp.zeros((16, 128), F32)
    for i in range(n):
        hot = (times == got[i, 18:19, 0:8]).astype(F32)
        total += lax.dot_general(hot, got[i, 0:8, :], (((1,), (0,)), ((), ())), precision=lax.Precision.HIGHEST)
        sums += got[i, 8:24, :]
    table[...] = total
    for row, vector in enumerate(vectors[:6]):
        vector[...] = sums[row : row + 1]
    vectors[6][...] = sums[6:10]


def normalize(values):
    centred = values - jnp.mean(values, axis=-1, keepdims=True)
    spread = jnp.mean(centred * centred, axis=-1, keepdims=True)
    return centred * lax.rsqrt(spread + 1e-05)


def scaled_norm(values, gain):
    return normalize(values) * gain


def exact_gelu(values):
    return jax.nn.gelu(values, approximate=False)


def layer(
    tokens,
    time_index,
    table_all,
    gain_one,
    bias_one,
    qkv_w,
    out_w,
    out_b,
    gain_two,
    bias_two,
    up_w,
    up_b,
    down_w,
    down_b,
    cotangent,
):
    row_count, model_width = tokens.shape
    seq_count = time_index.shape[0]
    length = row_count // seq_count
    head_dim = model_width // HEADS
    factor = head_dim ** (-0.5)
    levels = table_all.shape[0]
    gain_one_f = gain_one.astype(jnp.float32)
    gain_two_f = gain_two.astype(jnp.float32)
    one_hot = time_index[:, None] == jnp.arange(levels, dtype=jnp.int32)[None, :]
    embedding = jnp.dot(one_hot.astype(jnp.bfloat16), table_all, preferred_element_type=jnp.float32)
    scale_seq = (1.0 + embedding)[:, None, :]
    inputs = tokens.astype(jnp.float32)
    normed = (normalize(inputs) * gain_one_f + bias_one.astype(jnp.float32)).reshape(
        seq_count, length, model_width
    )
    scaled = (normed * scale_seq).astype(jnp.bfloat16).reshape(row_count, model_width)
    packed = jnp.dot(scaled, qkv_w, preferred_element_type=jnp.float32).astype(jnp.bfloat16)
    packed = packed.reshape(seq_count, length, 3, HEADS, head_dim)
    queries = packed[:, :, 0]
    key_heads = packed[:, :, 1]
    value_heads = packed[:, :, 2]
    scores = (
        jnp.einsum("sqhd,skhd->shqk", queries, key_heads, preferred_element_type=jnp.float32)
        * factor
    )
    attn_probs = jax.nn.softmax(scores, axis=-1)
    probs_low = attn_probs.astype(jnp.bfloat16)
    attn_mix = jnp.einsum(
        "shqk,skhd->sqhd", probs_low, value_heads, preferred_element_type=jnp.float32
    )
    attn_mix = attn_mix.astype(jnp.bfloat16).reshape(row_count, model_width)
    middle = (
        inputs
        + jnp.dot(attn_mix, out_w, preferred_element_type=jnp.float32)
        + out_b.astype(jnp.float32)
    )
    hidden_in = (normalize(middle) * gain_two_f + bias_two.astype(jnp.float32)).astype(jnp.bfloat16)
    pre_act = jnp.dot(hidden_in, up_w, preferred_element_type=jnp.float32) + up_b.astype(
        jnp.float32
    )
    activated = exact_gelu(pre_act).astype(jnp.bfloat16)
    block_out = (
        middle
        + jnp.dot(activated, down_w, preferred_element_type=jnp.float32)
        + down_b.astype(jnp.float32)
    ).astype(jnp.bfloat16)
    upstream = cotangent.astype(jnp.float32)
    grad_down = jnp.einsum("ti,td->id", activated, cotangent, preferred_element_type=jnp.float32)
    grad_down_b = jnp.sum(upstream, axis=0)
    d_act = jnp.einsum("td,id->ti", cotangent, down_w, preferred_element_type=jnp.float32)
    gelu_pull = jax.vjp(exact_gelu, pre_act)[1]
    d_pre = gelu_pull(d_act)[0].astype(jnp.bfloat16)
    grad_up = jnp.einsum("ti,tf->if", hidden_in, d_pre, preferred_element_type=jnp.float32)
    grad_up_b = jnp.sum(d_pre.astype(jnp.float32), axis=0)
    d_hidden = jnp.einsum("tf,if->ti", d_pre, up_w, preferred_element_type=jnp.float32)
    grad_ln2_bias = jnp.sum(d_hidden, axis=0)
    second_pull = jax.vjp(scaled_norm, middle, gain_two_f)[1]
    d_mid_part, grad_ln2_gain = second_pull(d_hidden)
    d_middle = upstream + d_mid_part
    d_mid_low = d_middle.astype(jnp.bfloat16)
    grad_out_w = jnp.einsum("ti,td->id", attn_mix, d_mid_low, preferred_element_type=jnp.float32)
    grad_out_b = jnp.sum(d_mid_low.astype(jnp.float32), axis=0)
    d_mix = jnp.einsum("td,id->ti", d_mid_low, out_w, preferred_element_type=jnp.float32)
    d_mix = d_mix.astype(jnp.bfloat16).reshape(seq_count, length, HEADS, head_dim)
    d_probs = jnp.einsum("sqhd,skhd->shqk", d_mix, value_heads, preferred_element_type=jnp.float32)
    d_values = jnp.einsum("shqk,sqhd->skhd", probs_low, d_mix, preferred_element_type=jnp.float32)
    d_scores = (
        attn_probs * (d_probs - jnp.sum(d_probs * attn_probs, axis=-1, keepdims=True))
    ).astype(jnp.bfloat16)
    d_queries = (
        jnp.einsum("shqk,skhd->sqhd", d_scores, key_heads, preferred_element_type=jnp.float32)
        * factor
    )
    d_keys = (
        jnp.einsum("shqk,sqhd->skhd", d_scores, queries, preferred_element_type=jnp.float32)
        * factor
    )
    d_packed = (
        jnp.stack([d_queries, d_keys, d_values], axis=2)
        .astype(jnp.bfloat16)
        .reshape(row_count, 3 * model_width)
    )
    grad_qkv = jnp.einsum("ti,tf->if", scaled, d_packed, preferred_element_type=jnp.float32)
    d_scaled = jnp.einsum("tf,if->ti", d_packed, qkv_w, preferred_element_type=jnp.float32).reshape(
        seq_count, length, model_width
    )
    d_normed = d_scaled * scale_seq
    grad_ln1_bias = jnp.sum(d_normed, axis=(0, 1))
    d_embedding = jnp.sum(d_scaled * normed, axis=1)
    grad_table = jnp.einsum(
        "sn,sd->nd", one_hot.astype(jnp.float32), d_embedding, precision=lax.Precision.HIGHEST
    )
    first_pull = jax.vjp(scaled_norm, inputs, gain_one_f)[1]
    d_in_part, grad_ln1_gain = first_pull(d_normed.reshape(row_count, model_width))
    grad_tokens = (d_middle + d_in_part).astype(jnp.bfloat16)
    return (
        block_out,
        grad_tokens,
        (grad_table, grad_ln1_gain, grad_ln1_bias, grad_qkv, grad_out_w, grad_out_b, grad_ln2_gain,
         grad_ln2_bias, grad_up, grad_up_b, grad_down, grad_down_b),
    )


def plain(*args):
    dims = (None, None, 1, 0, 0, 0, 0, 0, 0, 0, 0, 0, 0, 0, None)
    whole = [
        item if dim is None else lax.all_gather(item, "fsdp", axis=dim, tiled=True)
        for item, dim in zip(args, dims, strict=True)
    ]
    block_out, grad_tokens, grads = layer(*whole)
    shares = [
        lax.psum_scatter(grad, "fsdp", scatter_dimension=1 if place == 0 else 0, tiled=True)
        for place, grad in enumerate(grads)
    ]
    return (block_out, grad_tokens, *lax.psum(tuple(shares), "dp"))


def eight_by_four(
    tokens, time_index, time_table, ln1_gain, ln1_bias, w_qkv, w_out, b_out, ln2_gain, ln2_bias,
    w_up, b_up, w_down, b_down, cotangent,
):
    where = jnp.stack(coords()).astype(jnp.int32)
    seqs = time_index.shape[0]
    length = tokens.shape[0] // seqs
    vec = jnp.concatenate(
        [v.reshape(-1, 128) for v in (ln1_gain, ln1_bias, b_out, ln2_gain, ln2_bias, b_down, b_up)]
        + [jnp.zeros((6, 128), LOW)]
    )
    times = time_index.reshape(seqs, 1)
    chain.clear()

    (parts_first,) = own_first(where, w_qkv, w_out, w_up)
    small = jnp.concatenate([time_table, vec])
    small_side = swap(small, "y")
    (small_two,) = move([((2, 144, 128), [(small, (), 0), (small_side, (), 1)])])
    small_far = swap(small_two, "z2")
    pieces = [Piece(parts_first, (i,)) for i in range(3)]
    near = swap(parts_first, "z1")
    for piece in pieces:
        piece.move_z1(near, piece.index)

    def tick(*jobs, extra=(), passing=()):
        stages = {
            "z": ("two", "move_z2"), "y": ("four", "move_y"), "x": ("across_send", "move_x"), "c": ("core_send", "move_c"),
        }
        ready = [pieces[n] for stage, n in jobs if stage == "z" and pieces[n].pair is not None]
        jobs = [(pieces[n], *stages[stage]) for stage, n in jobs if stage != "z" or pieces[n].pair is None]
        made = move([getattr(p, make)() for p, make, _ in jobs] + list(extra), passing=passing)
        for (p, _, go), value in zip(jobs, made):
            getattr(p, go)(value)
        for p in ready:
            p.move_z2(p.pair)
        return made[len(jobs) :]

    extra = [((4, 144, 128), [(small_two, (), slice(0, 2)), (small_far, (), slice(2, 4))])]
    (small_four,) = tick(("z", 0), ("z", 1), extra=extra)
    small_near = swap(small_four, "z1")
    table, vec, up_b, scale = small_params(where, small_four, small_near, times)
    gain_one, bias_one, out_b, gain_two, bias_two, down_b = (vec[i : i + 1] for i in range(6))
    scale = scale.reshape(seqs, 1, -1)
    scaled = first_norm(tokens, gain_one, bias_one, scale)
    everything = slice(None)
    owns = [
        [(w_qkv, [(everything, pl.ds(0, 2048))], [0], 2048)],
        [(w_qkv, [(everything, pl.ds(2048, 1024))], [0], 1024), (w_out, [(everything, everything)], [1024], 1024)],
    ]
    for half in range(2):
        reads = [(everything, pl.ds(s * 512 + half * 256, 256)) for s in range(8)]
        owns.append([(w_up, reads, [s * 256 for s in range(8)], 256)])
    for half in range(2):
        reads = [(pl.ds(half * 256 + i * 128, 128), everything) for i in range(2)]
        owns.append([(w_down, reads, [0, 1024], 1024)])

    def whole(n):
        return (assemble(where, pieces[n], owns[n]))

    tick(("y", 0))
    (parts_other,) = simple(own_other_kernel, (w_up, w_down), [((3, 128, CW), LOW)], where=where)
    pieces += [Piece(parts_other, (i,), i >= 1) for i in range(3)]
    near_other = swap(parts_other, "z1")
    for i in range(3):
        pieces[3 + i].move_z1(near_other, (i,))
    pairs = tick(("x", 0), ("y", 1), ("z", 2), extra=[pieces[i].two() for i in range(3, 6)])
    for i in range(3):
        pieces[3 + i].pair = pairs[i]
    tick(("c", 0), ("x", 1), ("y", 2), ("z", 3))
    w_qk = whole(0)
    tick(("c", 1), ("x", 2), ("y", 3), ("z", 4))
    qk = (project(scaled, w_qk))
    vo = whole(1)
    begun = (attend(scaled, qk, vo, length, 0, 2))
    tick(("c", 2), ("x", 3), ("y", 4), ("z", 5))
    v, probs, mix = (attend(scaled, qk, vo, length, 2, 2, begun))
    middle, hidden = (second_norm(mix, tokens, vo, out_b, gain_two, bias_two))
    up_a = whole(2)
    tick(("c", 3), ("x", 4), ("y", 5))
    act_a, slope_a = (up(hidden, up_a, up_b[0:1]))
    up_b_w = whole(3)
    tick(("c", 4), ("x", 5))
    act_b, slope_b = (up(hidden, up_b_w, up_b[1:2]))
    def step(*jobs, passing=(), cost=0):
        lists = [getattr(r, stage)() for r, stage in jobs]
        made = add_up([item for items in lists for item in items], passing=passing, cost=cost)
        for (r, stage), items in zip(jobs, lists, strict=True):
            values, made = made[: len(items)], made[len(items) :]
            go = "go_last" if stage == "last_direct" else "go_" + stage
            getattr(r, go)(*values)
        return made

    acts = (act_a, act_b)
    downs = [whole(4)]
    away = (tall_away(where, acts, cotangent))
    (away,) = tick(("c", 5), passing=(away,))
    core_one = swap(away, "c")
    d_pre, up_sum_a = (pull(cotangent, downs[0], slope_a, 0))
    downs.append(whole(5))
    xa, yb, *keep = (tall_mine(where, acts, cotangent, core_one))
    one = Reduction(*keep)
    one.go_first(xa, yb)
    d_pre, up_sum_b = (pull(cotangent, downs[1], slope_b, 1, d_pre))
    pairs_two = [(hidden, d_pre, "layer")]
    core_two = swap((row_away(where, pairs_two)), "c")
    d_middle, d_low, d_mix, sums_two = (
        middle_back(d_pre, (up_a, up_b_w), middle, cotangent, gain_two, vo)
    )
    step((one, "second"), cost=42000000000)
    xa, yb, *keep = (row_mine(where, pairs_two, core_two))
    two = Reduction(*keep)
    two.go_first(xa, yb)
    d_packed = (attend_back(d_mix, probs, qk, v, length))
    step((one, "third"), cost=42000000000)
    pairs_three = [(scaled, d_packed, "layers"), (mix, d_low, "columns")]
    core_three = swap(row_away(where, pairs_three), "c")
    step((two, "second"), cost=38000000000)
    *sends, ka, kb = (row_mine(where, pairs_three, core_three))
    three = Reduction(ka, kb)
    three.go_first(*step((two, "third"), passing=sends))
    grad_tokens, sums_one, d_emb = (
        input_back(d_packed, w_qk, vo, tokens, d_middle, gain_one, bias_one, scale)
    )
    block_out = down(acts, downs, middle, down_b, 0, 2)
    step((one, "fourth"))
    simple(pause_kernel, (), [], cost=10000000000)
    step((three, "second"))
    (rows,) = (
        simple(
            rows_kernel,
            (d_emb, sums_one, sums_two, up_sum_a, up_sum_b, jnp.pad(time_index.astype(F32), (0, 120))[None]),
            [((32, 24, 128), F32)],
        )
    )
    got = lax.all_to_all(rows, BOTH, 0, 0)
    step((two, "fourth"), (three, "third_direct"))
    block_out = down(acts, downs, middle, down_b, 2, 2, (block_out,))
    (early,) = add_up([join(one, two)])
    early_x = swap(early, "x")
    grad_table, *sums = simple(
        table_kernel,
        (got,),
        [((128, 128), F32)] + [((1, 128), F32)] * 6 + [((4, 128), F32)],
        pin_out=range(8),
    )
    (late,) = add_up(three.last_direct(), cost=10000000000)
    late_x = swap(late, "x")
    (packed,) = add_up([pack_last(early, early_x, late)])
    other = swap(packed, "c")
    (down_shard,) = shard_of(tall_shard_kernel, where, (early, early_x, other), [(512, 1024)])
    (up_shard,) = shard_of(up_shard_kernel, where, (early, early_x, other), [(128, 4096)])
    (late_x,) = simple(pause_kernel, (), [], passing=(late_x,))
    late_corner = swap(late_x, "c")
    qkv_shard, out_shard = shard_of(
        qkv_shard_kernel, where, (late, late_x, other, late_corner), [(128, 3072), (128, 1024)]
    )
    return (
        block_out, grad_tokens, grad_table, sums[0][0], sums[1][0], qkv_shard, out_shard, sums[2][0], sums[3][0], sums[4][0],
        up_shard, sums[6].reshape(512), down_shard, sums[5][0],
    )


def solution(mesh):
    in_specs = (
        P(("fsdp", "dp"), None),
        P(("fsdp", "dp")),
        P(None, "fsdp"),
        P("fsdp"),
        P("fsdp"),
        P("fsdp", None),
        P("fsdp", None),
        P("fsdp"),
        P("fsdp"),
        P("fsdp"),
        P("fsdp", None),
        P("fsdp"),
        P("fsdp", None),
        P("fsdp"),
        P(("fsdp", "dp"), None),
    )
    out_specs = (
        P(("fsdp", "dp"), None),
        P(("fsdp", "dp"), None),
        P(None, "fsdp"),
        P("fsdp"),
        P("fsdp"),
        P("fsdp", None),
        P("fsdp", None),
        P("fsdp"),
        P("fsdp"),
        P("fsdp"),
        P("fsdp", None),
        P("fsdp"),
        P("fsdp", None),
        P("fsdp"),
    )
    local = eight_by_four if (mesh.shape["fsdp"], mesh.shape["dp"]) == (8, 4) else plain
    return jax.shard_map(local, mesh=mesh, in_specs=in_specs, out_specs=out_specs, check_vma=False)
```
